128 devices in a mesh: comp: 16 (over z, y), band: 8 (over x, core).
Axes of the slice: x: 4, y: 4, z: 4, core: 2. Of those that a mesh axis runs over, the one named last changes fastest.
Arguments:
- spectra: bfloat16 [32, 36, 32, 1440], P('comp', None, 'band'), may hold values from 0 to 6, as said below
- depth_class: int32 [32, 1440], P('band'), may hold values from 0 to 63
- group_speed: float32 [64, 32], replicated, may hold values from 0.15 to 0.5
- current: float32 [2, 32, 1440], P(None, 'band'), may hold values from -0.3 to 0.3
- depth_slope: float32 [2, 32, 1440], P(None, 'band'), may hold values from -4 to 4
- wind: float32 [2, 32, 1440], P(None, 'band'), may hold values from -32 to 32
- land_mask: int32 [32, 1440], P('band'), may hold values from 0 to 1, as said below
- block_counts: int32 [8, 16], P('band'), may hold values from 105 to 315, as said below
Outputs:
- spectra_out: bfloat16 [1152, 40320], P(None, ('comp', 'band'))
The draws below stay inside these ranges and needn't reach their ends.
Inputs may be any that keep to these rules, and one draw needn't show every extreme that they name: `spectra`: nonnegative densities. `land_mask`: band b's rows hold exactly as many sea cells as row b of block_counts sums to. `block_counts`: in every band one block has exactly 315 sea points.
All inputs are finite; a program needn't handle non-finite values.
Results may differ from the reference program's by a relative error of at most 0.0004.
Values may be sent and summed in bfloat16 or wider, within the bound.
A program may use at most 64 MiB of HBM per device.

```python
import math
import jax
import jax.numpy as jnp
from jax import lax

NF = 32
ND = 36
NLON = 1440
ROWS = 4
DEPTHS = 64
NLAT = 32
SLOTS = 315
N_COMP = 16
N_BAND = 8


def sea_plan(key):
    cell_count = ROWS * NLON
    first, second, third = jax.random.split(key, 3)
    block_sizes = jax.random.randint(first, (N_BAND, N_COMP), SLOTS // 3, SLOTS + 1)
    fullest = jax.random.randint(second, (N_BAND,), 0, N_COMP)
    block_sizes = jnp.where(jnp.arange(N_COMP)[None, :] == fullest[:, None], SLOTS, block_sizes).astype(jnp.int32)
    totals = jnp.sum(block_sizes, axis=1)

    def shuffled(band_key):
        return jax.random.permutation(band_key, cell_count)
    orders = jax.vmap(shuffled)(jax.random.split(third, N_BAND))
    chosen = (jnp.arange(cell_count)[None, :] < totals[:, None]).astype(jnp.int32)

    def placed(order_row, chosen_row):
        return jnp.zeros((cell_count,), jnp.int32).at[order_row].set(chosen_row)
    flags = jax.vmap(placed)(orders, chosen)
    return (flags, block_sizes)


def draw_land_mask(key, part):
    flags, unused = sea_plan(key)
    return (1 - flags).reshape(NLAT, NLON).astype(jnp.int32)


def draw_block_counts(key, part):
    unused, block_sizes = sea_plan(key)
    return block_sizes


def draw_spectra(key, part):
    key = jax.random.fold_in(key, 7)
    first = jax.random.fold_in(key, 0)
    ramp = (0.6 + 1.2 * jnp.arange(NF, dtype=jnp.float32) / max(NF - 1, 1))[:, None, None, None]
    values = jnp.exp(jax.random.uniform(first, (NF, ND, NLAT, NLON), jnp.float32, math.log(0.05), 0.0)) * ramp
    return values.astype(jnp.bfloat16)


def touch_ends(entries, key, low, high):
    longest = entries.shape.index(max(entries.shape))
    spots = []
    for shift in (0, 1):
        where = [jax.random.randint(jax.random.fold_in(key, axis), (), 0, length) for axis, length in enumerate(entries.shape)]
        where[longest] = (where[longest] + shift) % entries.shape[longest]
        spots.append(tuple(where))
    return entries.at[spots[0]].set(low).at[spots[1]].set(high)


def steps_of(key, shape, shards, smallest, top_value):
    level, own = 1.0, jax.random.fold_in(key, 6)
    for axis_at, shards_of in shards:
        steps = jnp.exp(jax.random.uniform(jax.random.fold_in(own, axis_at), (shards_of,), jnp.float32, smallest / len(shards), top_value / len(shards)))
        level = level * jnp.repeat(steps, shape[axis_at] // shards_of).reshape([-1 if axis == axis_at else 1 for axis in range(len(shape))])
    return level


def bell_draw(own_key, extent, deviation, bound, shards=(), kind=jnp.bfloat16):
    drawn = jax.random.normal(own_key, extent, jnp.float32) * deviation
    if len(shards) > 0:
        drawn = steps_of(own_key, extent, shards, -0.22, 0.18) * drawn
    return jnp.clip(drawn, min=-bound, max=bound).astype(kind)


def setup_inputs(seed: int = 0) -> dict:
    key_list = jax.random.split(jax.random.key(seed), 9)
    return {
        "spectra": draw_spectra(jax.random.fold_in(key_list[8], 71), 0),
        "depth_class": touch_ends(jax.random.randint(key_list[1], (NLAT, NLON), 0, DEPTHS), jax.random.fold_in(key_list[1], 1), 0, DEPTHS - 1).astype(jnp.int32),
        "group_speed": jnp.clip(jnp.exp(jax.random.uniform(key_list[2], (DEPTHS, NF), jnp.float32, math.log(0.15), math.log(0.5))), 0.15, 0.5),
        "current": bell_draw(key_list[3], (2, NLAT, NLON), 0.1, 0.3, ((1, 8),), jnp.float32),
        "depth_slope": bell_draw(key_list[4], (2, NLAT, NLON), 1.0, 4.0, ((1, 8),), jnp.float32),
        "wind": bell_draw(key_list[5], (2, NLAT, NLON), 8.0, 32.0, ((1, 8),), jnp.float32),
        "land_mask": draw_land_mask(jax.random.fold_in(key_list[8], 71), 0),
        "block_counts": draw_block_counts(jax.random.fold_in(key_list[8], 71), 0),
    }


GROWTH_RATE = 0.05
DAMPING = 1.5
TURNING_SCALE = 0.5

def upwind(far_behind, behind, centre, ahead, far_ahead, celerity):
    forward = (2.0 * ahead + 3.0 * centre - 6.0 * behind + far_behind) / 6.0
    backward = (-far_ahead + 6.0 * ahead - 3.0 * centre - 2.0 * behind) / 6.0
    return celerity * jnp.where(celerity > 0, forward, backward)

def wrapped(values, celerity, axis):
    return upwind(jnp.roll(values, 2, axis), jnp.roll(values, 1, axis), values, jnp.roll(values, -1, axis), jnp.roll(values, -2, axis), celerity)

def frequencies(count):
    angular = 2.0 * math.pi * 0.0418 * jnp.power(1.1, jnp.arange(count, dtype=jnp.float32))
    return (angular / angular[-1], 9.81 / angular)

def angles(count):
    heading = jnp.arange(count, dtype=jnp.float32) * (2.0 * math.pi / count)
    return (jnp.cos(heading), jnp.sin(heading))

def block_lists(band_mask, block_sizes, slot_count):
    sea_flag = (band_mask.reshape(-1) == 0).astype(jnp.int32)
    cell_count = sea_flag.shape[0]
    capacity = block_sizes.shape[0] * slot_count
    ranking = jnp.cumsum(sea_flag) - 1
    target = jnp.where(sea_flag == 1, ranking, capacity).astype(jnp.int32)
    ordered = jnp.zeros((capacity,), jnp.int32).at[target].set(jnp.arange(cell_count, dtype=jnp.int32), mode='drop')
    starts = jnp.cumsum(block_sizes) - block_sizes
    slot_ids = jnp.arange(slot_count, dtype=jnp.int32)
    position = jnp.minimum(starts[:, None] + slot_ids[None, :], capacity - 1).astype(jnp.int32)
    return jnp.where(slot_ids[None, :] < block_sizes[:, None], ordered[position], -1).astype(jnp.int32)

def sources(values, mean_sq, wind_u, wind_v, ratio, phase, cos_t, sin_t):
    strength = jnp.sqrt(mean_sq + 1e-06)
    wind_along = wind_u[None, None, :] * cos_t[None, :, None] + wind_v[None, None, :] * sin_t[None, :, None]
    growth = GROWTH_RATE * ratio[:, None, None] * jnp.maximum(wind_along / phase[:, None, None] - 1.0, 0.0)
    decay = DAMPING * ratio[:, None, None] * strength[None, None, :]
    return values * jnp.exp(growth - decay)

def reference(spectra, depth_class, group_speed, current, depth_slope, wind, land_mask, block_counts):
    sea_flag = (land_mask == 0).astype(jnp.float32)
    cos_t, sin_t = angles(ND)
    ratio, phase = frequencies(NF)
    latitude = (-60.0 + 120.0 * (jnp.arange(NLAT, dtype=jnp.float32) + 0.5) / NLAT) * (math.pi / 180.0)
    stretch = 1.0 / jnp.cos(latitude)
    speeds = jnp.moveaxis(group_speed[depth_class], -1, 0)

    def one_frequency(inputs):
        spectrum, celerity = inputs
        density = spectrum.astype(jnp.float32) * sea_flag
        speed_x = celerity[None] * cos_t[:, None, None] * stretch[None, :, None] + current[0][None]
        speed_y = celerity[None] * sin_t[:, None, None] + current[1][None]
        padded = jnp.pad(density, ((0, 0), (2, 2), (0, 0)))
        across = upwind(padded[:, :-4], padded[:, 1:-3], density, padded[:, 3:-1], padded[:, 4:], speed_y)
        advected = (density - wrapped(density, speed_x, 2) - across) * sea_flag
        turning = TURNING_SCALE * celerity[None] * (sin_t[:, None, None] * depth_slope[0][None] - cos_t[:, None, None] * depth_slope[1][None])
        return (advected - wrapped(advected, turning, 0)) * sea_flag
    refracted = lax.map(one_frequency, (spectra, speeds))
    flattened = refracted.reshape(NF * ND, NLAT * NLON)
    wind_east = wind[0].reshape(-1)
    wind_north = wind[1].reshape(-1)
    blocks_out = []
    for band_index in range(N_BAND):
        slot_cells = block_lists(land_mask[band_index * ROWS:(band_index + 1) * ROWS], block_counts[band_index], SLOTS)
        all_cells = (jnp.maximum(slot_cells, 0) + band_index * ROWS * NLON).reshape(-1).astype(jnp.int32)
        picked = jnp.take(flattened, all_cells, axis=1).reshape(NF, ND, -1)
        mean_sq = lax.optimization_barrier(jnp.mean(picked * picked, axis=(0, 1)))
        result = sources(picked, mean_sq, jnp.take(wind_east, all_cells), jnp.take(wind_north, all_cells), ratio, phase, cos_t, sin_t)
        occupied = (slot_cells.reshape(-1) >= 0).astype(jnp.float32)
        blocks_out.append((result * occupied[None, None, :]).astype(jnp.bfloat16).reshape(NF * ND, N_COMP, SLOTS))
    stacked = jnp.stack(blocks_out, axis=2)
    return stacked.reshape(NF * ND, N_COMP * N_BAND * SLOTS)
```

```python
import math

import jax
import jax.numpy as jnp
import numpy as np
from jax import lax
from jax.experimental import pallas as pl
from jax.experimental.pallas import tpu as pltpu
from jax.sharding import PartitionSpec as P

GROWTH_RATE = 0.05
DAMPING = 1.5
TURNING_SCALE = 0.5

FREQS = 2
LANES = 128
ND = 36
ROWS = 4
NLON = 1440
TILES = 12
GROUPS = ROWS * TILES
BLOCKS = 16
SLOTS = 315
STEPS = 96
COMPS = FREQS * ND
PACK = 184

AT_TILE, AT_GROUP, AT_KEEP, AT_LAST = 0, 128, 256, 384
AT_RANK, AT_LEN, AT_FIRST, AT_COUNT = 512, 640, 768, 896

(F_SEA, F_CX, F_CY, F_CUR0, F_CUR1, F_T0, F_T1) = range(7)

MESH = pl.DeviceIdType.MESH


def angles():
    heading = (np.arange(ND, dtype=np.float32) * np.float32(2.0 * math.pi / ND)).astype(np.float64)
    return (np.cos(heading).astype(np.float32), np.sin(heading).astype(np.float32))


def upwind12(far_behind, behind, centre, ahead, far_ahead, speed):
    forward = speed > 0
    down = jnp.where(forward, ahead, behind)
    up = jnp.where(forward, behind, ahead)
    far = jnp.where(forward, far_behind, far_ahead)
    return jnp.abs(speed) * ((2.0 * down + far) + (3.0 * centre - 6.0 * up))


def stencil_kernel(
    trig_ref, tab_ref, spec_ref, dn_ref, up_ref, fields_ref, depth_ref, gs_ref, stretch_ref, wind_ref, loc_ref,
    sb_ref, wsb_ref,
    x_ref, h_ref, adv_ref, t_ref, stage_ref, fl_ref,
):
    lane = lax.broadcasted_iota(jnp.int32, (8, LANES), 1)
    sub = lax.broadcasted_iota(jnp.int32, (8, LANES), 0)
    row = sub // 2
    tail = NLON - (TILES - 1) * LANES

    for j in range(TILES):
        idx = depth_ref[j]
        cel = jnp.take_along_axis(gs_ref[...], idx, axis=1)
        sixth = cel * (1.0 / 6.0)
        fl_ref[F_SEA, j] = fields_ref[0, j]
        fl_ref[F_CX, j] = sixth * stretch_ref[...]
        fl_ref[F_CY, j] = sixth
        fl_ref[F_CUR0, j] = fields_ref[1, j] * (1.0 / 6.0)
        fl_ref[F_CUR1, j] = fields_ref[2, j] * (1.0 / 6.0)
        fl_ref[F_T0, j] = (TURNING_SCALE * sixth) * fields_ref[3, j]
        fl_ref[F_T1, j] = (TURNING_SCALE * sixth) * fields_ref[4, j]

    def load(d, carry):
        base = pl.multiple_of(8 * d, 8)
        for j in range(TILES):
            width = LANES if j < TILES - 1 else tail
            cols = pl.ds(j * LANES, width)
            for f in range(FREQS):
                v = spec_ref[f, d, :, cols].astype(jnp.float32)
                x_ref[j, pl.ds(base + f, 4, stride=2), pl.ds(0, width)] = v
            h_ref[j, pl.ds(base, 4), pl.ds(0, width)] = dn_ref[d, :, cols].astype(jnp.float32)
            h_ref[j, pl.ds(base + 4, 4), pl.ds(0, width)] = up_ref[d, :, cols].astype(jnp.float32)
        return carry

    lax.fori_loop(0, ND, load, 0)

    def advect(d, carry):
        base = pl.multiple_of(8 * d, 8)
        cos_d = trig_ref[0, d]
        sin_d = trig_ref[1, d]
        x = [x_ref[j, pl.ds(base, 8), :] * fl_ref[F_SEA, j] for j in range(TILES - 1)]
        last = jnp.where(lane < tail, x_ref[TILES - 1, pl.ds(base, 8), :], 0.0) * fl_ref[F_SEA, TILES - 1]
        last = jnp.where(
            lane < tail,
            last,
            jnp.where(lane < tail + 2, pltpu.roll(x[0], tail, 1), pltpu.roll(last, LANES - tail, 1)),
        )
        x.append(last)
        r1 = [pltpu.roll(v, 1, 1) for v in x]
        r2 = [pltpu.roll(v, 2, 1) for v in x]
        l1 = [pltpu.roll(v, LANES - 1, 1) for v in x]
        l2 = [pltpu.roll(v, LANES - 2, 1) for v in x]
        for j in range(TILES):
            before, after = (j - 1) % TILES, (j + 1) % TILES
            v = x[j]
            behind = jnp.where(lane < 1, r1[before], r1[j])
            far_behind = jnp.where(lane < 2, r2[before], r2[j])
            ahead = jnp.where(lane >= LANES - 1, l1[after], l1[j])
            far_ahead = jnp.where(lane >= LANES - 2, l2[after], l2[j])
            speed = fl_ref[F_CX, j] * cos_d + fl_ref[F_CUR0, j]
            along = upwind12(far_behind, behind, v, ahead, far_ahead, speed)
            h = h_ref[j, pl.ds(base, 8), :]
            ahead = pltpu.roll(jnp.where(row == 0, h, v), 6, 0)
            far_ahead = pltpu.roll(jnp.where(row < 2, h, v), 4, 0)
            far_behind = pltpu.roll(jnp.where(row < 2, v, h), 4, 0)
            behind = pltpu.roll(jnp.where(row == 3, h, v), 2, 0)
            speed = fl_ref[F_CY, j] * sin_d + fl_ref[F_CUR1, j]
            across = upwind12(far_behind, behind, v, ahead, far_ahead, speed)
            out = (v - along - across) * fl_ref[F_SEA, j]
            if j == TILES - 1:
                out = jnp.where(lane < tail, out, 0.0)
            adv_ref[j, pl.ds(base, 8), :] = out
        return carry

    lax.fori_loop(0, ND, advect, 0)

    def refract(d, carry):
        cos_d = trig_ref[0, d]
        sin_d = trig_ref[1, d]

        def at(shift):
            k = d + shift
            k = jnp.where(k < 0, k + ND, jnp.where(k >= ND, k - ND, k))
            return pl.multiple_of(8 * k, 8)

        places = [at(s) for s in (-2, -1, 0, 1, 2)]
        for j in range(TILES):
            values = [adv_ref[j, pl.ds(p, 8), :] for p in places]
            speed = fl_ref[F_T0, j] * sin_d - fl_ref[F_T1, j] * cos_d
            out = (values[2] - upwind12(*values, speed)) * fl_ref[F_SEA, j]
            t_ref[j, pl.ds(d, 8, stride=ND), :] = out
        return carry

    lax.fori_loop(0, ND, refract, 0)

    lane_wide = lax.broadcasted_iota(jnp.int32, (COMPS, LANES), 1)

    def step(k, carry):
        acc, wacc = carry
        tile = tab_ref[AT_TILE + k]
        group = tab_ref[AT_GROUP + k]
        keep = tab_ref[AT_KEEP + k].astype(jnp.float32)
        r = group // TILES
        j = group - r * TILES
        local = lane + (tab_ref[AT_RANK + tile] - tab_ref[AT_FIRST + group])
        valid = (lane < tab_ref[AT_LEN + tile]) & (local >= 0) & (local < tab_ref[AT_COUNT + group])
        local = jnp.clip(local, 0, LANES - 1)
        cells = jnp.broadcast_to(loc_ref[pl.ds(group, 1), :], (8, LANES))
        idx = jnp.take_along_axis(cells, local, axis=1)
        parts = []
        for m in range(COMPS // 8):
            data = t_ref[j, pl.ds(pl.multiple_of(r * COMPS, 8) + 8 * m, 8), :]
            got = jnp.take_along_axis(data, idx, axis=1)
            part = jnp.where(valid, got, acc[m] * keep)
            stage_ref[k, pl.ds(8 * m, 8), :] = part
            parts.append(part)
        got = jnp.take_along_axis(wind_ref[group], idx, axis=1)
        wacc = jnp.where(valid, got, wacc * keep)
        stage_ref[k, pl.ds(COMPS, 8), :] = wacc
        return (tuple(parts), wacc)

    zero = jnp.zeros((8, LANES), jnp.float32)
    lax.fori_loop(0, STEPS, step, ((zero,) * (COMPS // 8), zero))

    def gather_out(c, carry):
        for j in range(2):
            k = tab_ref[AT_LAST + 3 * c + j]
            sb_ref[c, pl.ds(COMPS * j, COMPS), :] = stage_ref[k, pl.ds(0, COMPS), :]
            wsb_ref[c, j] = stage_ref[k, pl.ds(COMPS, 8), :]
        k = tab_ref[AT_LAST + 3 * c + 2]
        wsb_ref[c, 2] = stage_ref[k, pl.ds(COMPS, 8), :]
        for m in range(5):
            v = stage_ref[k, pl.ds(8 * m, 8), :]
            if m < 4:
                other = pltpu.roll(stage_ref[k, pl.ds(40 + 8 * m, 8), :], 64, 1)
                v = jnp.where(lane < 64, v, other)
            sb_ref[c, pl.ds(2 * COMPS + 8 * m, 8), :] = v
        return carry

    lax.fori_loop(0, BLOCKS, gather_out, 0)


def exchange_kernel(sb_ref, rb_ref, send_sem, recv_sem, own_sem):
    me = lax.axis_index("comp")
    barrier = pltpu.get_barrier_semaphore()
    for k in range(1, BLOCKS):
        peer = lax.rem(me + k, BLOCKS)
        pl.semaphore_signal(barrier, inc=1, device_id={"comp": peer}, device_id_type=MESH)
    own = pltpu.make_async_copy(sb_ref.at[me], rb_ref.at[me], own_sem)
    own.start()
    pl.semaphore_wait(barrier, BLOCKS - 1)
    copies = []
    for k in range(1, BLOCKS):
        peer = lax.rem(me + k, BLOCKS)
        copy = pltpu.make_async_remote_copy(
            src_ref=sb_ref.at[peer],
            dst_ref=rb_ref.at[me],
            send_sem=send_sem.at[k],
            recv_sem=recv_sem.at[k],
            device_id={"comp": peer},
            device_id_type=MESH,
        )
        copy.start()
        copies.append(copy)
    own.wait()
    for copy in copies:
        copy.wait()


def source_kernel(wind_ref, trig_ref, coef_ref, rb_ref, out_ref, wa_ref, v_ref):
    zero = jnp.zeros((8, LANES), jnp.float32)

    def squares(i, acc):
        acc = list(acc)
        for j in range(3):
            rows = COMPS if j < 2 else 40
            for m in range(rows // 8):
                v = rb_ref[i, pl.ds(COMPS * j + 8 * m, 8), :]
                acc[j] = acc[j] + v * v
        return tuple(acc)

    sums = lax.fori_loop(0, BLOCKS, squares, (zero, zero, zero))
    means = [jnp.sum(s, axis=0, keepdims=True) for s in sums]
    lane1 = lax.broadcasted_iota(jnp.int32, (1, LANES), 1)
    means[2] = jnp.where(lane1 < 64, means[2] + pltpu.roll(means[2], 64, 1), 0.0)
    total = BLOCKS * COMPS
    lane = lax.broadcasted_iota(jnp.int32, (8, LANES), 1)
    sub = lax.broadcasted_iota(jnp.int32, (8, LANES), 0)
    strength = [
        jnp.broadcast_to(jnp.sqrt(m * (1.0 / total) + 1e-6), (8, LANES)) for m in means
    ]
    for j in range(3):
        east = jnp.broadcast_to(wind_ref[j, 0:1, :], (8, LANES))
        north = jnp.broadcast_to(wind_ref[j, 1:2, :], (8, LANES))
        for m in range(COMPS // 8):
            wa_ref[j, pl.ds(8 * m, 8), :] = (
                east * trig_ref[0, pl.ds(8 * m, 8), :] + north * trig_ref[1, pl.ds(8 * m, 8), :]
            )

    def apply(i, carry):
        for j in range(3):
            for m in range(COMPS // 8):
                f0 = (8 * m) // ND
                f1 = (8 * m + 7) // ND

                def coef(q):
                    low = coef_ref[q, 2 * i + f0]
                    if f0 == f1:
                        return low
                    return jnp.where(sub < ND - 8 * m, low, coef_ref[q, 2 * i + f1])

                if j < 2:
                    v = rb_ref[i, pl.ds(COMPS * j + 8 * m, 8), :]
                elif m < 5:
                    v = rb_ref[i, pl.ds(2 * COMPS + 8 * m, 8), :]
                else:
                    v = pltpu.roll(rb_ref[i, pl.ds(2 * COMPS + 8 * (m - 5), 8), :], 64, 1)
                growth = jnp.maximum(wa_ref[j, pl.ds(8 * m, 8), :] * coef(0) - coef(1), 0.0)
                out = v * jnp.exp(growth - strength[j] * coef(2))
                v_ref[j, pl.ds(pl.multiple_of(COMPS * i, 8) + 8 * m, 8), :] = out
        return carry

    lax.fori_loop(0, BLOCKS, apply, 0)

    for m in range(BLOCKS * COMPS // LANES):
        for j in range(3):
            block = v_ref[j, pl.ds(LANES * m, LANES), :].T.astype(jnp.bfloat16)
            rows = min(LANES, SLOTS - LANES * j)
            out_ref[pl.ds(LANES * j, rows), pl.ds(LANES * m, LANES)] = block[:rows]


def tables(land_mask, counts):
    sea = (land_mask == 0).astype(jnp.float32)
    padded = jnp.pad(sea, ((0, 0), (0, TILES * LANES - NLON))).reshape(GROUPS, LANES)
    lanes = np.arange(LANES)
    upper = (lanes[:, None] <= lanes[None, :]).astype(np.float32)
    inclusive = jnp.dot(padded, upper, preferred_element_type=jnp.float32).astype(jnp.int32)
    local = jnp.sum((inclusive[:, :, None] <= lanes[None, None, :].astype(np.int32)).astype(jnp.int32), axis=1)
    local = jnp.minimum(local, LANES - 1)
    count = inclusive[:, LANES - 1]
    groups = np.arange(GROUPS)
    ends = jnp.sum(jnp.where(groups[None, :] <= groups[:, None], count[None, :], 0), axis=1)
    first = ends - count
    blocks = np.arange(BLOCKS)
    starts = jnp.sum(jnp.where(blocks[None, :] < blocks[:, None], counts[None, :], 0), axis=1)
    offset = (np.arange(3) * LANES).astype(np.int32)
    rank = (starts[:, None] + offset[None, :]).reshape(-1)
    length = jnp.clip(counts[:, None] - offset[None, :], 0, LANES).reshape(-1)
    last_rank = rank + jnp.maximum(length, 1) - 1
    low = jnp.minimum(jnp.sum((ends[None, :] <= rank[:, None]).astype(jnp.int32), axis=1), GROUPS - 1)
    high = jnp.minimum(jnp.sum((ends[None, :] <= last_rank[:, None]).astype(jnp.int32), axis=1), GROUPS - 1)
    width = jnp.where(length > 0, high - low + 1, 1)
    tiles = np.arange(3 * BLOCKS)
    stop = jnp.sum(jnp.where(tiles[None, :] <= tiles[:, None], width[None, :], 0), axis=1)
    steps = np.arange(LANES).astype(np.int32)
    tile = jnp.sum((stop[None, :] <= steps[:, None]).astype(jnp.int32), axis=1)
    tile = jnp.minimum(tile, 3 * BLOCKS - 1)
    hit = tile[:, None] == tiles[None, :].astype(np.int32)
    group = steps + jnp.sum(jnp.where(hit, (low - (stop - width))[None, :], 0), axis=1)
    group = jnp.clip(group, 0, GROUPS - 1)
    begin = jnp.sum(jnp.where(hit, (stop - width)[None, :], 0), axis=1)
    keep = (steps > begin).astype(jnp.int32)

    def wide(x):
        return jnp.pad(x.astype(jnp.int32), (0, LANES - x.shape[0]))

    table = jnp.concatenate(
        [tile, group, keep, wide(stop - 1), wide(rank), wide(length), wide(first), wide(count)]
    )
    return table, local


def per_cell(x):
    lead = x.shape[:-2]
    x = jnp.pad(x, ((0, 0),) * (x.ndim - 1) + ((0, TILES * LANES - NLON),))
    x = x.reshape(lead + (ROWS, 1, TILES, LANES))
    x = jnp.broadcast_to(x, lead + (ROWS, FREQS, TILES, LANES))
    x = jnp.moveaxis(x, -2, len(lead))
    return x.reshape(lead + (TILES, 2 * ROWS, LANES))


def body(spectra, depth_class, group_speed, current, depth_slope, wind, land_mask, block_counts):
    comp_index = lax.axis_index("comp")
    band_index = lax.axis_index("band")
    bands = lax.axis_size("band")
    cos_t, sin_t = angles()

    sea = (land_mask == 0).astype(jnp.bfloat16)

    def edge(lo):
        part = spectra[:, :, lo : lo + 2] * sea[lo : lo + 2]
        return jnp.transpose(part, (1, 2, 0, 3)).reshape(ND, 2 * FREQS, NLON)

    up_pairs = [(i, i + 1) for i in range(bands - 1)]
    down_pairs = [(i + 1, i) for i in range(bands - 1)]
    halo_up = lax.ppermute(edge(2), "band", up_pairs)
    halo_dn = lax.ppermute(edge(0), "band", down_pairs)

    table, local = tables(land_mask, block_counts[0])
    fields = per_cell(
        jnp.concatenate([(land_mask == 0).astype(jnp.float32)[None], current, depth_slope], axis=0)
    )
    depth = per_cell(depth_class)
    own = lax.dynamic_slice_in_dim(group_speed, comp_index * FREQS, FREQS, 1)
    own = jnp.pad(own.T, ((0, 0), (0, LANES - own.shape[0])))
    speeds = jnp.tile(own, (ROWS, 1))
    row_ids = (band_index * ROWS + jnp.arange(ROWS, dtype=jnp.int32)).astype(jnp.float32)
    latitude = (-60.0 + 120.0 * (row_ids + 0.5) / (ROWS * bands)) * (math.pi / 180.0)
    stretch = jnp.broadcast_to(jnp.repeat(1.0 / jnp.cos(latitude), FREQS)[:, None], (8, LANES))
    wide_wind = jnp.pad(wind, ((0, 0), (0, 0), (0, TILES * LANES - NLON))).reshape(2, GROUPS, LANES)
    wide_wind = jnp.pad(jnp.moveaxis(wide_wind, 0, 1), ((0, 0), (0, 6), (0, 0)))

    vmem = pl.BlockSpec(memory_space=pltpu.VMEM)
    smem = pl.BlockSpec(memory_space=pltpu.SMEM)
    sb, wsb = pl.pallas_call(
        stencil_kernel,
        out_shape=(
            jax.ShapeDtypeStruct((BLOCKS, PACK, LANES), jnp.float32),
            jax.ShapeDtypeStruct((BLOCKS, 3, 8, LANES), jnp.float32),
        ),
        in_specs=[smem, smem] + [vmem] * 9,
        out_specs=(vmem, vmem),
        scratch_shapes=[
            pltpu.VMEM((TILES, 8 * ND, LANES), jnp.float32),
            pltpu.VMEM((TILES, 8 * ND, LANES), jnp.float32),
            pltpu.VMEM((TILES, 8 * ND, LANES), jnp.float32),
            pltpu.VMEM((TILES, 8 * ND, LANES), jnp.float32),
            pltpu.VMEM((STEPS, COMPS + 8, LANES), jnp.float32),
            pltpu.VMEM((7, TILES, 8, LANES), jnp.float32),
        ],
        compiler_params=pltpu.CompilerParams(vmem_limit_bytes=48 * 1024 * 1024),
        name="stencil",
    )(
        jnp.asarray(np.stack([cos_t, sin_t])),
        table,
        spectra,
        halo_dn,
        halo_up,
        fields,
        depth,
        speeds,
        stretch,
        wide_wind,
        local,
    )

    rb = pl.pallas_call(
        exchange_kernel,
        out_shape=jax.ShapeDtypeStruct((BLOCKS, PACK, LANES), jnp.float32),
        in_specs=[vmem],
        out_specs=vmem,
        scratch_shapes=[
            pltpu.SemaphoreType.DMA((BLOCKS,)),
            pltpu.SemaphoreType.DMA((BLOCKS,)),
            pltpu.SemaphoreType.DMA,
        ],
        compiler_params=pltpu.CompilerParams(
            collective_id=0, has_side_effects=True, vmem_limit_bytes=16 * 1024 * 1024
        ),
        name="exchange",
    )(sb)

    angular = 2.0 * math.pi * 0.0418 * np.power(1.1, np.arange(BLOCKS * FREQS, dtype=np.float64))
    ratio = angular / angular[-1]
    phase = 9.81 / angular
    coef = np.stack([GROWTH_RATE * ratio / phase, GROWTH_RATE * ratio, DAMPING * ratio]).astype(np.float32)
    trig = np.stack([np.tile(cos_t, 2), np.tile(sin_t, 2)])
    trig = np.ascontiguousarray(np.broadcast_to(trig[:, :, None], (2, COMPS, LANES)))
    own_wind = lax.dynamic_index_in_dim(wsb, comp_index, 0, keepdims=False)
    out = pl.pallas_call(
        source_kernel,
        out_shape=jax.ShapeDtypeStruct((SLOTS, BLOCKS * COMPS), jnp.bfloat16),
        in_specs=[vmem, vmem, smem, vmem],
        out_specs=vmem,
        scratch_shapes=[
            pltpu.VMEM((3, COMPS, LANES), jnp.float32),
            pltpu.VMEM((3, BLOCKS * COMPS, LANES), jnp.float32),
        ],
        compiler_params=pltpu.CompilerParams(vmem_limit_bytes=16 * 1024 * 1024),
        name="sources",
    )(own_wind, jnp.asarray(trig), jnp.asarray(coef), rb)
    return out.T


def solution(mesh):
    return jax.shard_map(
        body,
        mesh=mesh,
        in_specs=(
            P("comp", None, "band", None),
            P("band", None),
            P(),
            P(None, "band", None),
            P(None, "band", None),
            P(None, "band", None),
            P("band", None),
            P("band", None),
        ),
        out_specs=P(None, ("comp", "band")),
        check_vma=False,
    )
```

```python
import math

import jax
import jax.numpy as jnp
import numpy as np
from jax import lax
from jax.experimental import pallas as pl
from jax.experimental.pallas import tpu as pltpu
from jax.sharding import PartitionSpec as P

GROWTH_RATE = 0.05
DAMPING = 1.5
TURNING_SCALE = 0.5

FREQS = 2
LANES = 128
ND = 36
ROWS = 4
NLON = 1440
TILES = 12
GROUPS = ROWS * TILES
BLOCKS = 16
SLOTS = 315
STEPS = 96
COMPS = FREQS * ND
PACK = 192
CHUNKS = 4
PER = TILES // CHUNKS
SIDE = 4

AT_TILE, AT_GROUP, AT_KEEP, AT_LAST = 0, 128, 256, 384
AT_RANK, AT_LEN, AT_FIRST, AT_COUNT = 512, 640, 768, 896
AT_SPOT = 1024

(F_SEA, F_CX, F_CY, F_CUR0, F_CUR1, F_T0, F_T1, F_W0, F_W1) = range(9)

MESH = pl.DeviceIdType.MESH


def angles():
    heading = (np.arange(ND, dtype=np.float32) * np.float32(2.0 * math.pi / ND)).astype(np.float64)
    return (np.cos(heading).astype(np.float32), np.sin(heading).astype(np.float32))


def upwind12(far_behind, behind, centre, ahead, far_ahead, speed):
    forward = speed > 0
    down = jnp.where(forward, ahead, behind)
    up = jnp.where(forward, behind, ahead)
    far = jnp.where(forward, far_behind, far_ahead)
    return jnp.abs(speed) * ((2.0 * down + far) + (3.0 * centre - 6.0 * up))


OFFSETS = sorted(
    [(a, b) for a in range(SIDE) for b in range(SIDE) if a or b],
    key=lambda o: -(min(o[0], SIDE - o[0]) + min(o[1], SIDE - o[1])),
)


def step_kernel(
    trig_ref, tab_ref, coef_ref, spec_ref, fields_ref, depth_ref, gs_ref, stretch_ref, loc_ref,
    rb_ref,
    x_ref, adv_ref, t_ref, stage_ref, idx_ref, dec_ref, fl_ref, hs_ref, hr_ref, sq_ref, part_ref, total_ref, level_ref, yr_ref, zr_ref, sb_ref,
    halo_send, halo_recv, sum_send, sum_recv, send_sem, recv_sem,
):
    lane = lax.broadcasted_iota(jnp.int32, (8, LANES), 1)
    sub = lax.broadcasted_iota(jnp.int32, (8, LANES), 0)
    row = sub // 2
    tail = NLON - (TILES - 1) * LANES
    me = lax.axis_index("comp")
    band = lax.axis_index("band")
    bands = lax.axis_size("band")
    z, y = me // SIDE, lax.rem(me, SIDE)
    north = lax.rem(band + 1, bands)
    south = lax.rem(band + bands - 1, bands)

    def peer(o):
        return lax.rem(z + o[0], SIDE) * SIDE + lax.rem(y + o[1], SIDE)

    barrier = pltpu.get_barrier_semaphore()
    for b in (north, south):
        pl.semaphore_signal(barrier, inc=1, device_id={"band": b}, device_id_type=MESH)
    for o in OFFSETS:
        pl.semaphore_signal(barrier, inc=1, device_id={"comp": peer(o)}, device_id_type=MESH)

    for j in range(TILES):
        cel = jnp.take_along_axis(gs_ref[...], depth_ref[j], axis=1)
        sixth = cel * (1.0 / 6.0)
        fl_ref[F_SEA, j] = fields_ref[0, j]
        fl_ref[F_CX, j] = sixth * stretch_ref[...]
        fl_ref[F_CY, j] = sixth
        fl_ref[F_CUR0, j] = fields_ref[1, j] * (1.0 / 6.0)
        fl_ref[F_CUR1, j] = fields_ref[2, j] * (1.0 / 6.0)
        fl_ref[F_T0, j] = (TURNING_SCALE * sixth) * fields_ref[3, j]
        fl_ref[F_T1, j] = (TURNING_SCALE * sixth) * fields_ref[4, j]

    even = lax.rem(sub, 2) == 0
    grow_a = jnp.where(even, coef_ref[0, FREQS * me], coef_ref[0, FREQS * me + 1])
    grow_b = jnp.where(even, coef_ref[1, FREQS * me], coef_ref[1, FREQS * me + 1])

    for j in range(TILES):
        fl_ref[F_W0, j] = fields_ref[5, j] * grow_a
        fl_ref[F_W1, j] = fields_ref[6, j] * grow_a

    def load(d, carry):
        base = pl.multiple_of(8 * d, 8)
        for j in range(TILES):
            width = LANES if j < TILES - 1 else tail
            for f in range(FREQS):
                v = spec_ref[f, d, :, pl.ds(j * LANES, width)].astype(jnp.float32)
                x_ref[j, pl.ds(base + f, 4, stride=2), pl.ds(0, width)] = v
        return carry

    lax.fori_loop(0, ND, load, 0)

    def prepare(q, carry):
        base = pl.multiple_of(32 * q, 32)
        first = [None] * 4
        for j in range(TILES):
            v = [x_ref[j, pl.ds(base + 8 * i, 8), :] for i in range(4)]
            if j == TILES - 1:
                v = [jnp.where(lane < tail, w, 0.0) for w in v]
            v = [w * fl_ref[F_SEA, j] for w in v]
            if j == 0:
                first = v
            if j == TILES - 1:
                v = [
                    jnp.where(
                        lane < tail,
                        w,
                        jnp.where(lane < tail + 2, pltpu.roll(a, tail, 1), pltpu.roll(w, LANES - tail, 1)),
                    )
                    for w, a in zip(v, first)
                ]
            for i in range(4):
                x_ref[j, pl.ds(base + 8 * i, 8), :] = v[i]
            turned = [pltpu.roll(w, 4, 0) for w in v]
            low = [jnp.where(sub < 4, v[i], turned[i + 1]) for i in (0, 2)]
            high = [jnp.where(sub < 4, turned[i], v[i + 1]) for i in (0, 2)]
            rows = pl.ds(pl.multiple_of(16 * q, 16), 16)
            hs_ref[0, j, rows, :] = jnp.concatenate(low, axis=0).astype(jnp.bfloat16)
            hs_ref[1, j, rows, :] = jnp.concatenate(high, axis=0).astype(jnp.bfloat16)
        return carry

    lax.fori_loop(0, ND // 4, prepare, 0)

    pl.semaphore_wait(barrier, len(OFFSETS) + 2)
    halos = []
    for c in range(CHUNKS):
        for side, b in ((0, south), (1, north)):
            copy = pltpu.make_async_remote_copy(
                src_ref=hs_ref.at[side, pl.ds(PER * c, PER)],
                dst_ref=hr_ref.at[side, pl.ds(PER * c, PER)],
                send_sem=halo_send.at[side, c],
                recv_sem=halo_recv.at[side, c],
                device_id={"band": b},
                device_id_type=MESH,
            )
            copy.start()
            halos.append(copy)

    def along(d, carry):
        base = pl.multiple_of(8 * d, 8)
        cos_d = trig_ref[0, d]
        x = [x_ref[j, pl.ds(base, 8), :] for j in range(TILES)]
        r1 = [pltpu.roll(v, 1, 1) for v in x]
        r2 = [pltpu.roll(v, 2, 1) for v in x]
        l1 = [pltpu.roll(v, LANES - 1, 1) for v in x]
        l2 = [pltpu.roll(v, LANES - 2, 1) for v in x]
        for j in range(TILES):
            before, after = (j - 1) % TILES, (j + 1) % TILES
            behind = jnp.where(lane < 1, r1[before], r1[j])
            far_behind = jnp.where(lane < 2, r2[before], r2[j])
            ahead = jnp.where(lane >= LANES - 1, l1[after], l1[j])
            far_ahead = jnp.where(lane >= LANES - 2, l2[after], l2[j])
            speed = fl_ref[F_CX, j] * cos_d + fl_ref[F_CUR0, j]
            out = x[j] - upwind12(far_behind, behind, x[j], ahead, far_ahead, speed)
            if j == TILES - 1:
                out = jnp.where(lane < tail, out, 0.0)
            adv_ref[j, pl.ds(base, 8), :] = out
        return carry

    lax.fori_loop(0, ND, along, 0)

    keep_dn = (band < bands - 1).astype(jnp.float32)
    keep_up = (band > 0).astype(jnp.float32)
    zero = jnp.zeros((8, LANES), jnp.float32)

    for c in range(CHUNKS):
        halos[2 * c].wait_recv()
        halos[2 * c + 1].wait_recv()

        def across(q, carry):
            rows = pl.ds(pl.multiple_of(16 * q, 16), 16)
            base = pl.multiple_of(32 * q, 32)
            for j in range(PER * c, PER * c + PER):
                dn = hr_ref[0, j, rows, :].astype(jnp.float32) * keep_dn
                up = hr_ref[1, j, rows, :].astype(jnp.float32) * keep_up
                for i in range(4):
                    a, b = dn[8 * (i // 2) : 8 * (i // 2) + 8], up[8 * (i // 2) : 8 * (i // 2) + 8]
                    if i % 2 == 0:
                        h = jnp.where(sub < 4, a, pltpu.roll(b, 4, 0))
                    else:
                        h = jnp.where(sub < 4, pltpu.roll(a, 4, 0), b)
                    here = pl.ds(base + 8 * i, 8)
                    v = x_ref[j, here, :]
                    ahead = pltpu.roll(jnp.where(row == 0, h, v), 6, 0)
                    far_ahead = pltpu.roll(jnp.where(row < 2, h, v), 4, 0)
                    far_behind = pltpu.roll(jnp.where(row < 2, v, h), 4, 0)
                    behind = pltpu.roll(jnp.where(row == 3, h, v), 2, 0)
                    speed = fl_ref[F_CY, j] * trig_ref[1, 4 * q + i] + fl_ref[F_CUR1, j]
                    flux = upwind12(far_behind, behind, v, ahead, far_ahead, speed)
                    adv_ref[j, here, :] = (adv_ref[j, here, :] - flux) * fl_ref[F_SEA, j]
            return carry

        lax.fori_loop(0, ND // 4, across, 0)

        def refract(d, sums):
            cos_d = trig_ref[0, d]
            sin_d = trig_ref[1, d]

            def at(shift):
                return pl.multiple_of(8 * lax.rem(d + (shift + ND), ND), 8)

            places = [at(s) for s in (-2, -1, 0, 1, 2)]
            sums = list(sums)
            for j in range(PER * c, PER * c + PER):
                values = [adv_ref[j, pl.ds(p, 8), :] for p in places]
                speed = fl_ref[F_T0, j] * sin_d - fl_ref[F_T1, j] * cos_d
                out = (values[2] - upwind12(*values, speed)) * fl_ref[F_SEA, j]
                sums[j - PER * c] = sums[j - PER * c] + out * out
                push = fl_ref[F_W0, j] * cos_d + fl_ref[F_W1, j] * sin_d
                t_ref[j, pl.ds(d, 8, stride=ND), :] = out * jnp.exp(jnp.maximum(push - grow_b, 0.0))
            return tuple(sums)

        sums = lax.fori_loop(0, ND, refract, (zero,) * PER)
        for i in range(PER):
            j = PER * c + i
            sq_ref[...] = sums[i] + pltpu.roll(sums[i], 7, 0)
            part_ref[pl.ds(4 * j, 4), :] = sq_ref[pl.ds(0, 4, stride=2), :]

    def reduce_start(axis, src, dst):
        copies = []
        for i in range(1, SIDE):
            o = (0, i) if axis == 0 else (i, 0)
            copy = pltpu.make_async_remote_copy(
                src_ref=src,
                dst_ref=dst.at[i - 1],
                send_sem=sum_send.at[axis, i - 1],
                recv_sem=sum_recv.at[axis, i - 1],
                device_id={"comp": peer(o)},
                device_id_type=MESH,
            )
            copy.start()
            copies.append(copy)
        return copies

    t_rows = t_ref.reshape(GROUPS, COMPS, LANES)

    def step(k, carry):
        tile = tab_ref[AT_TILE + k]
        group = tab_ref[AT_GROUP + k]
        keep = tab_ref[AT_KEEP + k].astype(jnp.float32)
        spot = tab_ref[AT_SPOT + k]
        local = lane + (tab_ref[AT_RANK + tile] - tab_ref[AT_FIRST + group])
        valid = (lane < tab_ref[AT_LEN + tile]) & (local >= 0) & (local < tab_ref[AT_COUNT + group])
        local = jnp.clip(local, 0, LANES - 1)
        idx = jnp.take_along_axis(loc_ref[group], local, axis=1)
        idx_ref[k] = jnp.where(valid, idx, -1)
        parts = []
        for m in range(COMPS // 8):
            data = t_rows[spot, pl.ds(8 * m, 8), :]
            got = jnp.take_along_axis(data, idx, axis=1)
            part = jnp.where(valid, got, carry[m] * keep)
            stage_ref[k, pl.ds(8 * m, 8), :] = part
            parts.append(part)
        return tuple(parts)

    sums_y = reduce_start(0, part_ref, yr_ref)
    carry = lax.fori_loop(0, STEPS // 2, step, (zero,) * (COMPS // 8), unroll=8)
    for copy in sums_y:
        copy.wait()
    for m in range(GROUPS // 8):
        rows = pl.ds(8 * m, 8)
        total_ref[rows, :] = (part_ref[rows, :] + yr_ref[0, rows, :]) + (yr_ref[1, rows, :] + yr_ref[2, rows, :])
    sums_z = reduce_start(1, total_ref, zr_ref)
    lax.fori_loop(STEPS // 2, STEPS, step, carry, unroll=8)
    for copy in sums_z:
        copy.wait()
    for m in range(GROUPS // 8):
        rows = pl.ds(8 * m, 8)
        total = (total_ref[rows, :] + zr_ref[0, rows, :]) + (zr_ref[1, rows, :] + zr_ref[2, rows, :])
        total = jnp.sqrt(total * (1.0 / (BLOCKS * COMPS)) + 1e-6)
        for i in range(8):
            level_ref[8 * m + i] = jnp.broadcast_to(total[i : i + 1], (8, LANES))

    def strengths(k, acc):
        keep = tab_ref[AT_KEEP + k].astype(jnp.float32)
        idx = idx_ref[k]
        got = jnp.take_along_axis(level_ref[tab_ref[AT_SPOT + k]], jnp.maximum(idx, 0), axis=1)
        acc = jnp.where(idx >= 0, got, acc * keep)
        dec_ref[k] = acc
        return acc

    lax.fori_loop(0, STEPS, strengths, zero, unroll=8)

    fade0 = coef_ref[2, FREQS * me]
    fade1 = coef_ref[2, FREQS * me + 1]

    def block(c, store):
        places = [tab_ref[AT_LAST + 3 * c + j] for j in range(3)]
        rows = []
        for j in range(3):
            s = dec_ref[places[j]]
            e0 = jnp.exp(-fade0 * s)
            e1 = jnp.exp(-fade1 * s)
            mixed = jnp.where(sub < 4, e0, e1)
            values = []
            for m in range(COMPS // 8):
                e = e0 if m < 4 else (mixed if m == 4 else e1)
                values.append(stage_ref[places[j], pl.ds(8 * m, 8), :] * e)
            if j < 2:
                rows += values
            else:
                for m in range(5):
                    v = values[m]
                    if m < 4:
                        v = jnp.where(lane < 64, v, pltpu.roll(values[5 + m], 64, 1))
                    rows.append(v)
                rows.append(zero)
        for m in range(PACK // 16):
            store(m, jnp.concatenate(rows[2 * m : 2 * m + 2], axis=0).astype(jnp.bfloat16))

    copies = []
    for i, o in enumerate(OFFSETS):
        other = peer(o)

        def put(m, v):
            sb_ref[i, pl.ds(16 * m, 16), :] = v

        block(other, put)
        copy = pltpu.make_async_remote_copy(
            src_ref=sb_ref.at[i],
            dst_ref=rb_ref.at[me],
            send_sem=send_sem.at[i],
            recv_sem=recv_sem.at[i],
            device_id={"comp": other},
            device_id_type=MESH,
        )
        copy.start()
        copies.append(copy)

    def put_own(m, v):
        rb_ref[me, pl.ds(16 * m, 16), :] = v

    block(me, put_own)
    for copy in halos:
        copy.wait_send()
    for copy in copies:
        copy.wait()


def finish_kernel(rb_ref, out_ref, v_ref):
    def spread(i, carry):
        base = pl.multiple_of(COMPS * i, 8)
        v = rb_ref[i].astype(jnp.float32)
        for j in range(2):
            v_ref[j, pl.ds(base, COMPS), :] = v[COMPS * j : COMPS * (j + 1)]
        v_ref[2, pl.ds(base, 40), :] = v[2 * COMPS : 2 * COMPS + 40]
        v_ref[2, pl.ds(base + 40, 32), :] = pltpu.roll(v[2 * COMPS : 2 * COMPS + 32], 64, 1)
        return carry

    lax.fori_loop(0, BLOCKS, spread, 0, unroll=4)
    for m in range(BLOCKS * COMPS // LANES):
        for j in range(3):
            block = v_ref[j, pl.ds(LANES * m, LANES), :].T.astype(jnp.bfloat16)
            rows = min(LANES, SLOTS - LANES * j)
            out_ref[pl.ds(LANES * j, rows), pl.ds(LANES * m, LANES)] = block[:rows]


def tables(land_mask, counts):
    sea = (land_mask == 0).astype(jnp.float32)
    padded = jnp.pad(sea, ((0, 0), (0, TILES * LANES - NLON))).reshape(GROUPS, LANES)
    lanes = np.arange(LANES)
    upper = (lanes[:, None] <= lanes[None, :]).astype(np.float32)
    inclusive = jnp.dot(padded, upper, preferred_element_type=jnp.float32).astype(jnp.int32)
    local = jnp.sum((inclusive[:, :, None] <= lanes[None, None, :].astype(np.int32)).astype(jnp.int32), axis=1)
    local = jnp.broadcast_to(jnp.minimum(local, LANES - 1)[:, None, :], (GROUPS, 8, LANES))
    count = inclusive[:, LANES - 1]
    groups = np.arange(GROUPS)
    ends = jnp.sum(jnp.where(groups[None, :] <= groups[:, None], count[None, :], 0), axis=1)
    first = ends - count
    blocks = np.arange(BLOCKS)
    starts = jnp.sum(jnp.where(blocks[None, :] < blocks[:, None], counts[None, :], 0), axis=1)
    offset = (np.arange(3) * LANES).astype(np.int32)
    rank = (starts[:, None] + offset[None, :]).reshape(-1)
    length = jnp.clip(counts[:, None] - offset[None, :], 0, LANES).reshape(-1)
    last_rank = rank + jnp.maximum(length, 1) - 1
    low = jnp.minimum(jnp.sum((ends[None, :] <= rank[:, None]).astype(jnp.int32), axis=1), GROUPS - 1)
    high = jnp.minimum(jnp.sum((ends[None, :] <= last_rank[:, None]).astype(jnp.int32), axis=1), GROUPS - 1)
    width = jnp.where(length > 0, high - low + 1, 1)
    tiles = np.arange(3 * BLOCKS)
    stop = jnp.sum(jnp.where(tiles[None, :] <= tiles[:, None], width[None, :], 0), axis=1)
    steps = np.arange(LANES).astype(np.int32)
    tile = jnp.sum((stop[None, :] <= steps[:, None]).astype(jnp.int32), axis=1)
    tile = jnp.minimum(tile, 3 * BLOCKS - 1)
    hit = tile[:, None] == tiles[None, :].astype(np.int32)
    group = steps + jnp.sum(jnp.where(hit, (low - (stop - width))[None, :], 0), axis=1)
    group = jnp.clip(group, 0, GROUPS - 1)
    begin = jnp.sum(jnp.where(hit, (stop - width)[None, :], 0), axis=1)
    keep = (steps > begin).astype(jnp.int32)

    def wide(x):
        return jnp.pad(x.astype(jnp.int32), (0, LANES - x.shape[0]))

    table = jnp.concatenate(
        [tile, group, keep, wide(stop - 1), wide(rank), wide(length), wide(first), wide(count), (group % TILES) * ROWS + group // TILES]
    )
    return table, local


def per_cell(x):
    lead = x.shape[:-2]
    x = jnp.pad(x, ((0, 0),) * (x.ndim - 1) + ((0, TILES * LANES - NLON),))
    x = x.reshape(lead + (ROWS, 1, TILES, LANES))
    x = jnp.broadcast_to(x, lead + (ROWS, FREQS, TILES, LANES))
    x = jnp.moveaxis(x, -2, len(lead))
    return x.reshape(lead + (TILES, 2 * ROWS, LANES))


def body(spectra, depth_class, group_speed, current, depth_slope, wind, land_mask, block_counts):
    comp_index = lax.axis_index("comp")
    band_index = lax.axis_index("band")
    bands = lax.axis_size("band")
    cos_t, sin_t = angles()

    table, local = tables(land_mask, block_counts[0])
    fields = per_cell(
        jnp.concatenate([(land_mask == 0).astype(jnp.float32)[None], current, depth_slope, wind], axis=0)
    )
    depth = per_cell(depth_class)
    own = lax.dynamic_slice_in_dim(group_speed, comp_index * FREQS, FREQS, 1)
    own = jnp.pad(own.T, ((0, 0), (0, LANES - own.shape[0])))
    speeds = jnp.tile(own, (ROWS, 1))
    row_ids = (band_index * ROWS + jnp.arange(ROWS, dtype=jnp.int32)).astype(jnp.float32)
    latitude = (-60.0 + 120.0 * (row_ids + 0.5) / (ROWS * bands)) * (math.pi / 180.0)
    stretch = jnp.broadcast_to(jnp.repeat(1.0 / jnp.cos(latitude), FREQS)[:, None], (8, LANES))

    angular = 2.0 * math.pi * 0.0418 * np.power(1.1, np.arange(BLOCKS * FREQS, dtype=np.float64))
    ratio = angular / angular[-1]
    phase = 9.81 / angular
    coef = np.stack([GROWTH_RATE * ratio / phase, GROWTH_RATE * ratio, DAMPING * ratio]).astype(np.float32)

    vmem = pl.BlockSpec(memory_space=pltpu.VMEM)
    smem = pl.BlockSpec(memory_space=pltpu.SMEM)
    f32, bf16 = jnp.float32, jnp.bfloat16
    dma = pltpu.SemaphoreType.DMA
    rb = pl.pallas_call(
        step_kernel,
        out_shape=jax.ShapeDtypeStruct((BLOCKS, PACK, LANES), bf16),
        in_specs=[smem] * 3 + [vmem] * 6,
        out_specs=vmem,
        scratch_shapes=[
            pltpu.VMEM((TILES, 8 * ND, LANES), f32),
            pltpu.VMEM((TILES, 8 * ND, LANES), f32),
            pltpu.VMEM((TILES, 8 * ND, LANES), f32),
            pltpu.VMEM((STEPS, COMPS, LANES), f32),
            pltpu.VMEM((STEPS, 8, LANES), jnp.int32),
            pltpu.VMEM((STEPS, 8, LANES), f32),
            pltpu.VMEM((9, TILES, 8, LANES), f32),
            pltpu.VMEM((2, TILES, 4 * ND, LANES), bf16),
            pltpu.VMEM((2, TILES, 4 * ND, LANES), bf16),
            pltpu.VMEM((8, LANES), f32),
            pltpu.VMEM((GROUPS, LANES), f32),
            pltpu.VMEM((GROUPS, LANES), f32),
            pltpu.VMEM((GROUPS, 8, LANES), f32),
            pltpu.VMEM((SIDE - 1, GROUPS, LANES), f32),
            pltpu.VMEM((SIDE - 1, GROUPS, LANES), f32),
            pltpu.VMEM((BLOCKS - 1, PACK, LANES), bf16),
            dma((2, CHUNKS)),
            dma((2, CHUNKS)),
            dma((2, SIDE - 1)),
            dma((2, SIDE - 1)),
            dma((BLOCKS - 1,)),
            dma((BLOCKS - 1,)),
        ],
        compiler_params=pltpu.CompilerParams(
            collective_id=0, has_side_effects=True, vmem_limit_bytes=40 * 1024 * 1024
        ),
        name="wave_step",
    )(
        jnp.asarray(np.stack([cos_t, sin_t])),
        table,
        jnp.asarray(coef),
        spectra,
        fields,
        depth,
        speeds,
        stretch,
        local,
    )

    out = pl.pallas_call(
        finish_kernel,
        out_shape=jax.ShapeDtypeStruct((SLOTS, BLOCKS * COMPS), bf16),
        in_specs=[vmem],
        out_specs=vmem,
        scratch_shapes=[pltpu.VMEM((3, BLOCKS * COMPS, LANES), f32)],
        compiler_params=pltpu.CompilerParams(vmem_limit_bytes=16 * 1024 * 1024),
        name="finish",
    )(rb)
    return out.T


def solution(mesh):
    return jax.shard_map(
        body,
        mesh=mesh,
        in_specs=(
            P("comp", None, "band", None),
            P("band", None),
            P(),
            P(None, "band", None),
            P(None, "band", None),
            P(None, "band", None),
            P("band", None),
            P("band", None),
        ),
        out_specs=P(None, ("comp", "band")),
        check_vma=False,
    )
```

```python
import math

import jax
import jax.numpy as jnp
import numpy as np
from jax import lax
from jax.experimental import pallas as pl
from jax.experimental.pallas import tpu as pltpu
from jax.sharding import PartitionSpec as P

GROWTH_RATE = 0.05
DAMPING = 1.5
TURNING_SCALE = 0.5

FREQS = 2
LANES = 128
ND = 36
ROWS = 4
NLON = 1440
TILES = 12
GROUPS = ROWS * TILES
BLOCKS = 16
SLOTS = 315
DEPTHS = 64
STEPS = 96
COMPS = FREQS * ND
PACK = 192
CHUNKS = 4
PER = TILES // CHUNKS
SIDE = 4

AT_SPOT, AT_KEEP, AT_DELTA, AT_LEN, AT_COUNT, AT_LAST = range(6)

(F_SEA, F_CX, F_CY, F_CUR0, F_CUR1, F_T0, F_T1, F_W0, F_W1) = range(9)

MESH = pl.DeviceIdType.MESH


def angles():
    heading = (np.arange(ND, dtype=np.float32) * np.float32(2.0 * math.pi / ND)).astype(np.float64)
    return (np.cos(heading).astype(np.float32), np.sin(heading).astype(np.float32))


def upwind12(far_behind, behind, centre, ahead, far_ahead, speed):
    forward = speed > 0
    down = jnp.where(forward, ahead, behind)
    up = jnp.where(forward, behind, ahead)
    far = jnp.where(forward, far_behind, far_ahead)
    return jnp.abs(speed) * ((2.0 * down + far) + (3.0 * centre - 6.0 * up))


OFFSETS = sorted(
    [(a, b) for a in range(SIDE) for b in range(SIDE) if a or b],
    key=lambda o: -(min(o[0], SIDE - o[0]) + min(o[1], SIDE - o[1])),
)


def step_kernel(
    trig_ref, coef_ref, stretch_ref, counts_ref, spec_ref, depth_ref, speed_ref, current_ref, slope_ref, wind_ref, land_ref,
    rb_ref,
    gs_ref, raw_ref, cls_ref, flag_ref, tabv_ref, tab_ref, loc_ref, x_ref, adv_ref, t_ref, stage_ref, idx_ref, dec_ref, fl_ref, hs_ref, hr_ref, sq_ref, part_ref, total_ref, level_ref, yr_ref, zr_ref, sb_ref,
    tab_sem, halo_send, halo_recv, sum_send, sum_recv, send_sem, recv_sem,
):
    lane = lax.broadcasted_iota(jnp.int32, (8, LANES), 1)
    sub = lax.broadcasted_iota(jnp.int32, (8, LANES), 0)
    row = sub // 2
    tail = NLON - (TILES - 1) * LANES
    me = lax.axis_index("comp")
    band = lax.axis_index("band")
    bands = lax.axis_size("band")
    z, y = me // SIDE, lax.rem(me, SIDE)
    north = lax.rem(band + 1, bands)
    south = lax.rem(band + bands - 1, bands)

    def peer(o):
        return lax.rem(z + o[0], SIDE) * SIDE + lax.rem(y + o[1], SIDE)

    barrier = pltpu.get_barrier_semaphore()
    for b in (north, south):
        pl.semaphore_signal(barrier, inc=1, device_id={"band": b}, device_id_type=MESH)
    for o in OFFSETS:
        pl.semaphore_signal(barrier, inc=1, device_id={"comp": peer(o)}, device_id_type=MESH)

    even = lax.rem(sub, 2) == 0
    even_half = lax.rem(lax.broadcasted_iota(jnp.int32, (8, DEPTHS), 0), 2) == 0
    gs_ref[:, pl.ds(0, DEPTHS)] = jnp.where(
        even_half,
        jnp.broadcast_to(speed_ref[pl.ds(FREQS * me, 1), :], (8, DEPTHS)),
        jnp.broadcast_to(speed_ref[pl.ds(FREQS * me + 1, 1), :], (8, DEPTHS)),
    )
    grow_a = jnp.where(even, coef_ref[0, FREQS * me], coef_ref[0, FREQS * me + 1])
    grow_b = jnp.where(even, coef_ref[1, FREQS * me], coef_ref[1, FREQS * me + 1])
    stretch = jnp.where(row == 0, stretch_ref[ROWS * band], stretch_ref[ROWS * band + 1])
    stretch = jnp.where(row == 2, stretch_ref[ROWS * band + 2], stretch)
    stretch = jnp.where(row == 3, stretch_ref[ROWS * band + 3], stretch)
    flag_ref[...] = jnp.zeros((LANES, LANES), jnp.float32)
    for j in range(TILES):
        width = LANES if j < TILES - 1 else tail
        cols = pl.ds(j * LANES, width)
        sea = (land_ref[:, cols] == 0).astype(jnp.float32)
        flag_ref[pl.ds(ROWS * j, ROWS), pl.ds(0, width)] = sea
        parts = [sea] + [ref[i, :, cols] for ref in (current_ref, slope_ref, wind_ref) for i in range(2)]
        for n, v in enumerate(parts):
            for f in range(FREQS):
                raw_ref[j, pl.ds(8 * n + f, 4, stride=2), pl.ds(0, width)] = v
        v = depth_ref[:, cols]
        for f in range(FREQS):
            cls_ref[j, pl.ds(f, 4, stride=2), pl.ds(0, width)] = v
    for j in range(TILES):
        def raw(n):
            v = raw_ref[j, pl.ds(8 * n, 8), :]
            return v if j < TILES - 1 else jnp.where(lane < tail, v, 0.0)

        cls = cls_ref[j]
        if j == TILES - 1:
            cls = jnp.where(lane < tail, cls, 0)
        cel = jnp.take_along_axis(gs_ref[...], cls, axis=1)
        sixth = cel * (1.0 / 6.0)
        fl_ref[F_SEA, j] = raw(0)
        fl_ref[F_CX, j] = sixth * stretch
        fl_ref[F_CY, j] = sixth
        fl_ref[F_CUR0, j] = raw(1) * (1.0 / 6.0)
        fl_ref[F_CUR1, j] = raw(2) * (1.0 / 6.0)
        fl_ref[F_T0, j] = (TURNING_SCALE * sixth) * raw(3)
        fl_ref[F_T1, j] = (TURNING_SCALE * sixth) * raw(4)
        fl_ref[F_W0, j] = raw(5) * grow_a
        fl_ref[F_W1, j] = raw(6) * grow_a

    def load(d, carry):
        base = pl.multiple_of(8 * d, 8)
        for j in range(TILES):
            width = LANES if j < TILES - 1 else tail
            for f in range(FREQS):
                v = spec_ref[f, d, :, pl.ds(j * LANES, width)].astype(jnp.float32)
                x_ref[j, pl.ds(base + f, 4, stride=2), pl.ds(0, width)] = v
        return carry

    lax.fori_loop(0, ND, load, 0)

    def prepare(q, carry):
        base = pl.multiple_of(32 * q, 32)
        first = [None] * 4
        for j in range(TILES):
            v = [x_ref[j, pl.ds(base + 8 * i, 8), :] for i in range(4)]
            if j == TILES - 1:
                v = [jnp.where(lane < tail, w, 0.0) for w in v]
            v = [w * fl_ref[F_SEA, j] for w in v]
            if j == 0:
                first = v
            if j == TILES - 1:
                v = [
                    jnp.where(
                        lane < tail,
                        w,
                        jnp.where(lane < tail + 2, pltpu.roll(a, tail, 1), pltpu.roll(w, LANES - tail, 1)),
                    )
                    for w, a in zip(v, first)
                ]
            for i in range(4):
                x_ref[j, pl.ds(base + 8 * i, 8), :] = v[i]
            turned = [pltpu.roll(w, 4, 0) for w in v]
            low = [jnp.where(sub < 4, v[i], turned[i + 1]) for i in (0, 2)]
            high = [jnp.where(sub < 4, turned[i], v[i + 1]) for i in (0, 2)]
            rows = pl.ds(pl.multiple_of(16 * q, 16), 16)
            hs_ref[0, j, rows, :] = jnp.concatenate(low, axis=0).astype(jnp.bfloat16)
            hs_ref[1, j, rows, :] = jnp.concatenate(high, axis=0).astype(jnp.bfloat16)
        return carry

    lax.fori_loop(0, ND // 4, prepare, 0)

    pl.semaphore_wait(barrier, len(OFFSETS) + 2)
    halos = []
    for c in range(CHUNKS):
        for side, b in ((0, south), (1, north)):
            copy = pltpu.make_async_remote_copy(
                src_ref=hs_ref.at[side, pl.ds(PER * c, PER)],
                dst_ref=hr_ref.at[side, pl.ds(PER * c, PER)],
                send_sem=halo_send.at[side, c],
                recv_sem=halo_recv.at[side, c],
                device_id={"band": b},
                device_id_type=MESH,
            )
            copy.start()
            halos.append(copy)

    build_tables(counts_ref, flag_ref, tabv_ref, loc_ref)
    table_copy = pltpu.make_async_copy(tabv_ref, tab_ref, tab_sem)
    table_copy.start()

    def along(d, carry):
        base = pl.multiple_of(8 * d, 8)
        cos_d = trig_ref[0, d]
        x = [x_ref[j, pl.ds(base, 8), :] for j in range(TILES)]
        r1 = [pltpu.roll(v, 1, 1) for v in x]
        r2 = [pltpu.roll(v, 2, 1) for v in x]
        l1 = [pltpu.roll(v, LANES - 1, 1) for v in x]
        l2 = [pltpu.roll(v, LANES - 2, 1) for v in x]
        for j in range(TILES):
            before, after = (j - 1) % TILES, (j + 1) % TILES
            behind = jnp.where(lane < 1, r1[before], r1[j])
            far_behind = jnp.where(lane < 2, r2[before], r2[j])
            ahead = jnp.where(lane >= LANES - 1, l1[after], l1[j])
            far_ahead = jnp.where(lane >= LANES - 2, l2[after], l2[j])
            speed = fl_ref[F_CX, j] * cos_d + fl_ref[F_CUR0, j]
            out = x[j] - upwind12(far_behind, behind, x[j], ahead, far_ahead, speed)
            if j == TILES - 1:
                out = jnp.where(lane < tail, out, 0.0)
            adv_ref[j, pl.ds(base, 8), :] = out
        return carry

    lax.fori_loop(0, ND, along, 0, unroll=2)

    keep_dn = (band < bands - 1).astype(jnp.float32)
    keep_up = (band > 0).astype(jnp.float32)
    zero = jnp.zeros((8, LANES), jnp.float32)

    for c in range(CHUNKS):
        halos[2 * c].wait_recv()
        halos[2 * c + 1].wait_recv()

        def across(q, carry):
            rows = pl.ds(pl.multiple_of(16 * q, 16), 16)
            base = pl.multiple_of(32 * q, 32)
            for j in range(PER * c, PER * c + PER):
                dn = hr_ref[0, j, rows, :].astype(jnp.float32) * keep_dn
                up = hr_ref[1, j, rows, :].astype(jnp.float32) * keep_up
                for i in range(4):
                    a, b = dn[8 * (i // 2) : 8 * (i // 2) + 8], up[8 * (i // 2) : 8 * (i // 2) + 8]
                    if i % 2 == 0:
                        h = jnp.where(sub < 4, a, pltpu.roll(b, 4, 0))
                    else:
                        h = jnp.where(sub < 4, pltpu.roll(a, 4, 0), b)
                    here = pl.ds(base + 8 * i, 8)
                    v = x_ref[j, here, :]
                    ahead = pltpu.roll(jnp.where(row == 0, h, v), 6, 0)
                    far_ahead = pltpu.roll(jnp.where(row < 2, h, v), 4, 0)
                    far_behind = pltpu.roll(jnp.where(row < 2, v, h), 4, 0)
                    behind = pltpu.roll(jnp.where(row == 3, h, v), 2, 0)
                    speed = fl_ref[F_CY, j] * trig_ref[1, 4 * q + i] + fl_ref[F_CUR1, j]
                    flux = upwind12(far_behind, behind, v, ahead, far_ahead, speed)
                    adv_ref[j, here, :] = (adv_ref[j, here, :] - flux) * fl_ref[F_SEA, j]
            return carry

        lax.fori_loop(0, ND // 4, across, 0)

        def refract(d, sums):
            cos_d = trig_ref[0, d]
            sin_d = trig_ref[1, d]

            def at(shift):
                return pl.multiple_of(8 * lax.rem(d + (shift + ND), ND), 8)

            places = [at(s) for s in (-2, -1, 0, 1, 2)]
            sums = list(sums)
            for j in range(PER * c, PER * c + PER):
                values = [adv_ref[j, pl.ds(p, 8), :] for p in places]
                speed = fl_ref[F_T0, j] * sin_d - fl_ref[F_T1, j] * cos_d
                out = (values[2] - upwind12(*values, speed)) * fl_ref[F_SEA, j]
                sums[j - PER * c] = sums[j - PER * c] + out * out
                push = fl_ref[F_W0, j] * cos_d + fl_ref[F_W1, j] * sin_d
                t_ref[j, pl.ds(d, 8, stride=ND), :] = out * jnp.exp(jnp.maximum(push - grow_b, 0.0))
            return tuple(sums)

        sums = lax.fori_loop(0, ND, refract, (zero,) * PER, unroll=3)
        for i in range(PER):
            j = PER * c + i
            sq_ref[...] = sums[i] + pltpu.roll(sums[i], 7, 0)
            part_ref[pl.ds(4 * j, 4), :] = sq_ref[pl.ds(0, 4, stride=2), :]

    def reduce_start(axis, src, dst):
        copies = []
        for i in range(1, SIDE):
            o = (0, i) if axis == 0 else (i, 0)
            copy = pltpu.make_async_remote_copy(
                src_ref=src,
                dst_ref=dst.at[i - 1],
                send_sem=sum_send.at[axis, i - 1],
                recv_sem=sum_recv.at[axis, i - 1],
                device_id={"comp": peer(o)},
                device_id_type=MESH,
            )
            copy.start()
            copies.append(copy)
        return copies

    t_rows = t_ref.reshape(GROUPS, COMPS, LANES)

    def step(k, carry):
        keep = tab_ref[AT_KEEP, k].astype(jnp.float32)
        spot = tab_ref[AT_SPOT, k]
        local = lane + tab_ref[AT_DELTA, k]
        valid = (lane < tab_ref[AT_LEN, k]) & (local >= 0) & (local < tab_ref[AT_COUNT, k])
        local = jnp.clip(local, 0, LANES - 1)
        idx = jnp.take_along_axis(loc_ref[spot], local, axis=1)
        idx_ref[k] = jnp.where(valid, idx, -1)
        parts = []
        for m in range(COMPS // 8):
            data = t_rows[spot, pl.ds(8 * m, 8), :]
            got = jnp.take_along_axis(data, idx, axis=1)
            part = jnp.where(valid, got, carry[m] * keep)
            stage_ref[k, pl.ds(8 * m, 8), :] = part
            parts.append(part)
        return tuple(parts)

    sums_y = reduce_start(0, part_ref, yr_ref)
    table_copy.wait()
    carry = lax.fori_loop(0, STEPS // 2, step, (zero,) * (COMPS // 8), unroll=8)
    for copy in sums_y:
        copy.wait()
    for m in range(GROUPS // 8):
        rows = pl.ds(8 * m, 8)
        total_ref[rows, :] = (part_ref[rows, :] + yr_ref[0, rows, :]) + (yr_ref[1, rows, :] + yr_ref[2, rows, :])
    sums_z = reduce_start(1, total_ref, zr_ref)
    lax.fori_loop(STEPS // 2, STEPS, step, carry, unroll=8)
    for copy in sums_z:
        copy.wait()
    for m in range(GROUPS // 8):
        rows = pl.ds(8 * m, 8)
        total = (total_ref[rows, :] + zr_ref[0, rows, :]) + (zr_ref[1, rows, :] + zr_ref[2, rows, :])
        total = jnp.sqrt(total * (1.0 / (BLOCKS * COMPS)) + 1e-6)
        for i in range(8):
            level_ref[8 * m + i] = jnp.broadcast_to(total[i : i + 1], (8, LANES))

    def strengths(k, acc):
        keep = tab_ref[AT_KEEP, k].astype(jnp.float32)
        idx = idx_ref[k]
        got = jnp.take_along_axis(level_ref[tab_ref[AT_SPOT, k]], jnp.maximum(idx, 0), axis=1)
        acc = jnp.where(idx >= 0, got, acc * keep)
        dec_ref[k] = acc
        return acc

    lax.fori_loop(0, STEPS, strengths, zero, unroll=8)

    fade0 = coef_ref[2, FREQS * me]
    fade1 = coef_ref[2, FREQS * me + 1]

    def block(c, store):
        places = [tab_ref[AT_LAST, 3 * c + j] for j in range(3)]
        rows = []
        for j in range(3):
            s = dec_ref[places[j]]
            e0 = jnp.exp(-fade0 * s)
            e1 = jnp.exp(-fade1 * s)
            mixed = jnp.where(sub < 4, e0, e1)
            values = []
            for m in range(COMPS // 8):
                e = e0 if m < 4 else (mixed if m == 4 else e1)
                values.append(stage_ref[places[j], pl.ds(8 * m, 8), :] * e)
            if j < 2:
                rows += values
            else:
                for m in range(5):
                    v = values[m]
                    if m < 4:
                        v = jnp.where(lane < 64, v, pltpu.roll(values[5 + m], 64, 1))
                    rows.append(v)
                rows.append(zero)
        for m in range(PACK // 16):
            store(m, jnp.concatenate(rows[2 * m : 2 * m + 2], axis=0).astype(jnp.bfloat16))

    copies = []
    for i, o in enumerate(OFFSETS):
        other = peer(o)

        def put(m, v):
            sb_ref[i, pl.ds(16 * m, 16), :] = v

        block(other, put)
        copy = pltpu.make_async_remote_copy(
            src_ref=sb_ref.at[i],
            dst_ref=rb_ref.at[me],
            send_sem=send_sem.at[i],
            recv_sem=recv_sem.at[i],
            device_id={"comp": other},
            device_id_type=MESH,
        )
        copy.start()
        copies.append(copy)

    def put_own(m, v):
        rb_ref[me, pl.ds(16 * m, 16), :] = v

    block(me, put_own)
    for copy in halos:
        copy.wait_send()
    for copy in copies:
        copy.wait()


def finish_kernel(rb_ref, out_ref, v_ref):
    def spread(i, carry):
        base = pl.multiple_of(COMPS * i, 8)
        v = rb_ref[i].astype(jnp.float32)
        for j in range(2):
            v_ref[j, pl.ds(base, COMPS), :] = v[COMPS * j : COMPS * (j + 1)]
        v_ref[2, pl.ds(base, 40), :] = v[2 * COMPS : 2 * COMPS + 40]
        v_ref[2, pl.ds(base + 40, 32), :] = pltpu.roll(v[2 * COMPS : 2 * COMPS + 32], 64, 1)
        return carry

    lax.fori_loop(0, BLOCKS, spread, 0, unroll=4)
    for m in range(BLOCKS * COMPS // LANES):
        for j in range(3):
            block = v_ref[j, pl.ds(LANES * m, LANES), :].T.astype(jnp.bfloat16)
            rows = min(LANES, SLOTS - LANES * j)
            out_ref[pl.ds(LANES * j, rows), pl.ds(LANES * m, LANES)] = block[:rows]


def build_tables(counts_ref, flag_ref, tabv_ref, loc_ref):
    f32, bf16, i32 = jnp.float32, jnp.bfloat16, jnp.int32
    sub = lax.broadcasted_iota(i32, (LANES, LANES), 0)
    lanes = lax.broadcasted_iota(i32, (LANES, LANES), 1)
    lane = lax.broadcasted_iota(i32, (8, LANES), 1)

    def order(i):
        return jnp.where(i < GROUPS, (i & (ROWS - 1)) * TILES + (i >> 2), i)

    def product(a, b, dims=(((1,), (0,)), ((), ()))):
        return lax.dot_general(a, b, dims, preferred_element_type=f32)

    upper = (sub <= lanes).astype(f32).astype(bf16)
    ones = jnp.ones((LANES, LANES), bf16)
    flags = flag_ref[...].astype(bf16)
    inclusive = product(flags, upper)
    count_rows = product(flags, ones)
    ends = product((order(lanes) <= order(sub)).astype(f32).astype(bf16), count_rows.astype(bf16))[:GROUPS]
    count = product(ones[:16], flags, (((1,), (1,)), ((), ())))
    first = product(count.astype(bf16), (order(sub) < order(lanes)).astype(f32).astype(bf16))
    count, first = count[:8].astype(i32), first[:8].astype(i32)

    wide = lanes[:GROUPS]
    shift = wide - (inclusive[:GROUPS].astype(i32) - 1)
    word = jnp.where(flag_ref[pl.ds(0, GROUPS), :] > 0, wide + LANES * shift + LANES * LANES, 0)
    for k in range(7):
        bit = LANES << k
        moved = pltpu.roll(word, LANES - (1 << k), 1)
        word = jnp.where((moved & bit) != 0, moved, jnp.where((word & bit) != 0, 0, word))
    word = word & (LANES - 1)
    for g in range(GROUPS):
        loc_ref[g] = jnp.broadcast_to(word[g : g + 1], (8, LANES))

    block = (lane * 171) >> 9
    part = lane - 3 * block
    size = jnp.zeros((8, LANES), i32)
    rank = jnp.zeros((8, LANES), i32)
    start = 0
    for c in range(BLOCKS):
        n = counts_ref[0, c]
        size = jnp.where(block == c, n, size)
        rank = jnp.where(block == c, start, rank)
        start = start + n
    rank = rank + LANES * part
    length = jnp.clip(size - LANES * part, 0, LANES)
    real = lane < 3 * BLOCKS

    def groups_before(r):
        hit = (ends <= r[:1].astype(f32)).astype(f32)
        return jnp.minimum(jnp.broadcast_to(jnp.sum(hit, axis=0, keepdims=True), (8, LANES)), GROUPS - 1.0)

    low = groups_before(rank)
    high = groups_before(rank + jnp.maximum(length, 1) - 1)
    width = jnp.where(real, jnp.where(length > 0, high - low + 1.0, 1.0), 0.0)
    stop = product(jnp.concatenate([width, width], axis=0).astype(bf16), upper)[:8]
    begin = stop - width
    column = jnp.sum(jnp.where(wide <= sub[:GROUPS], width[:1], 0.0), axis=1, keepdims=True)
    tile = jnp.sum((column <= wide.astype(f32)).astype(f32), axis=0, keepdims=True)
    tile = jnp.broadcast_to(jnp.minimum(tile, 3 * BLOCKS - 1.0), (8, LANES)).astype(i32)

    def at(values, index):
        return jnp.take_along_axis(values, index, axis=1)

    group = lane + at((low - begin).astype(i32), tile)
    group = jnp.clip(group, 0, GROUPS - 1)
    r = (group * 171) >> 11
    spot = ROWS * (group - TILES * r) + r
    tabv_ref[AT_SPOT : AT_SPOT + 1] = spot[:1]
    tabv_ref[AT_KEEP : AT_KEEP + 1] = (lane > at(begin.astype(i32), tile)).astype(i32)[:1]
    tabv_ref[AT_DELTA : AT_DELTA + 1] = (at(rank, tile) - at(first, spot))[:1]
    tabv_ref[AT_LEN : AT_LEN + 1] = at(length, tile)[:1]
    tabv_ref[AT_COUNT : AT_COUNT + 1] = at(count, spot)[:1]
    tabv_ref[AT_LAST : AT_LAST + 1] = jnp.clip((stop - 1.0).astype(i32), 0, STEPS - 1)[:1]
    tabv_ref[AT_LAST + 1 :] = jnp.zeros((7 - AT_LAST, LANES), i32)


def body(spectra, depth_class, group_speed, current, depth_slope, wind, land_mask, block_counts):
    cos_t, sin_t = angles()
    latitude = (-60.0 + 120.0 * (np.arange(ROWS * lax.axis_size("band")) + 0.5) / (ROWS * lax.axis_size("band"))) * (
        math.pi / 180.0
    )
    stretch = (1.0 / np.cos(latitude)).astype(np.float32)
    angular = 2.0 * math.pi * 0.0418 * np.power(1.1, np.arange(BLOCKS * FREQS, dtype=np.float64))
    ratio = angular / angular[-1]
    phase = 9.81 / angular
    coef = np.stack([GROWTH_RATE * ratio / phase, GROWTH_RATE * ratio, DAMPING * ratio]).astype(np.float32)

    vmem = pl.BlockSpec(memory_space=pltpu.VMEM)
    smem = pl.BlockSpec(memory_space=pltpu.SMEM)
    f32, bf16 = jnp.float32, jnp.bfloat16
    dma = pltpu.SemaphoreType.DMA
    rb = pl.pallas_call(
        step_kernel,
        out_shape=jax.ShapeDtypeStruct((BLOCKS, PACK, LANES), bf16),
        in_specs=[smem] * 4 + [vmem] * 7,
        out_specs=vmem,
        scratch_shapes=[
            pltpu.VMEM((8, LANES), f32),
            pltpu.VMEM((TILES, 8 * 7, LANES), f32),
            pltpu.VMEM((TILES, 8, LANES), jnp.int32),
            pltpu.VMEM((LANES, LANES), f32),
            pltpu.VMEM((8, LANES), jnp.int32),
            pltpu.SMEM((8, LANES), jnp.int32),
            pltpu.VMEM((GROUPS, 8, LANES), jnp.int32),
            pltpu.VMEM((TILES, 8 * ND, LANES), f32),
            pltpu.VMEM((TILES, 8 * ND, LANES), f32),
            pltpu.VMEM((TILES, 8 * ND, LANES), f32),
            pltpu.VMEM((STEPS, COMPS, LANES), f32),
            pltpu.VMEM((STEPS, 8, LANES), jnp.int32),
            pltpu.VMEM((STEPS, 8, LANES), f32),
            pltpu.VMEM((9, TILES, 8, LANES), f32),
            pltpu.VMEM((2, TILES, 4 * ND, LANES), bf16),
            pltpu.VMEM((2, TILES, 4 * ND, LANES), bf16),
            pltpu.VMEM((8, LANES), f32),
            pltpu.VMEM((GROUPS, LANES), f32),
            pltpu.VMEM((GROUPS, LANES), f32),
            pltpu.VMEM((GROUPS, 8, LANES), f32),
            pltpu.VMEM((SIDE - 1, GROUPS, LANES), f32),
            pltpu.VMEM((SIDE - 1, GROUPS, LANES), f32),
            pltpu.VMEM((BLOCKS - 1, PACK, LANES), bf16),
            dma,
            dma((2, CHUNKS)),
            dma((2, CHUNKS)),
            dma((2, SIDE - 1)),
            dma((2, SIDE - 1)),
            dma((BLOCKS - 1,)),
            dma((BLOCKS - 1,)),
        ],
        compiler_params=pltpu.CompilerParams(
            collective_id=0, has_side_effects=True, vmem_limit_bytes=40 * 1024 * 1024
        ),
        name="wave_step",
    )(
        jnp.asarray(np.stack([cos_t, sin_t])),
        jnp.asarray(coef),
        jnp.asarray(stretch),
        block_counts,
        spectra,
        depth_class,
        group_speed.T,
        current,
        depth_slope,
        wind,
        land_mask,
    )

    out = pl.pallas_call(
        finish_kernel,
        out_shape=jax.ShapeDtypeStruct((SLOTS, BLOCKS * COMPS), bf16),
        in_specs=[vmem],
        out_specs=vmem,
        scratch_shapes=[pltpu.VMEM((3, BLOCKS * COMPS, LANES), f32)],
        compiler_params=pltpu.CompilerParams(vmem_limit_bytes=16 * 1024 * 1024),
        name="finish",
    )(rb)
    return out.T


def solution(mesh):
    return jax.shard_map(
        body,
        mesh=mesh,
        in_specs=(
            P("comp", None, "band", None),
            P("band", None),
            P(),
            P(None, "band", None),
            P(None, "band", None),
            P(None, "band", None),
            P("band", None),
            P("band", None),
        ),
        out_specs=P(None, ("comp", "band")),
        check_vma=False,
    )
```

```python
import math

import jax
import jax.numpy as jnp
import numpy as np
from jax import lax
from jax.experimental import pallas as pl
from jax.experimental.pallas import tpu as pltpu
from jax.sharding import PartitionSpec as P

GROWTH_RATE = 0.05
DAMPING = 1.5
TURNING_SCALE = 0.5

FREQS = 2
LANES = 128
ND = 36
ROWS = 4
NLON = 1440
TILES = 12
GROUPS = ROWS * TILES
BLOCKS = 16
SLOTS = 315
DEPTHS = 64
STEPS = 96
COMPS = FREQS * ND
PACK = 192
CHUNKS = 4
PER = TILES // CHUNKS
SIDE = 4

AT_SPOT, AT_KEEP, AT_DELTA, AT_LEN, AT_COUNT, AT_LAST = range(6)

(F_SEA, F_CX, F_CY, F_CUR0, F_CUR1, F_T0, F_T1) = range(7)

MESH = pl.DeviceIdType.MESH


def angles():
    heading = (np.arange(ND, dtype=np.float32) * np.float32(2.0 * math.pi / ND)).astype(np.float64)
    return (np.cos(heading).astype(np.float32), np.sin(heading).astype(np.float32))


def upwind12(far_behind, behind, centre, ahead, far_ahead, speed):
    forward = speed > 0
    down = jnp.where(forward, ahead, behind)
    up = jnp.where(forward, behind, ahead)
    far = jnp.where(forward, far_behind, far_ahead)
    return jnp.abs(speed) * ((2.0 * down + far) + (3.0 * centre - 6.0 * up))


OFFSETS = sorted(
    [(a, b) for a in range(SIDE) for b in range(SIDE) if a or b],
    key=lambda o: -(min(o[0], SIDE - o[0]) + min(o[1], SIDE - o[1])),
)


def step_kernel(
    scalars_hbm, compass_hbm, counts_hbm, spec_hbm, depth_hbm, speed_hbm, current_hbm, slope_hbm, wind_hbm, land_hbm,
    rb_ref,
    scalars_ref, compass_ref, counts_ref, spec_ref, depth_ref, speed_ref, current_ref, slope_ref, wind_ref, land_ref,
    gust_ref, gusts_ref,
    gs_ref, raw_ref, cls_ref, flag_ref, tabv_ref, tab_ref, loc_ref, x_ref, adv_ref, t_ref, stage_ref, grown_ref, idx_ref, dec_ref, fl_ref, hs_ref, hr_ref, sq_ref, part_ref, total_ref, level_ref, yr_ref, zr_ref, sb_ref,
    in_sem, tab_sem, halo_send, halo_recv, sum_send, sum_recv, send_sem, recv_sem,
):
    arrivals = [
        pltpu.make_async_copy(src, dst, in_sem.at[i])
        for i, (src, dst) in enumerate(
            [
                (land_hbm, land_ref),
                (spec_hbm, spec_ref),
                (scalars_hbm, scalars_ref),
                (speed_hbm, speed_ref),
                (depth_hbm, depth_ref),
                (current_hbm, current_ref),
                (slope_hbm, slope_ref),
                (wind_hbm, wind_ref),
                (counts_hbm, counts_ref),
                (compass_hbm, compass_ref),
            ]
        )
    ]
    for copy in arrivals:
        copy.start()
    lane = lax.broadcasted_iota(jnp.int32, (8, LANES), 1)
    sub = lax.broadcasted_iota(jnp.int32, (8, LANES), 0)
    row = sub // 2
    tail = NLON - (TILES - 1) * LANES
    me = lax.axis_index("comp")
    band = lax.axis_index("band")
    bands = lax.axis_size("band")
    z, y = me // SIDE, lax.rem(me, SIDE)
    north = lax.rem(band + 1, bands)
    south = lax.rem(band + bands - 1, bands)

    def peer(o):
        return lax.rem(z + o[0], SIDE) * SIDE + lax.rem(y + o[1], SIDE)

    barrier = pltpu.get_barrier_semaphore()
    for b in (north, south):
        pl.semaphore_signal(barrier, inc=1, device_id={"band": b}, device_id_type=MESH)
    for o in OFFSETS:
        pl.semaphore_signal(barrier, inc=1, device_id={"comp": peer(o)}, device_id_type=MESH)

    for copy in arrivals:
        copy.wait()

    even_half = lax.rem(lax.broadcasted_iota(jnp.int32, (8, DEPTHS), 0), 2) == 0
    gs_ref[:, pl.ds(0, DEPTHS)] = jnp.where(
        even_half,
        jnp.broadcast_to(speed_ref[pl.ds(FREQS * me, 1), :], (8, DEPTHS)),
        jnp.broadcast_to(speed_ref[pl.ds(FREQS * me + 1, 1), :], (8, DEPTHS)),
    )
    stretch = jnp.where(row == 0, scalars_ref[5, ROWS * band], scalars_ref[5, ROWS * band + 1])
    stretch = jnp.where(row == 2, scalars_ref[5, ROWS * band + 2], stretch)
    stretch = jnp.where(row == 3, scalars_ref[5, ROWS * band + 3], stretch)
    flag_ref[...] = jnp.zeros((LANES, LANES), jnp.float32)
    for j in range(TILES):
        width = LANES if j < TILES - 1 else tail
        cols = pl.ds(j * LANES, width)
        sea = (land_ref[:, cols] == 0).astype(jnp.float32)
        flag_ref[pl.ds(ROWS * j, ROWS), pl.ds(0, width)] = sea
        for i in range(2):
            gust = wind_ref[i, :, cols]
            for r in range(ROWS):
                gust_ref[ROWS * j + r, i : i + 1, pl.ds(0, width)] = gust[r : r + 1]
        parts = [sea] + [ref[i, :, cols] for ref in (current_ref, slope_ref) for i in range(2)]
        for n, v in enumerate(parts):
            for f in range(FREQS):
                raw_ref[j, pl.ds(8 * n + f, 4, stride=2), pl.ds(0, width)] = v
        v = depth_ref[:, cols]
        for f in range(FREQS):
            cls_ref[j, pl.ds(f, 4, stride=2), pl.ds(0, width)] = v
    for j in range(TILES):
        def raw(n):
            v = raw_ref[j, pl.ds(8 * n, 8), :]
            return v if j < TILES - 1 else jnp.where(lane < tail, v, 0.0)

        cls = cls_ref[j]
        if j == TILES - 1:
            cls = jnp.where(lane < tail, cls, 0)
        cel = jnp.take_along_axis(gs_ref[...], cls, axis=1)
        sixth = cel * (1.0 / 6.0)
        fl_ref[F_SEA, j] = raw(0)
        fl_ref[F_CX, j] = sixth * stretch
        fl_ref[F_CY, j] = sixth
        fl_ref[F_CUR0, j] = raw(1) * (1.0 / 6.0)
        fl_ref[F_CUR1, j] = raw(2) * (1.0 / 6.0)
        fl_ref[F_T0, j] = (TURNING_SCALE * sixth) * raw(3)
        fl_ref[F_T1, j] = (TURNING_SCALE * sixth) * raw(4)

    def load(d, carry):
        base = pl.multiple_of(8 * d, 8)
        for j in range(TILES):
            width = LANES if j < TILES - 1 else tail
            for f in range(FREQS):
                v = spec_ref[f, d, :, pl.ds(j * LANES, width)].astype(jnp.float32)
                x_ref[j, pl.ds(base + f, 4, stride=2), pl.ds(0, width)] = v
        return carry

    lax.fori_loop(0, ND, load, 0)

    def prepare(q, carry):
        base = pl.multiple_of(32 * q, 32)
        first = [None] * 4
        for j in range(TILES):
            v = [x_ref[j, pl.ds(base + 8 * i, 8), :] for i in range(4)]
            if j == TILES - 1:
                v = [jnp.where(lane < tail, w, 0.0) for w in v]
            v = [w * fl_ref[F_SEA, j] for w in v]
            if j == 0:
                first = v
            if j == TILES - 1:
                v = [
                    jnp.where(
                        lane < tail,
                        w,
                        jnp.where(lane < tail + 2, pltpu.roll(a, tail, 1), pltpu.roll(w, LANES - tail, 1)),
                    )
                    for w, a in zip(v, first)
                ]
            for i in range(4):
                x_ref[j, pl.ds(base + 8 * i, 8), :] = v[i]
            turned = [pltpu.roll(w, 4, 0) for w in v]
            low = [jnp.where(sub < 4, v[i], turned[i + 1]) for i in (0, 2)]
            high = [jnp.where(sub < 4, turned[i], v[i + 1]) for i in (0, 2)]
            rows = pl.ds(pl.multiple_of(16 * q, 16), 16)
            hs_ref[0, j, rows, :] = jnp.concatenate(low, axis=0).astype(jnp.bfloat16)
            hs_ref[1, j, rows, :] = jnp.concatenate(high, axis=0).astype(jnp.bfloat16)
        return carry

    lax.fori_loop(0, ND // 4, prepare, 0)

    pl.semaphore_wait(barrier, len(OFFSETS) + 2)
    halos = []
    for c in range(CHUNKS):
        for side, b in ((0, south), (1, north)):
            copy = pltpu.make_async_remote_copy(
                src_ref=hs_ref.at[side, pl.ds(PER * c, PER)],
                dst_ref=hr_ref.at[side, pl.ds(PER * c, PER)],
                send_sem=halo_send.at[side, c],
                recv_sem=halo_recv.at[side, c],
                device_id={"band": b},
                device_id_type=MESH,
            )
            copy.start()
            halos.append(copy)

    build_tables(counts_ref, flag_ref, tabv_ref, loc_ref)
    table_copy = pltpu.make_async_copy(tabv_ref, tab_ref, tab_sem)
    table_copy.start()

    def along(d, carry):
        base = pl.multiple_of(8 * d, 8)
        cos_d = scalars_ref[0, d]
        x = [x_ref[j, pl.ds(base, 8), :] for j in range(TILES)]
        r1 = [pltpu.roll(v, 1, 1) for v in x]
        r2 = [pltpu.roll(v, 2, 1) for v in x]
        l1 = [pltpu.roll(v, LANES - 1, 1) for v in x]
        l2 = [pltpu.roll(v, LANES - 2, 1) for v in x]
        for j in range(TILES):
            before, after = (j - 1) % TILES, (j + 1) % TILES
            behind = jnp.where(lane < 1, r1[before], r1[j])
            far_behind = jnp.where(lane < 2, r2[before], r2[j])
            ahead = jnp.where(lane >= LANES - 1, l1[after], l1[j])
            far_ahead = jnp.where(lane >= LANES - 2, l2[after], l2[j])
            speed = fl_ref[F_CX, j] * cos_d + fl_ref[F_CUR0, j]
            out = x[j] - upwind12(far_behind, behind, x[j], ahead, far_ahead, speed)
            if j == TILES - 1:
                out = jnp.where(lane < tail, out, 0.0)
            adv_ref[j, pl.ds(base, 8), :] = out
        return carry

    lax.fori_loop(0, ND, along, 0, unroll=2)

    keep_dn = (band < bands - 1).astype(jnp.float32)
    keep_up = (band > 0).astype(jnp.float32)
    zero = jnp.zeros((8, LANES), jnp.float32)

    for c in range(CHUNKS):
        halos[2 * c].wait_recv()
        halos[2 * c + 1].wait_recv()

        def across(q, carry):
            rows = pl.ds(pl.multiple_of(16 * q, 16), 16)
            base = pl.multiple_of(32 * q, 32)
            for j in range(PER * c, PER * c + PER):
                dn = hr_ref[0, j, rows, :].astype(jnp.float32) * keep_dn
                up = hr_ref[1, j, rows, :].astype(jnp.float32) * keep_up
                for i in range(4):
                    a, b = dn[8 * (i // 2) : 8 * (i // 2) + 8], up[8 * (i // 2) : 8 * (i // 2) + 8]
                    if i % 2 == 0:
                        h = jnp.where(sub < 4, a, pltpu.roll(b, 4, 0))
                    else:
                        h = jnp.where(sub < 4, pltpu.roll(a, 4, 0), b)
                    here = pl.ds(base + 8 * i, 8)
                    v = x_ref[j, here, :]
                    ahead = pltpu.roll(jnp.where(row == 0, h, v), 6, 0)
                    far_ahead = pltpu.roll(jnp.where(row < 2, h, v), 4, 0)
                    far_behind = pltpu.roll(jnp.where(row < 2, v, h), 4, 0)
                    behind = pltpu.roll(jnp.where(row == 3, h, v), 2, 0)
                    speed = fl_ref[F_CY, j] * scalars_ref[1, 4 * q + i] + fl_ref[F_CUR1, j]
                    flux = upwind12(far_behind, behind, v, ahead, far_ahead, speed)
                    adv_ref[j, here, :] = (adv_ref[j, here, :] - flux) * fl_ref[F_SEA, j]
            return carry

        lax.fori_loop(0, ND // 4, across, 0, unroll=1)

        def refract(d, sums):
            cos_d = scalars_ref[0, d]
            sin_d = scalars_ref[1, d]

            def at(shift):
                return pl.multiple_of(8 * lax.rem(d + (shift + ND), ND), 8)

            places = [at(s) for s in (-2, -1, 0, 1, 2)]
            sums = list(sums)
            for j in range(PER * c, PER * c + PER):
                values = [adv_ref[j, pl.ds(p, 8), :] for p in places]
                speed = fl_ref[F_T0, j] * sin_d - fl_ref[F_T1, j] * cos_d
                out = (values[2] - upwind12(*values, speed)) * fl_ref[F_SEA, j]
                sums[j - PER * c] = sums[j - PER * c] + out * out
                t_ref[j, pl.ds(d, 8, stride=ND), :] = out
            return tuple(sums)

        sums = lax.fori_loop(0, ND, refract, (zero,) * PER, unroll=3)
        for i in range(PER):
            j = PER * c + i
            sq_ref[...] = sums[i] + pltpu.roll(sums[i], 7, 0)
            part_ref[pl.ds(4 * j, 4), :] = sq_ref[pl.ds(0, 4, stride=2), :]

    def reduce_start(axis, src, dst):
        copies = []
        for i in range(1, SIDE):
            o = (0, i) if axis == 0 else (i, 0)
            copy = pltpu.make_async_remote_copy(
                src_ref=src,
                dst_ref=dst.at[i - 1],
                send_sem=sum_send.at[axis, i - 1],
                recv_sem=sum_recv.at[axis, i - 1],
                device_id={"comp": peer(o)},
                device_id_type=MESH,
            )
            copy.start()
            copies.append(copy)
        return copies

    t_rows = t_ref.reshape(GROUPS, COMPS, LANES)

    def step(k, carry):
        keep = tab_ref[AT_KEEP, k].astype(jnp.float32)
        spot = tab_ref[AT_SPOT, k]
        local = lane + tab_ref[AT_DELTA, k]
        valid = (lane < tab_ref[AT_LEN, k]) & (local >= 0) & (local < tab_ref[AT_COUNT, k])
        local = jnp.clip(local, 0, LANES - 1)
        idx = jnp.take_along_axis(loc_ref[spot], local, axis=1)
        idx_ref[k] = jnp.where(valid, idx, -1)
        parts = []
        for m in range(COMPS // 8):
            data = t_rows[spot, pl.ds(8 * m, 8), :]
            got = jnp.take_along_axis(data, idx, axis=1)
            part = jnp.where(valid, got, carry[m] * keep)
            stage_ref[k, pl.ds(8 * m, 8), :] = part
            parts.append(part)
        gust = jnp.where(valid, jnp.take_along_axis(gust_ref[spot], idx, axis=1), carry[COMPS // 8])
        gusts_ref[k] = gust
        return tuple(parts) + (gust,)

    sums_y = reduce_start(0, part_ref, yr_ref)
    table_copy.wait()
    lax.fori_loop(0, STEPS, step, (zero,) * (COMPS // 8 + 1), unroll=8)
    for copy in sums_y:
        copy.wait()
    for m in range(GROUPS // 8):
        rows = pl.ds(8 * m, 8)
        total_ref[rows, :] = (part_ref[rows, :] + yr_ref[0, rows, :]) + (yr_ref[1, rows, :] + yr_ref[2, rows, :])
    sums_z = reduce_start(1, total_ref, zr_ref)

    def by_row(q):
        low, high = scalars_ref[q, FREQS * me], scalars_ref[q, FREQS * me + 1]
        mixed = jnp.where(sub < 4, low, high)
        return [low if m < 4 else (mixed if m == 4 else high) for m in range(COMPS // 8)]

    rise, calm = by_row(2), by_row(3)
    for i in range(2):
        for m in range(COMPS // 8):
            rows = pl.ds(8 * m, 8)
            compass_ref[i, rows, :] = compass_ref[i, rows, :] * rise[m]

    def grow(c, carry):
        for j in range(3):
            k = tab_ref[AT_LAST, 3 * c + j]
            gust = gusts_ref[k]
            east = jnp.broadcast_to(gust[0:1], (8, LANES))
            north = jnp.broadcast_to(gust[1:2], (8, LANES))
            for m in range(COMPS // 8):
                rows = pl.ds(8 * m, 8)
                push = east * compass_ref[0, rows, :] + north * compass_ref[1, rows, :]
                grown_ref[3 * c + j, rows, :] = stage_ref[k, rows, :] * jnp.exp(jnp.maximum(push - calm[m], 0.0))
        return carry

    lax.fori_loop(0, BLOCKS, grow, 0)
    for copy in sums_z:
        copy.wait()
    for m in range(GROUPS // 8):
        rows = pl.ds(8 * m, 8)
        total = (total_ref[rows, :] + zr_ref[0, rows, :]) + (zr_ref[1, rows, :] + zr_ref[2, rows, :])
        total = jnp.sqrt(total * (1.0 / (BLOCKS * COMPS)) + 1e-6)
        for i in range(8):
            level_ref[8 * m + i] = jnp.broadcast_to(total[i : i + 1], (8, LANES))

    def strengths(k, acc):
        keep = tab_ref[AT_KEEP, k].astype(jnp.float32)
        idx = idx_ref[k]
        got = jnp.take_along_axis(level_ref[tab_ref[AT_SPOT, k]], jnp.maximum(idx, 0), axis=1)
        acc = jnp.where(idx >= 0, got, acc * keep)
        dec_ref[k] = acc
        return acc

    lax.fori_loop(0, STEPS, strengths, zero, unroll=16)

    fade0 = scalars_ref[4, FREQS * me]
    fade1 = scalars_ref[4, FREQS * me + 1]

    def block(c, store):
        places = [tab_ref[AT_LAST, 3 * c + j] for j in range(3)]
        rows = []
        for j in range(3):
            s = dec_ref[places[j]]
            e0 = jnp.exp(-fade0 * s)
            e1 = jnp.exp(-fade1 * s)
            mixed = jnp.where(sub < 4, e0, e1)
            values = []
            for m in range(COMPS // 8):
                e = e0 if m < 4 else (mixed if m == 4 else e1)
                values.append(grown_ref[3 * c + j, pl.ds(8 * m, 8), :] * e)
            if j < 2:
                rows += values
            else:
                for m in range(5):
                    v = values[m]
                    if m < 4:
                        v = jnp.where(lane < 64, v, pltpu.roll(values[5 + m], 64, 1))
                    rows.append(v)
                rows.append(zero)
        for m in range(PACK // 16):
            store(m, jnp.concatenate(rows[2 * m : 2 * m + 2], axis=0).astype(jnp.bfloat16))

    copies = []
    for i, o in enumerate(OFFSETS):
        other = peer(o)

        def put(m, v):
            sb_ref[i, pl.ds(16 * m, 16), :] = v

        block(other, put)
        copy = pltpu.make_async_remote_copy(
            src_ref=sb_ref.at[i],
            dst_ref=rb_ref.at[me],
            send_sem=send_sem.at[i],
            recv_sem=recv_sem.at[i],
            device_id={"comp": other},
            device_id_type=MESH,
        )
        copy.start()
        copies.append(copy)

    def put_own(m, v):
        rb_ref[me, pl.ds(16 * m, 16), :] = v

    block(me, put_own)
    for copy in halos:
        copy.wait_send()
    for copy in copies:
        copy.wait()


def finish_kernel(rb_ref, out_ref, v_ref):
    def spread(i, carry):
        base = pl.multiple_of(COMPS * i, 8)
        v = rb_ref[i].astype(jnp.float32)
        for j in range(2):
            v_ref[j, pl.ds(base, COMPS), :] = v[COMPS * j : COMPS * (j + 1)]
        v_ref[2, pl.ds(base, 40), :] = v[2 * COMPS : 2 * COMPS + 40]
        v_ref[2, pl.ds(base + 40, 32), :] = pltpu.roll(v[2 * COMPS : 2 * COMPS + 32], 64, 1)
        return carry

    lax.fori_loop(0, BLOCKS, spread, 0, unroll=4)
    for m in range(BLOCKS * COMPS // LANES):
        for j in range(3):
            block = v_ref[j, pl.ds(LANES * m, LANES), :].T.astype(jnp.bfloat16)
            rows = min(LANES, SLOTS - LANES * j)
            out_ref[pl.ds(LANES * j, rows), pl.ds(LANES * m, LANES)] = block[:rows]


def build_tables(counts_ref, flag_ref, tabv_ref, loc_ref):
    f32, bf16, i32 = jnp.float32, jnp.bfloat16, jnp.int32
    sub = lax.broadcasted_iota(i32, (LANES, LANES), 0)
    lanes = lax.broadcasted_iota(i32, (LANES, LANES), 1)
    lane = lax.broadcasted_iota(i32, (8, LANES), 1)

    def order(i):
        return jnp.where(i < GROUPS, (i & (ROWS - 1)) * TILES + (i >> 2), i)

    def product(a, b, dims=(((1,), (0,)), ((), ()))):
        return lax.dot_general(a, b, dims, preferred_element_type=f32)

    upper = (sub <= lanes).astype(f32).astype(bf16)
    ones = jnp.ones((LANES, LANES), bf16)
    flags = flag_ref[...].astype(bf16)
    inclusive = product(flags, upper)
    count_rows = product(flags, ones)
    ends = product((order(lanes) <= order(sub)).astype(f32).astype(bf16), count_rows.astype(bf16))[:GROUPS]
    count = product(ones[:16], flags, (((1,), (1,)), ((), ())))
    first = product(count.astype(bf16), (order(sub) < order(lanes)).astype(f32).astype(bf16))
    count, first = count[:8].astype(i32), first[:8].astype(i32)

    wide = lanes[:GROUPS]
    shift = wide - (inclusive[:GROUPS].astype(i32) - 1)
    word = jnp.where(flag_ref[pl.ds(0, GROUPS), :] > 0, wide + LANES * shift + LANES * LANES, 0)
    for k in range(7):
        bit = LANES << k
        moved = pltpu.roll(word, LANES - (1 << k), 1)
        word = jnp.where((moved & bit) != 0, moved, jnp.where((word & bit) != 0, 0, word))
    word = word & (LANES - 1)
    for g in range(GROUPS):
        loc_ref[g] = jnp.broadcast_to(word[g : g + 1], (8, LANES))

    block = (lane * 171) >> 9
    part = lane - 3 * block
    size = jnp.zeros((8, LANES), i32)
    rank = jnp.zeros((8, LANES), i32)
    start = 0
    for c in range(BLOCKS):
        n = counts_ref[0, c]
        size = jnp.where(block == c, n, size)
        rank = jnp.where(block == c, start, rank)
        start = start + n
    rank = rank + LANES * part
    length = jnp.clip(size - LANES * part, 0, LANES)
    real = lane < 3 * BLOCKS

    def groups_before(r):
        hit = (ends <= r[:1].astype(f32)).astype(f32)
        return jnp.minimum(jnp.broadcast_to(jnp.sum(hit, axis=0, keepdims=True), (8, LANES)), GROUPS - 1.0)

    low = groups_before(rank)
    high = groups_before(rank + jnp.maximum(length, 1) - 1)
    width = jnp.where(real, jnp.where(length > 0, high - low + 1.0, 1.0), 0.0)
    stop = product(jnp.concatenate([width, width], axis=0).astype(bf16), upper)[:8]
    begin = stop - width
    column = jnp.sum(jnp.where(wide <= sub[:GROUPS], width[:1], 0.0), axis=1, keepdims=True)
    tile = jnp.sum((column <= wide.astype(f32)).astype(f32), axis=0, keepdims=True)
    tile = jnp.broadcast_to(jnp.minimum(tile, 3 * BLOCKS - 1.0), (8, LANES)).astype(i32)

    def at(values, index):
        return jnp.take_along_axis(values, index, axis=1)

    group = lane + at((low - begin).astype(i32), tile)
    group = jnp.clip(group, 0, GROUPS - 1)
    r = (group * 171) >> 11
    spot = ROWS * (group - TILES * r) + r
    tabv_ref[AT_SPOT : AT_SPOT + 1] = spot[:1]
    tabv_ref[AT_KEEP : AT_KEEP + 1] = (lane > at(begin.astype(i32), tile)).astype(i32)[:1]
    tabv_ref[AT_DELTA : AT_DELTA + 1] = (at(rank, tile) - at(first, spot))[:1]
    tabv_ref[AT_LEN : AT_LEN + 1] = at(length, tile)[:1]
    tabv_ref[AT_COUNT : AT_COUNT + 1] = at(count, spot)[:1]
    tabv_ref[AT_LAST : AT_LAST + 1] = jnp.clip((stop - 1.0).astype(i32), 0, STEPS - 1)[:1]
    tabv_ref[AT_LAST + 1 :] = jnp.zeros((7 - AT_LAST, LANES), i32)


def body(spectra, depth_class, group_speed, current, depth_slope, wind, land_mask, block_counts):
    cos_t, sin_t = angles()
    latitude = (-60.0 + 120.0 * (np.arange(ROWS * lax.axis_size("band")) + 0.5) / (ROWS * lax.axis_size("band"))) * (
        math.pi / 180.0
    )
    stretch = (1.0 / np.cos(latitude)).astype(np.float32)
    angular = 2.0 * math.pi * 0.0418 * np.power(1.1, np.arange(BLOCKS * FREQS, dtype=np.float64))
    ratio = angular / angular[-1]
    phase = 9.81 / angular
    coef = np.stack([GROWTH_RATE * ratio / phase, GROWTH_RATE * ratio, DAMPING * ratio]).astype(np.float32)

    scalars = np.zeros((8, LANES), np.float32)
    scalars[0, :ND], scalars[1, :ND] = cos_t, sin_t
    scalars[2:5, : BLOCKS * FREQS] = coef
    scalars[5, : stretch.size] = stretch
    compass = np.stack([np.tile(cos_t, FREQS), np.tile(sin_t, FREQS)])
    compass = np.ascontiguousarray(np.broadcast_to(compass[:, :, None], (2, COMPS, LANES)))

    vmem = pl.BlockSpec(memory_space=pltpu.VMEM)
    f32, bf16 = jnp.float32, jnp.bfloat16
    dma = pltpu.SemaphoreType.DMA
    rb = pl.pallas_call(
        step_kernel,
        out_shape=jax.ShapeDtypeStruct((BLOCKS, PACK, LANES), bf16),
        in_specs=[pl.BlockSpec(memory_space=pltpu.HBM)] * 10,
        out_specs=vmem,
        scratch_shapes=[
            pltpu.SMEM((8, LANES), f32),
            pltpu.VMEM((2, COMPS, LANES), f32),
            pltpu.SMEM(block_counts.shape, jnp.int32),
            pltpu.VMEM(spectra.shape, bf16),
            pltpu.VMEM(depth_class.shape, jnp.int32),
            pltpu.VMEM(group_speed.shape[::-1], f32),
            pltpu.VMEM(current.shape, f32),
            pltpu.VMEM(depth_slope.shape, f32),
            pltpu.VMEM(wind.shape, f32),
            pltpu.VMEM(land_mask.shape, jnp.int32),
            pltpu.VMEM((GROUPS, 8, LANES), f32),
            pltpu.VMEM((STEPS, 8, LANES), f32),
            pltpu.VMEM((8, LANES), f32),
            pltpu.VMEM((TILES, 8 * 5, LANES), f32),
            pltpu.VMEM((TILES, 8, LANES), jnp.int32),
            pltpu.VMEM((LANES, LANES), f32),
            pltpu.VMEM((8, LANES), jnp.int32),
            pltpu.SMEM((8, LANES), jnp.int32),
            pltpu.VMEM((GROUPS, 8, LANES), jnp.int32),
            pltpu.VMEM((TILES, 8 * ND, LANES), f32),
            pltpu.VMEM((TILES, 8 * ND, LANES), f32),
            pltpu.VMEM((TILES, 8 * ND, LANES), f32),
            pltpu.VMEM((STEPS, COMPS, LANES), f32),
            pltpu.VMEM((3 * BLOCKS, COMPS, LANES), f32),
            pltpu.VMEM((STEPS, 8, LANES), jnp.int32),
            pltpu.VMEM((STEPS, 8, LANES), f32),
            pltpu.VMEM((7, TILES, 8, LANES), f32),
            pltpu.VMEM((2, TILES, 4 * ND, LANES), bf16),
            pltpu.VMEM((2, TILES, 4 * ND, LANES), bf16),
            pltpu.VMEM((8, LANES), f32),
            pltpu.VMEM((GROUPS, LANES), f32),
            pltpu.VMEM((GROUPS, LANES), f32),
            pltpu.VMEM((GROUPS, 8, LANES), f32),
            pltpu.VMEM((SIDE - 1, GROUPS, LANES), f32),
            pltpu.VMEM((SIDE - 1, GROUPS, LANES), f32),
            pltpu.VMEM((BLOCKS - 1, PACK, LANES), bf16),
            dma((10,)),
            dma,
            dma((2, CHUNKS)),
            dma((2, CHUNKS)),
            dma((2, SIDE - 1)),
            dma((2, SIDE - 1)),
            dma((BLOCKS - 1,)),
            dma((BLOCKS - 1,)),
        ],
        compiler_params=pltpu.CompilerParams(
            collective_id=0, has_side_effects=True, vmem_limit_bytes=40 * 1024 * 1024
        ),
        name="wave_step",
    )(
        jnp.asarray(scalars),
        jnp.asarray(compass),
        block_counts,
        spectra,
        depth_class,
        group_speed.T,
        current,
        depth_slope,
        wind,
        land_mask,
    )

    out = pl.pallas_call(
        finish_kernel,
        out_shape=jax.ShapeDtypeStruct((SLOTS, BLOCKS * COMPS), bf16),
        in_specs=[vmem],
        out_specs=vmem,
        scratch_shapes=[pltpu.VMEM((3, BLOCKS * COMPS, LANES), f32)],
        compiler_params=pltpu.CompilerParams(vmem_limit_bytes=16 * 1024 * 1024),
        name="finish",
    )(rb)
    return out.T


def solution(mesh):
    return jax.shard_map(
        body,
        mesh=mesh,
        in_specs=(
            P("comp", None, "band", None),
            P("band", None),
            P(),
            P(None, "band", None),
            P(None, "band", None),
            P(None, "band", None),
            P("band", None),
            P("band", None),
        ),
        out_specs=P(None, ("comp", "band")),
        check_vma=False,
    )
```

```python
import math

import jax
import jax.numpy as jnp
import numpy as np
from jax import lax
from jax.experimental import pallas as pl
from jax.experimental.pallas import tpu as pltpu
from jax.sharding import PartitionSpec as P

GROWTH_RATE = 0.05
DAMPING = 1.5
TURNING_SCALE = 0.5

FREQS = 2
LANES = 128
ND = 36
ROWS = 4
NLON = 1440
TILES = 12
GROUPS = ROWS * TILES
BLOCKS = 16
SLOTS = 315
DEPTHS = 64
STEPS = 96
COMPS = FREQS * ND
PACK = 192
CHUNKS = 4
PER = TILES // CHUNKS
SIDE = 4

AT_SPOT, AT_KEEP, AT_DELTA, AT_LEN, AT_COUNT, AT_LAST = range(6)

(F_SEA, F_CX, F_CY, F_CUR0, F_CUR1, F_T0, F_T1) = range(7)

MESH = pl.DeviceIdType.MESH


def angles():
    heading = (np.arange(ND, dtype=np.float32) * np.float32(2.0 * math.pi / ND)).astype(np.float64)
    return (np.cos(heading).astype(np.float32), np.sin(heading).astype(np.float32))


def upwind12(far_behind, behind, centre, ahead, far_ahead, speed):
    forward = speed > 0
    down = jnp.where(forward, ahead, behind)
    up = jnp.where(forward, behind, ahead)
    far = jnp.where(forward, far_behind, far_ahead)
    return jnp.abs(speed) * ((2.0 * down + far) + (3.0 * centre - 6.0 * up))


OFFSETS = sorted(
    [(a, b) for a in range(SIDE) for b in range(SIDE) if a or b],
    key=lambda o: -(min(o[0], SIDE - o[0]) + min(o[1], SIDE - o[1])),
)


def step_kernel(
    scalars_hbm, compass_hbm, counts_hbm, spec_hbm, depth_hbm, speed_hbm, current_hbm, slope_hbm, wind_hbm, land_hbm,
    rb_ref,
    scalars_ref, compass_ref, counts_ref, spec_ref, depth_ref, speed_ref, current_ref, slope_ref, wind_ref, land_ref,
    gust_ref, gusts_ref,
    gs_ref, raw_ref, cls_ref, flag_ref, tabv_ref, tab_ref, loc_ref, x_ref, adv_ref, t_ref, stage_ref, grown_ref, idx_ref, dec_ref, fl_ref, hs_ref, hr_ref, sq_ref, part_ref, total_ref, level_ref, yr_ref, zr_ref, sb_ref,
    in_sem, tab_sem, halo_send, halo_recv, sum_send, sum_recv, send_sem, recv_sem,
):
    arrivals = [
        pltpu.make_async_copy(src, dst, in_sem.at[i])
        for i, (src, dst) in enumerate(
            [
                (land_hbm, land_ref),
                (spec_hbm, spec_ref),
                (scalars_hbm, scalars_ref),
                (speed_hbm, speed_ref),
                (depth_hbm, depth_ref),
                (current_hbm, current_ref),
                (slope_hbm, slope_ref),
                (wind_hbm, wind_ref),
                (counts_hbm, counts_ref),
                (compass_hbm, compass_ref),
            ]
        )
    ]
    for copy in arrivals:
        copy.start()
    lane = lax.broadcasted_iota(jnp.int32, (8, LANES), 1)
    sub = lax.broadcasted_iota(jnp.int32, (8, LANES), 0)
    row = sub // 2
    tail = NLON - (TILES - 1) * LANES
    me = lax.axis_index("comp")
    band = lax.axis_index("band")
    bands = lax.axis_size("band")
    z, y = me // SIDE, lax.rem(me, SIDE)
    north = lax.rem(band + 1, bands)
    south = lax.rem(band + bands - 1, bands)

    def peer(o):
        return lax.rem(z + o[0], SIDE) * SIDE + lax.rem(y + o[1], SIDE)

    barrier = pltpu.get_barrier_semaphore()
    for b in (north, south):
        pl.semaphore_signal(barrier, inc=1, device_id={"band": b}, device_id_type=MESH)
    for o in OFFSETS:
        pl.semaphore_signal(barrier, inc=1, device_id={"comp": peer(o)}, device_id_type=MESH)

    for copy in arrivals:
        copy.wait()

    even_half = lax.rem(lax.broadcasted_iota(jnp.int32, (8, DEPTHS), 0), 2) == 0
    gs_ref[:, pl.ds(0, DEPTHS)] = jnp.where(
        even_half,
        jnp.broadcast_to(speed_ref[pl.ds(FREQS * me, 1), :], (8, DEPTHS)),
        jnp.broadcast_to(speed_ref[pl.ds(FREQS * me + 1, 1), :], (8, DEPTHS)),
    )
    stretch = jnp.where(row == 0, scalars_ref[5, ROWS * band], scalars_ref[5, ROWS * band + 1])
    stretch = jnp.where(row == 2, scalars_ref[5, ROWS * band + 2], stretch)
    stretch = jnp.where(row == 3, scalars_ref[5, ROWS * band + 3], stretch)
    flag_ref[...] = jnp.zeros((LANES, LANES), jnp.float32)
    for j in range(TILES):
        width = LANES if j < TILES - 1 else tail
        cols = pl.ds(j * LANES, width)
        sea = (land_ref[:, cols] == 0).astype(jnp.float32)
        flag_ref[pl.ds(ROWS * j, ROWS), pl.ds(0, width)] = sea
        for i in range(2):
            gust = wind_ref[i, :, cols]
            for r in range(ROWS):
                gust_ref[ROWS * j + r, i : i + 1, pl.ds(0, width)] = gust[r : r + 1]
        parts = [sea] + [ref[i, :, cols] for ref in (current_ref, slope_ref) for i in range(2)]
        for n, v in enumerate(parts):
            for f in range(FREQS):
                raw_ref[j, pl.ds(8 * n + f, 4, stride=2), pl.ds(0, width)] = v
        v = depth_ref[:, cols]
        for f in range(FREQS):
            cls_ref[j, pl.ds(f, 4, stride=2), pl.ds(0, width)] = v
    for j in range(TILES):
        def raw(n):
            v = raw_ref[j, pl.ds(8 * n, 8), :]
            return v if j < TILES - 1 else jnp.where(lane < tail, v, 0.0)

        cls = cls_ref[j]
        if j == TILES - 1:
            cls = jnp.where(lane < tail, cls, 0)
        cel = jnp.take_along_axis(gs_ref[...], cls, axis=1)
        sixth = cel * (1.0 / 6.0)
        fl_ref[F_SEA, j] = raw(0)
        fl_ref[F_CX, j] = sixth * stretch
        fl_ref[F_CY, j] = sixth
        fl_ref[F_CUR0, j] = raw(1) * (1.0 / 6.0)
        fl_ref[F_CUR1, j] = raw(2) * (1.0 / 6.0)
        fl_ref[F_T0, j] = (TURNING_SCALE * sixth) * raw(3)
        fl_ref[F_T1, j] = (TURNING_SCALE * sixth) * raw(4)

    def load(d, carry):
        base = pl.multiple_of(8 * d, 8)
        for j in range(TILES):
            width = LANES if j < TILES - 1 else tail
            for f in range(FREQS):
                v = spec_ref[f, d, :, pl.ds(j * LANES, width)].astype(jnp.float32)
                x_ref[j, pl.ds(base + f, 4, stride=2), pl.ds(0, width)] = v
        return carry

    lax.fori_loop(0, ND, load, 0)

    def prepare(q, carry):
        base = pl.multiple_of(32 * q, 32)
        first = [None] * 4
        for j in range(TILES):
            v = [x_ref[j, pl.ds(base + 8 * i, 8), :] for i in range(4)]
            if j == TILES - 1:
                v = [jnp.where(lane < tail, w, 0.0) for w in v]
            v = [w * fl_ref[F_SEA, j] for w in v]
            if j == 0:
                first = v
            if j == TILES - 1:
                v = [
                    jnp.where(
                        lane < tail,
                        w,
                        jnp.where(lane < tail + 2, pltpu.roll(a, tail, 1), pltpu.roll(w, LANES - tail, 1)),
                    )
                    for w, a in zip(v, first)
                ]
            for i in range(4):
                x_ref[j, pl.ds(base + 8 * i, 8), :] = v[i]
            turned = [pltpu.roll(w, 4, 0) for w in v]
            low = [jnp.where(sub < 4, v[i], turned[i + 1]) for i in (0, 2)]
            high = [jnp.where(sub < 4, turned[i], v[i + 1]) for i in (0, 2)]
            rows = pl.ds(pl.multiple_of(16 * q, 16), 16)
            hs_ref[0, j, rows, :] = jnp.concatenate(low, axis=0).astype(jnp.bfloat16)
            hs_ref[1, j, rows, :] = jnp.concatenate(high, axis=0).astype(jnp.bfloat16)
        return carry

    lax.fori_loop(0, ND // 4, prepare, 0, unroll=3)

    pl.semaphore_wait(barrier, len(OFFSETS) + 2)
    halos = []
    for c in range(CHUNKS):
        for side, b in ((0, south), (1, north)):
            copy = pltpu.make_async_remote_copy(
                src_ref=hs_ref.at[side, pl.ds(PER * c, PER)],
                dst_ref=hr_ref.at[side, pl.ds(PER * c, PER)],
                send_sem=halo_send.at[side, c],
                recv_sem=halo_recv.at[side, c],
                device_id={"band": b},
                device_id_type=MESH,
            )
            copy.start()
            halos.append(copy)

    build_tables(counts_ref, flag_ref, tabv_ref, loc_ref)
    table_copy = pltpu.make_async_copy(tabv_ref, tab_ref, tab_sem)
    table_copy.start()

    def along(d, carry):
        base = pl.multiple_of(8 * d, 8)
        cos_d = scalars_ref[0, d]
        x = [x_ref[j, pl.ds(base, 8), :] for j in range(TILES)]
        r1 = [pltpu.roll(v, 1, 1) for v in x]
        r2 = [pltpu.roll(v, 2, 1) for v in x]
        l1 = [pltpu.roll(v, LANES - 1, 1) for v in x]
        l2 = [pltpu.roll(v, LANES - 2, 1) for v in x]
        for j in range(TILES):
            before, after = (j - 1) % TILES, (j + 1) % TILES
            behind = jnp.where(lane < 1, r1[before], r1[j])
            far_behind = jnp.where(lane < 2, r2[before], r2[j])
            ahead = jnp.where(lane >= LANES - 1, l1[after], l1[j])
            far_ahead = jnp.where(lane >= LANES - 2, l2[after], l2[j])
            speed = fl_ref[F_CX, j] * cos_d + fl_ref[F_CUR0, j]
            out = x[j] - upwind12(far_behind, behind, x[j], ahead, far_ahead, speed)
            if j == TILES - 1:
                out = jnp.where(lane < tail, out, 0.0)
            adv_ref[j, pl.ds(base, 8), :] = out
        return carry

    lax.fori_loop(0, ND, along, 0, unroll=4)

    keep_dn = (band < bands - 1).astype(jnp.float32)
    keep_up = (band > 0).astype(jnp.float32)
    zero = jnp.zeros((8, LANES), jnp.float32)

    for c in range(CHUNKS):
        halos[2 * c].wait_recv()
        halos[2 * c + 1].wait_recv()

        def across(q, carry):
            rows = pl.ds(pl.multiple_of(16 * q, 16), 16)
            base = pl.multiple_of(32 * q, 32)
            for j in range(PER * c, PER * c + PER):
                dn = hr_ref[0, j, rows, :].astype(jnp.float32) * keep_dn
                up = hr_ref[1, j, rows, :].astype(jnp.float32) * keep_up
                for i in range(4):
                    a, b = dn[8 * (i // 2) : 8 * (i // 2) + 8], up[8 * (i // 2) : 8 * (i // 2) + 8]
                    if i % 2 == 0:
                        h = jnp.where(sub < 4, a, pltpu.roll(b, 4, 0))
                    else:
                        h = jnp.where(sub < 4, pltpu.roll(a, 4, 0), b)
                    here = pl.ds(base + 8 * i, 8)
                    v = x_ref[j, here, :]
                    ahead = pltpu.roll(jnp.where(row == 0, h, v), 6, 0)
                    far_ahead = pltpu.roll(jnp.where(row < 2, h, v), 4, 0)
                    far_behind = pltpu.roll(jnp.where(row < 2, v, h), 4, 0)
                    behind = pltpu.roll(jnp.where(row == 3, h, v), 2, 0)
                    speed = fl_ref[F_CY, j] * scalars_ref[1, 4 * q + i] + fl_ref[F_CUR1, j]
                    flux = upwind12(far_behind, behind, v, ahead, far_ahead, speed)
                    adv_ref[j, here, :] = (adv_ref[j, here, :] - flux) * fl_ref[F_SEA, j]
            return carry

        lax.fori_loop(0, ND // 4, across, 0, unroll=3)

        def refract(d, sums):
            cos_d = scalars_ref[0, d]
            sin_d = scalars_ref[1, d]

            def at(shift):
                return pl.multiple_of(8 * lax.rem(d + (shift + ND), ND), 8)

            places = [at(s) for s in (-2, -1, 0, 1, 2)]
            sums = list(sums)
            for j in range(PER * c, PER * c + PER):
                values = [adv_ref[j, pl.ds(p, 8), :] for p in places]
                speed = fl_ref[F_T0, j] * sin_d - fl_ref[F_T1, j] * cos_d
                out = (values[2] - upwind12(*values, speed)) * fl_ref[F_SEA, j]
                sums[j - PER * c] = sums[j - PER * c] + out * out
                t_ref[j, pl.ds(d, 8, stride=ND), :] = out
            return tuple(sums)

        sums = lax.fori_loop(0, ND, refract, (zero,) * PER, unroll=6)
        for i in range(PER):
            j = PER * c + i
            sq_ref[...] = sums[i] + pltpu.roll(sums[i], 7, 0)
            part_ref[pl.ds(4 * j, 4), :] = sq_ref[pl.ds(0, 4, stride=2), :]

    def reduce_start(axis, src, dst):
        copies = []
        for i in range(1, SIDE):
            o = (0, i) if axis == 0 else (i, 0)
            copy = pltpu.make_async_remote_copy(
                src_ref=src,
                dst_ref=dst.at[i - 1],
                send_sem=sum_send.at[axis, i - 1],
                recv_sem=sum_recv.at[axis, i - 1],
                device_id={"comp": peer(o)},
                device_id_type=MESH,
            )
            copy.start()
            copies.append(copy)
        return copies

    t_rows = t_ref.reshape(GROUPS, COMPS, LANES)

    def step(k, carry):
        keep = tab_ref[AT_KEEP, k].astype(jnp.float32)
        spot = tab_ref[AT_SPOT, k]
        local = lane + tab_ref[AT_DELTA, k]
        valid = (lane < tab_ref[AT_LEN, k]) & (local >= 0) & (local < tab_ref[AT_COUNT, k])
        local = jnp.clip(local, 0, LANES - 1)
        idx = jnp.take_along_axis(loc_ref[spot], local, axis=1)
        idx_ref[k] = jnp.where(valid, idx, -1)
        parts = []
        for m in range(COMPS // 8):
            data = t_rows[spot, pl.ds(8 * m, 8), :]
            got = jnp.take_along_axis(data, idx, axis=1)
            part = jnp.where(valid, got, carry[m] * keep)
            stage_ref[k, pl.ds(8 * m, 8), :] = part
            parts.append(part)
        gust = jnp.where(valid, jnp.take_along_axis(gust_ref[spot], idx, axis=1), carry[COMPS // 8])
        gusts_ref[k] = gust
        return tuple(parts) + (gust,)

    sums_y = reduce_start(0, part_ref, yr_ref)
    table_copy.wait()
    lax.fori_loop(0, STEPS, step, (zero,) * (COMPS // 8 + 1), unroll=8)
    for copy in sums_y:
        copy.wait()
    for m in range(GROUPS // 8):
        rows = pl.ds(8 * m, 8)
        total_ref[rows, :] = (part_ref[rows, :] + yr_ref[0, rows, :]) + (yr_ref[1, rows, :] + yr_ref[2, rows, :])
    sums_z = reduce_start(1, total_ref, zr_ref)

    def by_row(q):
        low, high = scalars_ref[q, FREQS * me], scalars_ref[q, FREQS * me + 1]
        mixed = jnp.where(sub < 4, low, high)
        return [low if m < 4 else (mixed if m == 4 else high) for m in range(COMPS // 8)]

    rise, calm = by_row(2), by_row(3)
    for i in range(2):
        for m in range(COMPS // 8):
            rows = pl.ds(8 * m, 8)
            compass_ref[i, rows, :] = compass_ref[i, rows, :] * rise[m]

    def grow(c, carry):
        for j in range(3):
            k = tab_ref[AT_LAST, 3 * c + j]
            gust = gusts_ref[k]
            east = jnp.broadcast_to(gust[0:1], (8, LANES))
            north = jnp.broadcast_to(gust[1:2], (8, LANES))
            for m in range(COMPS // 8):
                rows = pl.ds(8 * m, 8)
                push = east * compass_ref[0, rows, :] + north * compass_ref[1, rows, :]
                grown_ref[3 * c + j, rows, :] = stage_ref[k, rows, :] * jnp.exp(jnp.maximum(push - calm[m], 0.0))
        return carry

    lax.fori_loop(0, BLOCKS, grow, 0, unroll=2)
    for copy in sums_z:
        copy.wait()
    for m in range(GROUPS // 8):
        rows = pl.ds(8 * m, 8)
        total = (total_ref[rows, :] + zr_ref[0, rows, :]) + (zr_ref[1, rows, :] + zr_ref[2, rows, :])
        total = jnp.sqrt(total * (1.0 / (BLOCKS * COMPS)) + 1e-6)
        for i in range(8):
            level_ref[8 * m + i] = jnp.broadcast_to(total[i : i + 1], (8, LANES))

    def strengths(k, acc):
        keep = tab_ref[AT_KEEP, k].astype(jnp.float32)
        idx = idx_ref[k]
        got = jnp.take_along_axis(level_ref[tab_ref[AT_SPOT, k]], jnp.maximum(idx, 0), axis=1)
        acc = jnp.where(idx >= 0, got, acc * keep)
        dec_ref[k] = acc
        return acc

    lax.fori_loop(0, STEPS, strengths, zero, unroll=32)

    fade0 = scalars_ref[4, FREQS * me]
    fade1 = scalars_ref[4, FREQS * me + 1]

    def block(c, store):
        places = [tab_ref[AT_LAST, 3 * c + j] for j in range(3)]
        rows = []
        for j in range(3):
            s = dec_ref[places[j]]
            e0 = jnp.exp(-fade0 * s)
            e1 = jnp.exp(-fade1 * s)
            mixed = jnp.where(sub < 4, e0, e1)
            values = []
            for m in range(COMPS // 8):
                e = e0 if m < 4 else (mixed if m == 4 else e1)
                values.append(grown_ref[3 * c + j, pl.ds(8 * m, 8), :] * e)
            if j < 2:
                rows += values
            else:
                for m in range(5):
                    v = values[m]
                    if m < 4:
                        v = jnp.where(lane < 64, v, pltpu.roll(values[5 + m], 64, 1))
                    rows.append(v)
                rows.append(zero)
        for m in range(PACK // 16):
            store(m, jnp.concatenate(rows[2 * m : 2 * m + 2], axis=0).astype(jnp.bfloat16))

    copies = []
    for i, o in enumerate(OFFSETS):
        other = peer(o)

        def put(m, v):
            sb_ref[i, pl.ds(16 * m, 16), :] = v

        block(other, put)
        copy = pltpu.make_async_remote_copy(
            src_ref=sb_ref.at[i],
            dst_ref=rb_ref.at[me],
            send_sem=send_sem.at[i],
            recv_sem=recv_sem.at[i],
            device_id={"comp": other},
            device_id_type=MESH,
        )
        copy.start()
        copies.append(copy)

    def put_own(m, v):
        rb_ref[me, pl.ds(16 * m, 16), :] = v

    block(me, put_own)
    for copy in halos:
        copy.wait_send()
    for copy in copies:
        copy.wait()


def finish_kernel(rb_ref, out_ref, v_ref):
    def spread(i, carry):
        base = pl.multiple_of(COMPS * i, 8)
        v = rb_ref[i].astype(jnp.float32)
        for j in range(2):
            v_ref[j, pl.ds(base, COMPS), :] = v[COMPS * j : COMPS * (j + 1)]
        v_ref[2, pl.ds(base, 40), :] = v[2 * COMPS : 2 * COMPS + 40]
        v_ref[2, pl.ds(base + 40, 32), :] = pltpu.roll(v[2 * COMPS : 2 * COMPS + 32], 64, 1)
        return carry

    lax.fori_loop(0, BLOCKS, spread, 0, unroll=4)
    for m in range(BLOCKS * COMPS // LANES):
        for j in range(3):
            block = v_ref[j, pl.ds(LANES * m, LANES), :].T.astype(jnp.bfloat16)
            rows = min(LANES, SLOTS - LANES * j)
            out_ref[pl.ds(LANES * j, rows), pl.ds(LANES * m, LANES)] = block[:rows]


def build_tables(counts_ref, flag_ref, tabv_ref, loc_ref):
    f32, bf16, i32 = jnp.float32, jnp.bfloat16, jnp.int32
    sub = lax.broadcasted_iota(i32, (LANES, LANES), 0)
    lanes = lax.broadcasted_iota(i32, (LANES, LANES), 1)
    lane = lax.broadcasted_iota(i32, (8, LANES), 1)

    def order(i):
        return jnp.where(i < GROUPS, (i & (ROWS - 1)) * TILES + (i >> 2), i)

    def product(a, b, dims=(((1,), (0,)), ((), ()))):
        return lax.dot_general(a, b, dims, preferred_element_type=f32)

    upper = (sub <= lanes).astype(f32).astype(bf16)
    ones = jnp.ones((LANES, LANES), bf16)
    flags = flag_ref[...].astype(bf16)
    inclusive = product(flags, upper)
    count_rows = product(flags, ones)
    ends = product((order(lanes) <= order(sub)).astype(f32).astype(bf16), count_rows.astype(bf16))[:GROUPS]
    count = product(ones[:16], flags, (((1,), (1,)), ((), ())))
    first = product(count.astype(bf16), (order(sub) < order(lanes)).astype(f32).astype(bf16))
    count, first = count[:8].astype(i32), first[:8].astype(i32)

    wide = lanes[:GROUPS]
    shift = wide - (inclusive[:GROUPS].astype(i32) - 1)
    word = jnp.where(flag_ref[pl.ds(0, GROUPS), :] > 0, wide + LANES * shift + LANES * LANES, 0)
    for k in range(7):
        bit = LANES << k
        moved = pltpu.roll(word, LANES - (1 << k), 1)
        word = jnp.where((moved & bit) != 0, moved, jnp.where((word & bit) != 0, 0, word))
    word = word & (LANES - 1)
    for g in range(GROUPS):
        loc_ref[g] = jnp.broadcast_to(word[g : g + 1], (8, LANES))

    block = (lane * 171) >> 9
    part = lane - 3 * block
    size = jnp.zeros((8, LANES), i32)
    rank = jnp.zeros((8, LANES), i32)
    start = 0
    for c in range(BLOCKS):
        n = counts_ref[0, c]
        size = jnp.where(block == c, n, size)
        rank = jnp.where(block == c, start, rank)
        start = start + n
    rank = rank + LANES * part
    length = jnp.clip(size - LANES * part, 0, LANES)
    real = lane < 3 * BLOCKS

    def groups_before(r):
        hit = (ends <= r[:1].astype(f32)).astype(f32)
        return jnp.minimum(jnp.broadcast_to(jnp.sum(hit, axis=0, keepdims=True), (8, LANES)), GROUPS - 1.0)

    low = groups_before(rank)
    high = groups_before(rank + jnp.maximum(length, 1) - 1)
    width = jnp.where(real, jnp.where(length > 0, high - low + 1.0, 1.0), 0.0)
    stop = product(jnp.concatenate([width, width], axis=0).astype(bf16), upper)[:8]
    begin = stop - width
    column = jnp.sum(jnp.where(wide <= sub[:GROUPS], width[:1], 0.0), axis=1, keepdims=True)
    tile = jnp.sum((column <= wide.astype(f32)).astype(f32), axis=0, keepdims=True)
    tile = jnp.broadcast_to(jnp.minimum(tile, 3 * BLOCKS - 1.0), (8, LANES)).astype(i32)

    def at(values, index):
        return jnp.take_along_axis(values, index, axis=1)

    group = lane + at((low - begin).astype(i32), tile)
    group = jnp.clip(group, 0, GROUPS - 1)
    r = (group * 171) >> 11
    spot = ROWS * (group - TILES * r) + r
    tabv_ref[AT_SPOT : AT_SPOT + 1] = spot[:1]
    tabv_ref[AT_KEEP : AT_KEEP + 1] = (lane > at(begin.astype(i32), tile)).astype(i32)[:1]
    tabv_ref[AT_DELTA : AT_DELTA + 1] = (at(rank, tile) - at(first, spot))[:1]
    tabv_ref[AT_LEN : AT_LEN + 1] = at(length, tile)[:1]
    tabv_ref[AT_COUNT : AT_COUNT + 1] = at(count, spot)[:1]
    tabv_ref[AT_LAST : AT_LAST + 1] = jnp.clip((stop - 1.0).astype(i32), 0, STEPS - 1)[:1]
    tabv_ref[AT_LAST + 1 :] = jnp.zeros((7 - AT_LAST, LANES), i32)


def body(spectra, depth_class, group_speed, current, depth_slope, wind, land_mask, block_counts):
    cos_t, sin_t = angles()
    latitude = (-60.0 + 120.0 * (np.arange(ROWS * lax.axis_size("band")) + 0.5) / (ROWS * lax.axis_size("band"))) * (
        math.pi / 180.0
    )
    stretch = (1.0 / np.cos(latitude)).astype(np.float32)
    angular = 2.0 * math.pi * 0.0418 * np.power(1.1, np.arange(BLOCKS * FREQS, dtype=np.float64))
    ratio = angular / angular[-1]
    phase = 9.81 / angular
    coef = np.stack([GROWTH_RATE * ratio / phase, GROWTH_RATE * ratio, DAMPING * ratio]).astype(np.float32)

    scalars = np.zeros((8, LANES), np.float32)
    scalars[0, :ND], scalars[1, :ND] = cos_t, sin_t
    scalars[2:5, : BLOCKS * FREQS] = coef
    scalars[5, : stretch.size] = stretch
    compass = np.stack([np.tile(cos_t, FREQS), np.tile(sin_t, FREQS)])
    compass = np.ascontiguousarray(np.broadcast_to(compass[:, :, None], (2, COMPS, LANES)))

    vmem = pl.BlockSpec(memory_space=pltpu.VMEM)
    f32, bf16 = jnp.float32, jnp.bfloat16
    dma = pltpu.SemaphoreType.DMA
    rb = pl.pallas_call(
        step_kernel,
        out_shape=jax.ShapeDtypeStruct((BLOCKS, PACK, LANES), bf16),
        in_specs=[pl.BlockSpec(memory_space=pltpu.HBM)] * 10,
        out_specs=vmem,
        scratch_shapes=[
            pltpu.SMEM((8, LANES), f32),
            pltpu.VMEM((2, COMPS, LANES), f32),
            pltpu.SMEM(block_counts.shape, jnp.int32),
            pltpu.VMEM(spectra.shape, bf16),
            pltpu.VMEM(depth_class.shape, jnp.int32),
            pltpu.VMEM(group_speed.shape[::-1], f32),
            pltpu.VMEM(current.shape, f32),
            pltpu.VMEM(depth_slope.shape, f32),
            pltpu.VMEM(wind.shape, f32),
            pltpu.VMEM(land_mask.shape, jnp.int32),
            pltpu.VMEM((GROUPS, 8, LANES), f32),
            pltpu.VMEM((STEPS, 8, LANES), f32),
            pltpu.VMEM((8, LANES), f32),
            pltpu.VMEM((TILES, 8 * 5, LANES), f32),
            pltpu.VMEM((TILES, 8, LANES), jnp.int32),
            pltpu.VMEM((LANES, LANES), f32),
            pltpu.VMEM((8, LANES), jnp.int32),
            pltpu.SMEM((8, LANES), jnp.int32),
            pltpu.VMEM((GROUPS, 8, LANES), jnp.int32),
            pltpu.VMEM((TILES, 8 * ND, LANES), f32),
            pltpu.VMEM((TILES, 8 * ND, LANES), f32),
            pltpu.VMEM((TILES, 8 * ND, LANES), f32),
            pltpu.VMEM((STEPS, COMPS, LANES), f32),
            pltpu.VMEM((3 * BLOCKS, COMPS, LANES), f32),
            pltpu.VMEM((STEPS, 8, LANES), jnp.int32),
            pltpu.VMEM((STEPS, 8, LANES), f32),
            pltpu.VMEM((7, TILES, 8, LANES), f32),
            pltpu.VMEM((2, TILES, 4 * ND, LANES), bf16),
            pltpu.VMEM((2, TILES, 4 * ND, LANES), bf16),
            pltpu.VMEM((8, LANES), f32),
            pltpu.VMEM((GROUPS, LANES), f32),
            pltpu.VMEM((GROUPS, LANES), f32),
            pltpu.VMEM((GROUPS, 8, LANES), f32),
            pltpu.VMEM((SIDE - 1, GROUPS, LANES), f32),
            pltpu.VMEM((SIDE - 1, GROUPS, LANES), f32),
            pltpu.VMEM((BLOCKS - 1, PACK, LANES), bf16),
            dma((10,)),
            dma,
            dma((2, CHUNKS)),
            dma((2, CHUNKS)),
            dma((2, SIDE - 1)),
            dma((2, SIDE - 1)),
            dma((BLOCKS - 1,)),
            dma((BLOCKS - 1,)),
        ],
        compiler_params=pltpu.CompilerParams(
            collective_id=0, has_side_effects=True, vmem_limit_bytes=58 * 1024 * 1024
        ),
        name="wave_step",
    )(
        jnp.asarray(scalars),
        jnp.asarray(compass),
        block_counts,
        spectra,
        depth_class,
        group_speed.T,
        current,
        depth_slope,
        wind,
        land_mask,
    )

    out = pl.pallas_call(
        finish_kernel,
        out_shape=jax.ShapeDtypeStruct((SLOTS, BLOCKS * COMPS), bf16),
        in_specs=[vmem],
        out_specs=vmem,
        scratch_shapes=[pltpu.VMEM((3, BLOCKS * COMPS, LANES), f32)],
        compiler_params=pltpu.CompilerParams(vmem_limit_bytes=16 * 1024 * 1024),
        name="finish",
    )(rb)
    return out.T


def solution(mesh):
    return jax.shard_map(
        body,
        mesh=mesh,
        in_specs=(
            P("comp", None, "band", None),
            P("band", None),
            P(),
            P(None, "band", None),
            P(None, "band", None),
            P(None, "band", None),
            P("band", None),
            P("band", None),
        ),
        out_specs=P(None, ("comp", "band")),
        check_vma=False,
    )
```

```python
import math

import jax
import jax.numpy as jnp
import numpy as np
from jax import lax
from jax.experimental import pallas as pl
from jax.experimental.pallas import tpu as pltpu
from jax.sharding import PartitionSpec as P

GROWTH_RATE = 0.05
DAMPING = 1.5
TURNING_SCALE = 0.5

FREQS = 2
LANES = 128
ND = 36
ROWS = 4
NLON = 1440
TILES = 12
GROUPS = ROWS * TILES
BLOCKS = 16
SLOTS = 315
DEPTHS = 64
STEPS = 96
COMPS = FREQS * ND
PACK = 192
CHUNKS = 4
PER = TILES // CHUNKS
RUN = 6
SIDE = 4

AT_SPOT, AT_KEEP, AT_DELTA, AT_LEN, AT_COUNT, AT_LAST = range(6)

(F_SEA, F_CX, F_CY, F_CUR0, F_CUR1, F_T0, F_T1) = range(7)

MESH = pl.DeviceIdType.MESH


def angles():
    heading = (np.arange(ND, dtype=np.float32) * np.float32(2.0 * math.pi / ND)).astype(np.float64)
    return (np.cos(heading).astype(np.float32), np.sin(heading).astype(np.float32))


def upwind12(far_behind, behind, centre, ahead, far_ahead, speed):
    forward = speed > 0
    down = jnp.where(forward, ahead, behind)
    up = jnp.where(forward, behind, ahead)
    far = jnp.where(forward, far_behind, far_ahead)
    return jnp.abs(speed) * ((2.0 * down + far) + (3.0 * centre - 6.0 * up))


OFFSETS = sorted(
    [(a, b) for a in range(SIDE) for b in range(SIDE) if a or b],
    key=lambda o: -(min(o[0], SIDE - o[0]) + min(o[1], SIDE - o[1])),
)


def step_kernel(
    scalars_hbm, compass_hbm, counts_hbm, spec_hbm, depth_hbm, speed_hbm, current_hbm, slope_hbm, wind_hbm, land_hbm,
    rb_ref,
    scalars_ref, compass_ref, counts_ref, spec_ref, depth_ref, speed_ref, current_ref, slope_ref, wind_ref, land_ref,
    gust_ref, gusts_ref,
    gs_ref, raw_ref, cls_ref, flag_ref, tabv_ref, tab_ref, loc_ref, x_ref, adv_ref, t_ref, stage_ref, grown_ref, idx_ref, dec_ref, fl_ref, hs_ref, hr_ref, sq_ref, part_ref, total_ref, level_ref, yr_ref, zr_ref, sb_ref, own_ref,
    in_sem, tab_sem, own_sem, halo_send, halo_recv, sum_send, sum_recv, send_sem, recv_sem,
):
    arrivals = [
        pltpu.make_async_copy(src, dst, in_sem.at[i])
        for i, (src, dst) in enumerate(
            [
                (land_hbm, land_ref),
                (spec_hbm, spec_ref),
                (scalars_hbm, scalars_ref),
                (speed_hbm, speed_ref),
                (depth_hbm, depth_ref),
                (current_hbm, current_ref),
                (slope_hbm, slope_ref),
                (wind_hbm, wind_ref),
                (counts_hbm, counts_ref),
                (compass_hbm, compass_ref),
            ]
        )
    ]
    for copy in arrivals:
        copy.start()
    lane = lax.broadcasted_iota(jnp.int32, (8, LANES), 1)
    sub = lax.broadcasted_iota(jnp.int32, (8, LANES), 0)
    row = sub // 2
    tail = NLON - (TILES - 1) * LANES
    me = lax.axis_index("comp")
    band = lax.axis_index("band")
    bands = lax.axis_size("band")
    z, y = me // SIDE, lax.rem(me, SIDE)
    north = lax.rem(band + 1, bands)
    south = lax.rem(band + bands - 1, bands)

    def peer(o):
        return lax.rem(z + o[0], SIDE) * SIDE + lax.rem(y + o[1], SIDE)

    barrier = pltpu.get_barrier_semaphore()
    for b in (north, south):
        pl.semaphore_signal(barrier, inc=1, device_id={"band": b}, device_id_type=MESH)
    for o in OFFSETS:
        pl.semaphore_signal(barrier, inc=1, device_id={"comp": peer(o)}, device_id_type=MESH)

    for copy in arrivals:
        copy.wait()

    even_half = lax.rem(lax.broadcasted_iota(jnp.int32, (8, DEPTHS), 0), 2) == 0
    gs_ref[:, pl.ds(0, DEPTHS)] = jnp.where(
        even_half,
        jnp.broadcast_to(speed_ref[pl.ds(FREQS * me, 1), :], (8, DEPTHS)),
        jnp.broadcast_to(speed_ref[pl.ds(FREQS * me + 1, 1), :], (8, DEPTHS)),
    )
    stretch = jnp.where(row == 0, scalars_ref[5, ROWS * band], scalars_ref[5, ROWS * band + 1])
    stretch = jnp.where(row == 2, scalars_ref[5, ROWS * band + 2], stretch)
    stretch = jnp.where(row == 3, scalars_ref[5, ROWS * band + 3], stretch)
    flag_ref[...] = jnp.zeros((LANES, LANES), jnp.float32)
    for j in range(TILES):
        width = LANES if j < TILES - 1 else tail
        cols = pl.ds(j * LANES, width)
        sea = (land_ref[:, cols] == 0).astype(jnp.float32)
        flag_ref[pl.ds(ROWS * j, ROWS), pl.ds(0, width)] = sea
        for i in range(2):
            gust = wind_ref[i, :, cols]
            for r in range(ROWS):
                gust_ref[ROWS * j + r, i : i + 1, pl.ds(0, width)] = gust[r : r + 1]
        parts = [sea] + [ref[i, :, cols] for ref in (current_ref, slope_ref) for i in range(2)]
        for n, v in enumerate(parts):
            for f in range(FREQS):
                raw_ref[j, pl.ds(8 * n + f, 4, stride=2), pl.ds(0, width)] = v
        v = depth_ref[:, cols]
        for f in range(FREQS):
            cls_ref[j, pl.ds(f, 4, stride=2), pl.ds(0, width)] = v
    for j in range(TILES):
        def raw(n):
            v = raw_ref[j, pl.ds(8 * n, 8), :]
            return v if j < TILES - 1 else jnp.where(lane < tail, v, 0.0)

        cls = cls_ref[j]
        if j == TILES - 1:
            cls = jnp.where(lane < tail, cls, 0)
        cel = jnp.take_along_axis(gs_ref[...], cls, axis=1)
        sea = raw(0)
        sixth = cel * (sea * (1.0 / 6.0))
        fl_ref[F_SEA, j] = sea
        fl_ref[F_CX, j] = sixth * stretch
        fl_ref[F_CY, j] = sixth
        fl_ref[F_CUR0, j] = raw(1) * (sea * (1.0 / 6.0))
        fl_ref[F_CUR1, j] = raw(2) * (sea * (1.0 / 6.0))
        fl_ref[F_T0, j] = (TURNING_SCALE * sixth) * raw(3)
        fl_ref[F_T1, j] = (TURNING_SCALE * sixth) * raw(4)

    def load(d, carry):
        base = pl.multiple_of(8 * d, 8)
        for j in range(TILES):
            width = LANES if j < TILES - 1 else tail
            for f in range(FREQS):
                v = spec_ref[f, d, :, pl.ds(j * LANES, width)].astype(jnp.float32)
                x_ref[j, pl.ds(base + f, 4, stride=2), pl.ds(0, width)] = v
        return carry

    lax.fori_loop(0, ND, load, 0)

    def prepare(q, carry):
        base = pl.multiple_of(32 * q, 32)
        first = [None] * 4
        for j in range(TILES):
            v = [x_ref[j, pl.ds(base + 8 * i, 8), :] for i in range(4)]
            if j == TILES - 1:
                v = [jnp.where(lane < tail, w, 0.0) for w in v]
            v = [w * fl_ref[F_SEA, j] for w in v]
            if j == 0:
                first = v
            if j == TILES - 1:
                v = [
                    jnp.where(
                        lane < tail,
                        w,
                        jnp.where(lane < tail + 2, pltpu.roll(a, tail, 1), pltpu.roll(w, LANES - tail, 1)),
                    )
                    for w, a in zip(v, first)
                ]
            for i in range(4):
                x_ref[j, pl.ds(base + 8 * i, 8), :] = v[i]
            turned = [pltpu.roll(w, 4, 0) for w in v]
            low = [jnp.where(sub < 4, v[i], turned[i + 1]) for i in (0, 2)]
            high = [jnp.where(sub < 4, turned[i], v[i + 1]) for i in (0, 2)]
            rows = pl.ds(pl.multiple_of(16 * q, 16), 16)
            hs_ref[0, j, rows, :] = jnp.concatenate(low, axis=0).astype(jnp.bfloat16)
            hs_ref[1, j, rows, :] = jnp.concatenate(high, axis=0).astype(jnp.bfloat16)
        return carry

    lax.fori_loop(0, ND // 4, prepare, 0, unroll=3)

    pl.semaphore_wait(barrier, len(OFFSETS) + 2)
    halos = []
    for c in range(CHUNKS):
        for side, b in ((0, south), (1, north)):
            copy = pltpu.make_async_remote_copy(
                src_ref=hs_ref.at[side, pl.ds(PER * c, PER)],
                dst_ref=hr_ref.at[side, pl.ds(PER * c, PER)],
                send_sem=halo_send.at[side, c],
                recv_sem=halo_recv.at[side, c],
                device_id={"band": b},
                device_id_type=MESH,
            )
            copy.start()
            halos.append(copy)

    build_tables(counts_ref, flag_ref, tabv_ref, loc_ref)
    table_copy = pltpu.make_async_copy(tabv_ref, tab_ref, tab_sem)
    table_copy.start()

    def along(d, carry):
        base = pl.multiple_of(8 * d, 8)
        cos_d = scalars_ref[0, d]
        x = [x_ref[j, pl.ds(base, 8), :] for j in range(TILES)]
        r1 = [pltpu.roll(v, 1, 1) for v in x]
        r2 = [pltpu.roll(v, 2, 1) for v in x]
        l1 = [pltpu.roll(v, LANES - 1, 1) for v in x]
        l2 = [pltpu.roll(v, LANES - 2, 1) for v in x]
        for j in range(TILES):
            before, after = (j - 1) % TILES, (j + 1) % TILES
            behind = jnp.where(lane < 1, r1[before], r1[j])
            far_behind = jnp.where(lane < 2, r2[before], r2[j])
            ahead = jnp.where(lane >= LANES - 1, l1[after], l1[j])
            far_ahead = jnp.where(lane >= LANES - 2, l2[after], l2[j])
            speed = fl_ref[F_CX, j] * cos_d + fl_ref[F_CUR0, j]
            out = x[j] - upwind12(far_behind, behind, x[j], ahead, far_ahead, speed)
            adv_ref[j, pl.ds(base + 16, 8), :] = out
        return carry

    lax.fori_loop(0, ND, along, 0, unroll=4)

    keep_dn = (band < bands - 1).astype(jnp.float32)
    keep_up = (band > 0).astype(jnp.float32)
    zero = jnp.zeros((8, LANES), jnp.float32)

    def reduce_start(axis, c, src, dst):
        copies = []
        for i in range(1, SIDE):
            o = (0, i) if axis == 0 else (i, 0)
            copy = pltpu.make_async_remote_copy(
                src_ref=src.at[c],
                dst_ref=dst.at[c, i - 1],
                send_sem=sum_send.at[axis, c, i - 1],
                recv_sem=sum_recv.at[axis, c, i - 1],
                device_id={"comp": peer(o)},
                device_id_type=MESH,
            )
            copy.start()
            copies.append(copy)
        return copies

    sums_y, sums_z = [], []

    def pass_on(c):
        for copy in sums_y[c]:
            copy.wait()
        total_ref[c] = (part_ref[c] + yr_ref[c, 0]) + (yr_ref[c, 1] + yr_ref[c, 2])
        sums_z.append(reduce_start(1, c, total_ref, zr_ref))

    part_ref[...] = jnp.zeros((CHUNKS, 16, LANES), jnp.float32)

    for c in range(CHUNKS):
        halos[2 * c].wait_recv()
        halos[2 * c + 1].wait_recv()

        def across(q, carry):
            rows = pl.ds(pl.multiple_of(16 * q, 16), 16)
            base = pl.multiple_of(32 * q, 32)
            for j in range(PER * c, PER * c + PER):
                dn = hr_ref[0, j, rows, :].astype(jnp.float32) * keep_dn
                up = hr_ref[1, j, rows, :].astype(jnp.float32) * keep_up
                for i in range(4):
                    a, b = dn[8 * (i // 2) : 8 * (i // 2) + 8], up[8 * (i // 2) : 8 * (i // 2) + 8]
                    if i % 2 == 0:
                        h = jnp.where(sub < 4, a, pltpu.roll(b, 4, 0))
                    else:
                        h = jnp.where(sub < 4, pltpu.roll(a, 4, 0), b)
                    here = pl.ds(base + 8 * i, 8)
                    v = x_ref[j, here, :]
                    ahead = pltpu.roll(jnp.where(row == 0, h, v), 6, 0)
                    far_ahead = pltpu.roll(jnp.where(row < 2, h, v), 4, 0)
                    far_behind = pltpu.roll(jnp.where(row < 2, v, h), 4, 0)
                    behind = pltpu.roll(jnp.where(row == 3, h, v), 2, 0)
                    speed = fl_ref[F_CY, j] * scalars_ref[1, 4 * q + i] + fl_ref[F_CUR1, j]
                    flux = upwind12(far_behind, behind, v, ahead, far_ahead, speed)
                    there = pl.ds(base + (8 * i + 16), 8)
                    adv_ref[j, there, :] = adv_ref[j, there, :] - flux
            return carry

        lax.fori_loop(0, ND // 4, across, 0, unroll=3)

        for j in range(PER * c, PER * c + PER):
            adv_ref[j, pl.ds(0, 16), :] = adv_ref[j, pl.ds(8 * ND, 16), :]
            adv_ref[j, pl.ds(8 * ND + 16, 16), :] = adv_ref[j, pl.ds(16, 16), :]

        def refract(q, sums):
            base = pl.multiple_of(8 * RUN * q, 8)
            sums = list(sums)
            for j in range(PER * c, PER * c + PER):
                near = [adv_ref[j, pl.ds(base + 8 * i, 8), :] for i in range(RUN + 4)]
                t0, t1 = fl_ref[F_T0, j], fl_ref[F_T1, j]
                for i in range(RUN):
                    d = RUN * q + i
                    speed = t0 * scalars_ref[1, d] - t1 * scalars_ref[0, d]
                    out = near[i + 2] - upwind12(*near[i : i + 5], speed)
                    sums[j - PER * c] = sums[j - PER * c] + out * out
                    t_ref[j, pl.ds(d, 8, stride=ND), :] = out
            return tuple(sums)

        sums = lax.fori_loop(0, ND // RUN, refract, (zero,) * PER, unroll=2)
        for i in range(PER):
            j = PER * c + i
            sq_ref[...] = sums[i] + pltpu.roll(sums[i], 7, 0)
            part_ref[c, pl.ds(4 * i, 4), :] = sq_ref[pl.ds(0, 4, stride=2), :]
        sums_y.append(reduce_start(0, c, part_ref, yr_ref))
        if c >= 2:
            pass_on(c - 2)

    t_rows = t_ref.reshape(GROUPS, COMPS, LANES)

    def step(k, carry):
        keep = tab_ref[AT_KEEP, k].astype(jnp.float32)
        spot = tab_ref[AT_SPOT, k]
        local = lane + tab_ref[AT_DELTA, k]
        valid = (lane < tab_ref[AT_LEN, k]) & (local >= 0) & (local < tab_ref[AT_COUNT, k])
        local = jnp.clip(local, 0, LANES - 1)
        idx = jnp.take_along_axis(loc_ref[spot], local, axis=1)
        idx_ref[k] = jnp.where(valid, idx, -1)
        parts = []
        for m in range(COMPS // 8):
            data = t_rows[spot, pl.ds(8 * m, 8), :]
            got = jnp.take_along_axis(data, idx, axis=1)
            part = jnp.where(valid, got, carry[m] * keep)
            stage_ref[k, pl.ds(8 * m, 8), :] = part
            parts.append(part)
        gust = jnp.where(valid, jnp.take_along_axis(gust_ref[spot], idx, axis=1), carry[COMPS // 8])
        gusts_ref[k] = gust
        return tuple(parts) + (gust,)

    table_copy.wait()
    carry = lax.fori_loop(0, STEPS // 2, step, (zero,) * (COMPS // 8 + 1), unroll=8)
    pass_on(CHUNKS - 2)
    pass_on(CHUNKS - 1)
    lax.fori_loop(STEPS // 2, STEPS, step, carry, unroll=8)

    def by_row(q):
        low, high = scalars_ref[q, FREQS * me], scalars_ref[q, FREQS * me + 1]
        mixed = jnp.where(sub < 4, low, high)
        return [low if m < 4 else (mixed if m == 4 else high) for m in range(COMPS // 8)]

    rise, calm = by_row(2), by_row(3)
    for i in range(2):
        for m in range(COMPS // 8):
            rows = pl.ds(8 * m, 8)
            compass_ref[i, rows, :] = compass_ref[i, rows, :] * rise[m]

    def grow(c, carry):
        for j in range(3):
            k = tab_ref[AT_LAST, 3 * c + j]
            gust = gusts_ref[k]
            east = jnp.broadcast_to(gust[0:1], (8, LANES))
            north = jnp.broadcast_to(gust[1:2], (8, LANES))
            for m in range(COMPS // 8):
                rows = pl.ds(8 * m, 8)
                push = east * compass_ref[0, rows, :] + north * compass_ref[1, rows, :]
                grown_ref[3 * c + j, rows, :] = stage_ref[k, rows, :] * jnp.exp(jnp.maximum(push - calm[m], 0.0))
        return carry

    lax.fori_loop(0, BLOCKS, grow, 0, unroll=2)
    for c in range(CHUNKS):
        for copy in sums_z[c]:
            copy.wait()
        total = (total_ref[c] + zr_ref[c, 0]) + (zr_ref[c, 1] + zr_ref[c, 2])
        total = jnp.sqrt(total * (1.0 / (BLOCKS * COMPS)) + 1e-6)
        for i in range(ROWS * PER):
            level_ref[ROWS * PER * c + i] = jnp.broadcast_to(total[i : i + 1], (8, LANES))

    def strengths(k, acc):
        keep = tab_ref[AT_KEEP, k].astype(jnp.float32)
        idx = idx_ref[k]
        got = jnp.take_along_axis(level_ref[tab_ref[AT_SPOT, k]], jnp.maximum(idx, 0), axis=1)
        acc = jnp.where(idx >= 0, got, acc * keep)
        dec_ref[k] = acc
        return acc

    lax.fori_loop(0, STEPS, strengths, zero, unroll=32)

    fade0 = scalars_ref[4, FREQS * me]
    fade1 = scalars_ref[4, FREQS * me + 1]

    def block(c, store):
        places = [tab_ref[AT_LAST, 3 * c + j] for j in range(3)]
        rows = []
        for j in range(3):
            s = dec_ref[places[j]]
            e0 = jnp.exp(-fade0 * s)
            e1 = jnp.exp(-fade1 * s)
            mixed = jnp.where(sub < 4, e0, e1)
            values = []
            for m in range(COMPS // 8):
                e = e0 if m < 4 else (mixed if m == 4 else e1)
                values.append(grown_ref[3 * c + j, pl.ds(8 * m, 8), :] * e)
            if j < 2:
                rows += values
            else:
                for m in range(5):
                    v = values[m]
                    if m < 4:
                        v = jnp.where(lane < 64, v, pltpu.roll(values[5 + m], 64, 1))
                    rows.append(v)
                rows.append(zero)
        for m in range(PACK // 16):
            store(m, jnp.concatenate(rows[2 * m : 2 * m + 2], axis=0).astype(jnp.bfloat16))

    copies = []
    for i, o in enumerate(OFFSETS):
        other = peer(o)

        def put(m, v):
            sb_ref[i, pl.ds(16 * m, 16), :] = v

        block(other, put)
        copy = pltpu.make_async_remote_copy(
            src_ref=sb_ref.at[i],
            dst_ref=rb_ref.at[me],
            send_sem=send_sem.at[i],
            recv_sem=recv_sem.at[i],
            device_id={"comp": other},
            device_id_type=MESH,
        )
        copy.start()
        copies.append(copy)

    def put_own(m, v):
        own_ref[pl.ds(16 * m, 16), :] = v

    block(me, put_own)
    own_copy = pltpu.make_async_copy(own_ref, rb_ref.at[me], own_sem)
    own_copy.start()
    own_copy.wait()
    for copy in halos:
        copy.wait_send()
    for copy in copies:
        copy.wait()


def finish_kernel(rb_ref, out_ref, in_ref, v_ref, in_sem):
    copy = pltpu.make_async_copy(rb_ref, in_ref, in_sem)
    copy.start()
    copy.wait()

    def spread(i, carry):
        base = pl.multiple_of(COMPS * i, 8)
        v = in_ref[i].astype(jnp.float32)
        for j in range(2):
            v_ref[j, pl.ds(base, COMPS), :] = v[COMPS * j : COMPS * (j + 1)]
        v_ref[2, pl.ds(base, 40), :] = v[2 * COMPS : 2 * COMPS + 40]
        v_ref[2, pl.ds(base + 40, 32), :] = pltpu.roll(v[2 * COMPS : 2 * COMPS + 32], 64, 1)
        return carry

    lax.fori_loop(0, BLOCKS, spread, 0, unroll=4)
    for m in range(BLOCKS * COMPS // LANES):
        for j in range(3):
            block = v_ref[j, pl.ds(LANES * m, LANES), :].T.astype(jnp.bfloat16)
            rows = min(LANES, SLOTS - LANES * j)
            out_ref[pl.ds(LANES * j, rows), pl.ds(LANES * m, LANES)] = block[:rows]


def build_tables(counts_ref, flag_ref, tabv_ref, loc_ref):
    f32, bf16, i32 = jnp.float32, jnp.bfloat16, jnp.int32
    sub = lax.broadcasted_iota(i32, (LANES, LANES), 0)
    lanes = lax.broadcasted_iota(i32, (LANES, LANES), 1)
    lane = lax.broadcasted_iota(i32, (8, LANES), 1)

    def order(i):
        return jnp.where(i < GROUPS, (i & (ROWS - 1)) * TILES + (i >> 2), i)

    def product(a, b, dims=(((1,), (0,)), ((), ()))):
        return lax.dot_general(a, b, dims, preferred_element_type=f32)

    upper = (sub <= lanes).astype(f32).astype(bf16)
    ones = jnp.ones((LANES, LANES), bf16)
    flags = flag_ref[...].astype(bf16)
    inclusive = product(flags, upper)
    count_rows = product(flags, ones)
    ends = product((order(lanes) <= order(sub)).astype(f32).astype(bf16), count_rows.astype(bf16))[:GROUPS]
    count = product(ones[:16], flags, (((1,), (1,)), ((), ())))
    first = product(count.astype(bf16), (order(sub) < order(lanes)).astype(f32).astype(bf16))
    count, first = count[:8].astype(i32), first[:8].astype(i32)

    wide = lanes[:GROUPS]
    shift = wide - (inclusive[:GROUPS].astype(i32) - 1)
    word = jnp.where(flag_ref[pl.ds(0, GROUPS), :] > 0, wide + LANES * shift + LANES * LANES, 0)
    for k in range(7):
        bit = LANES << k
        moved = pltpu.roll(word, LANES - (1 << k), 1)
        word = jnp.where((moved & bit) != 0, moved, jnp.where((word & bit) != 0, 0, word))
    word = word & (LANES - 1)
    for g in range(GROUPS):
        loc_ref[g] = jnp.broadcast_to(word[g : g + 1], (8, LANES))

    block = (lane * 171) >> 9
    part = lane - 3 * block
    size = jnp.zeros((8, LANES), i32)
    rank = jnp.zeros((8, LANES), i32)
    start = 0
    for c in range(BLOCKS):
        n = counts_ref[0, c]
        size = jnp.where(block == c, n, size)
        rank = jnp.where(block == c, start, rank)
        start = start + n
    rank = rank + LANES * part
    length = jnp.clip(size - LANES * part, 0, LANES)
    real = lane < 3 * BLOCKS

    def groups_before(r):
        hit = (ends <= r[:1].astype(f32)).astype(f32)
        return jnp.minimum(jnp.broadcast_to(jnp.sum(hit, axis=0, keepdims=True), (8, LANES)), GROUPS - 1.0)

    low = groups_before(rank)
    high = groups_before(rank + jnp.maximum(length, 1) - 1)
    width = jnp.where(real, jnp.where(length > 0, high - low + 1.0, 1.0), 0.0)
    stop = product(jnp.concatenate([width, width], axis=0).astype(bf16), upper)[:8]
    begin = stop - width
    column = jnp.sum(jnp.where(wide <= sub[:GROUPS], width[:1], 0.0), axis=1, keepdims=True)
    tile = jnp.sum((column <= wide.astype(f32)).astype(f32), axis=0, keepdims=True)
    tile = jnp.broadcast_to(jnp.minimum(tile, 3 * BLOCKS - 1.0), (8, LANES)).astype(i32)

    def at(values, index):
        return jnp.take_along_axis(values, index, axis=1)

    group = lane + at((low - begin).astype(i32), tile)
    group = jnp.clip(group, 0, GROUPS - 1)
    r = (group * 171) >> 11
    spot = ROWS * (group - TILES * r) + r
    tabv_ref[AT_SPOT : AT_SPOT + 1] = spot[:1]
    tabv_ref[AT_KEEP : AT_KEEP + 1] = (lane > at(begin.astype(i32), tile)).astype(i32)[:1]
    tabv_ref[AT_DELTA : AT_DELTA + 1] = (at(rank, tile) - at(first, spot))[:1]
    tabv_ref[AT_LEN : AT_LEN + 1] = at(length, tile)[:1]
    tabv_ref[AT_COUNT : AT_COUNT + 1] = at(count, spot)[:1]
    tabv_ref[AT_LAST : AT_LAST + 1] = jnp.clip((stop - 1.0).astype(i32), 0, STEPS - 1)[:1]
    tabv_ref[AT_LAST + 1 :] = jnp.zeros((7 - AT_LAST, LANES), i32)


def body(spectra, depth_class, group_speed, current, depth_slope, wind, land_mask, block_counts):
    cos_t, sin_t = angles()
    latitude = (-60.0 + 120.0 * (np.arange(ROWS * lax.axis_size("band")) + 0.5) / (ROWS * lax.axis_size("band"))) * (
        math.pi / 180.0
    )
    stretch = (1.0 / np.cos(latitude)).astype(np.float32)
    angular = 2.0 * math.pi * 0.0418 * np.power(1.1, np.arange(BLOCKS * FREQS, dtype=np.float64))
    ratio = angular / angular[-1]
    phase = 9.81 / angular
    coef = np.stack([GROWTH_RATE * ratio / phase, GROWTH_RATE * ratio, DAMPING * ratio]).astype(np.float32)

    scalars = np.zeros((8, LANES), np.float32)
    scalars[0, :ND], scalars[1, :ND] = cos_t, sin_t
    scalars[2:5, : BLOCKS * FREQS] = coef
    scalars[5, : stretch.size] = stretch
    compass = np.stack([np.tile(cos_t, FREQS), np.tile(sin_t, FREQS)])
    compass = np.ascontiguousarray(np.broadcast_to(compass[:, :, None], (2, COMPS, LANES)))

    vmem = pl.BlockSpec(memory_space=pltpu.VMEM)
    f32, bf16 = jnp.float32, jnp.bfloat16
    dma = pltpu.SemaphoreType.DMA
    rb = pl.pallas_call(
        step_kernel,
        out_shape=jax.ShapeDtypeStruct((BLOCKS, PACK, LANES), bf16),
        in_specs=[pl.BlockSpec(memory_space=pltpu.HBM)] * 10,
        out_specs=pl.BlockSpec(memory_space=pltpu.HBM),
        scratch_shapes=[
            pltpu.SMEM((8, LANES), f32),
            pltpu.VMEM((2, COMPS, LANES), f32),
            pltpu.SMEM(block_counts.shape, jnp.int32),
            pltpu.VMEM(spectra.shape, bf16),
            pltpu.VMEM(depth_class.shape, jnp.int32),
            pltpu.VMEM(group_speed.shape[::-1], f32),
            pltpu.VMEM(current.shape, f32),
            pltpu.VMEM(depth_slope.shape, f32),
            pltpu.VMEM(wind.shape, f32),
            pltpu.VMEM(land_mask.shape, jnp.int32),
            pltpu.VMEM((GROUPS, 8, LANES), f32),
            pltpu.VMEM((STEPS, 8, LANES), f32),
            pltpu.VMEM((8, LANES), f32),
            pltpu.VMEM((TILES, 8 * 5, LANES), f32),
            pltpu.VMEM((TILES, 8, LANES), jnp.int32),
            pltpu.VMEM((LANES, LANES), f32),
            pltpu.VMEM((8, LANES), jnp.int32),
            pltpu.SMEM((8, LANES), jnp.int32),
            pltpu.VMEM((GROUPS, 8, LANES), jnp.int32),
            pltpu.VMEM((TILES, 8 * ND, LANES), f32),
            pltpu.VMEM((TILES, 8 * (ND + 4), LANES), f32),
            pltpu.VMEM((TILES, 8 * ND, LANES), f32),
            pltpu.VMEM((STEPS, COMPS, LANES), f32),
            pltpu.VMEM((3 * BLOCKS, COMPS, LANES), f32),
            pltpu.VMEM((STEPS, 8, LANES), jnp.int32),
            pltpu.VMEM((STEPS, 8, LANES), f32),
            pltpu.VMEM((7, TILES, 8, LANES), f32),
            pltpu.VMEM((2, TILES, 4 * ND, LANES), bf16),
            pltpu.VMEM((2, TILES, 4 * ND, LANES), bf16),
            pltpu.VMEM((8, LANES), f32),
            pltpu.VMEM((CHUNKS, 16, LANES), f32),
            pltpu.VMEM((CHUNKS, 16, LANES), f32),
            pltpu.VMEM((GROUPS, 8, LANES), f32),
            pltpu.VMEM((CHUNKS, SIDE - 1, 16, LANES), f32),
            pltpu.VMEM((CHUNKS, SIDE - 1, 16, LANES), f32),
            pltpu.VMEM((BLOCKS - 1, PACK, LANES), bf16),
            pltpu.VMEM((PACK, LANES), bf16),
            dma((10,)),
            dma,
            dma,
            dma((2, CHUNKS)),
            dma((2, CHUNKS)),
            dma((2, CHUNKS, SIDE - 1)),
            dma((2, CHUNKS, SIDE - 1)),
            dma((BLOCKS - 1,)),
            dma((BLOCKS - 1,)),
        ],
        compiler_params=pltpu.CompilerParams(
            collective_id=0, has_side_effects=True, vmem_limit_bytes=58 * 1024 * 1024
        ),
        name="wave_step",
    )(
        jnp.asarray(scalars),
        jnp.asarray(compass),
        block_counts,
        spectra,
        depth_class,
        group_speed.T,
        current,
        depth_slope,
        wind,
        land_mask,
    )

    out = pl.pallas_call(
        finish_kernel,
        out_shape=jax.ShapeDtypeStruct((SLOTS, BLOCKS * COMPS), bf16),
        in_specs=[pl.BlockSpec(memory_space=pltpu.HBM)],
        out_specs=vmem,
        scratch_shapes=[
            pltpu.VMEM((BLOCKS, PACK, LANES), bf16),
            pltpu.VMEM((3, BLOCKS * COMPS, LANES), f32),
            dma,
        ],
        compiler_params=pltpu.CompilerParams(vmem_limit_bytes=58 * 1024 * 1024),
        name="finish",
    )(rb)
    return out.T


def solution(mesh):
    return jax.shard_map(
        body,
        mesh=mesh,
        in_specs=(
            P("comp", None, "band", None),
            P("band", None),
            P(),
            P(None, "band", None),
            P(None, "band", None),
            P(None, "band", None),
            P("band", None),
            P("band", None),
        ),
        out_specs=P(None, ("comp", "band")),
        check_vma=False,
    )
```

```python
import math

import jax
import jax.numpy as jnp
import numpy as np
from jax import lax
from jax.experimental import pallas as pl
from jax.experimental.pallas import tpu as pltpu
from jax.sharding import PartitionSpec as P

GROWTH_RATE = 0.05
DAMPING = 1.5
TURNING_SCALE = 0.5

FREQS = 2
LANES = 128
ND = 36
ROWS = 4
NLON = 1440
TILES = 12
GROUPS = ROWS * TILES
BLOCKS = 16
SLOTS = 315
DEPTHS = 64
STEPS = 96
COMPS = FREQS * ND
PACK = 192
CHUNKS = 3
PER = TILES // CHUNKS
RUN = 6
SIDE = 4

AT_SPOT, AT_KEEP, AT_DELTA, AT_LEN, AT_COUNT, AT_LAST = range(6)

(F_SEA, F_CX, F_CY, F_CUR0, F_CUR1, F_T0, F_T1) = range(7)

MESH = pl.DeviceIdType.MESH


def angles():
    heading = (np.arange(ND, dtype=np.float32) * np.float32(2.0 * math.pi / ND)).astype(np.float64)
    return (np.cos(heading).astype(np.float32), np.sin(heading).astype(np.float32))


def upwind12(far_behind, behind, centre, ahead, far_ahead, speed):
    forward = speed > 0
    down = jnp.where(forward, ahead, behind)
    up = jnp.where(forward, behind, ahead)
    far = jnp.where(forward, far_behind, far_ahead)
    return jnp.abs(speed) * ((2.0 * down + far) + (3.0 * centre - 6.0 * up))


OFFSETS = sorted(
    [(a, b) for a in range(SIDE) for b in range(SIDE) if a or b],
    key=lambda o: -(min(o[0], SIDE - o[0]) + min(o[1], SIDE - o[1])),
)


def step_kernel(
    scalars_hbm, compass_hbm, counts_hbm, spec_hbm, depth_hbm, speed_hbm, current_hbm, slope_hbm, wind_hbm, land_hbm,
    rb_ref,
    scalars_ref, compass_ref, counts_ref, spec_ref, depth_ref, speed_ref, current_ref, slope_ref, wind_ref, land_ref,
    gust_ref, gusts_ref,
    gs_ref, raw_ref, cls_ref, flag_ref, tabv_ref, tab_ref, loc_ref, x_ref, adv_ref, t_ref, stage_ref, grown_ref, idx_ref, dec_ref, fl_ref, hs_ref, hr_ref, sq_ref, part_ref, total_ref, level_ref, yr_ref, zr_ref, sb_ref, own_ref,
    in_sem, tab_sem, own_sem, halo_send, halo_recv, sum_send, sum_recv, send_sem, recv_sem,
):
    arrivals = [
        pltpu.make_async_copy(src, dst, in_sem.at[i])
        for i, (src, dst) in enumerate(
            [
                (land_hbm, land_ref),
                (spec_hbm, spec_ref),
                (scalars_hbm, scalars_ref),
                (speed_hbm, speed_ref),
                (depth_hbm, depth_ref),
                (current_hbm, current_ref),
                (slope_hbm, slope_ref),
                (wind_hbm, wind_ref),
                (counts_hbm, counts_ref),
                (compass_hbm, compass_ref),
            ]
        )
    ]
    for copy in arrivals:
        copy.start()
    lane = lax.broadcasted_iota(jnp.int32, (8, LANES), 1)
    sub = lax.broadcasted_iota(jnp.int32, (8, LANES), 0)
    row = sub // 2
    tail = NLON - (TILES - 1) * LANES
    me = lax.axis_index("comp")
    band = lax.axis_index("band")
    bands = lax.axis_size("band")
    z, y = me // SIDE, lax.rem(me, SIDE)
    north = lax.rem(band + 1, bands)
    south = lax.rem(band + bands - 1, bands)

    def peer(o):
        return lax.rem(z + o[0], SIDE) * SIDE + lax.rem(y + o[1], SIDE)

    barrier = pltpu.get_barrier_semaphore()
    for b in (north, south):
        pl.semaphore_signal(barrier, inc=1, device_id={"band": b}, device_id_type=MESH)
    for o in OFFSETS:
        pl.semaphore_signal(barrier, inc=1, device_id={"comp": peer(o)}, device_id_type=MESH)

    for copy in arrivals:
        copy.wait()

    even_half = lax.rem(lax.broadcasted_iota(jnp.int32, (8, DEPTHS), 0), 2) == 0
    gs_ref[:, pl.ds(0, DEPTHS)] = jnp.where(
        even_half,
        jnp.broadcast_to(speed_ref[pl.ds(FREQS * me, 1), :], (8, DEPTHS)),
        jnp.broadcast_to(speed_ref[pl.ds(FREQS * me + 1, 1), :], (8, DEPTHS)),
    )
    stretch = jnp.where(row == 0, scalars_ref[5, ROWS * band], scalars_ref[5, ROWS * band + 1])
    stretch = jnp.where(row == 2, scalars_ref[5, ROWS * band + 2], stretch)
    stretch = jnp.where(row == 3, scalars_ref[5, ROWS * band + 3], stretch)
    flag_ref[...] = jnp.zeros((LANES, LANES), jnp.float32)
    for j in range(TILES):
        width = LANES if j < TILES - 1 else tail
        cols = pl.ds(j * LANES, width)
        sea = (land_ref[:, cols] == 0).astype(jnp.float32)
        flag_ref[pl.ds(ROWS * j, ROWS), pl.ds(0, width)] = sea
        for i in range(2):
            gust = wind_ref[i, :, cols]
            for r in range(ROWS):
                gust_ref[ROWS * j + r, i : i + 1, pl.ds(0, width)] = gust[r : r + 1]
        parts = [sea] + [ref[i, :, cols] for ref in (current_ref, slope_ref) for i in range(2)]
        for n, v in enumerate(parts):
            for f in range(FREQS):
                raw_ref[j, pl.ds(8 * n + f, 4, stride=2), pl.ds(0, width)] = v
        v = depth_ref[:, cols]
        for f in range(FREQS):
            cls_ref[j, pl.ds(f, 4, stride=2), pl.ds(0, width)] = v
    for j in range(TILES):
        def raw(n):
            v = raw_ref[j, pl.ds(8 * n, 8), :]
            return v if j < TILES - 1 else jnp.where(lane < tail, v, 0.0)

        cls = cls_ref[j]
        if j == TILES - 1:
            cls = jnp.where(lane < tail, cls, 0)
        cel = jnp.take_along_axis(gs_ref[...], cls, axis=1)
        sea = raw(0)
        sixth = cel * (sea * (1.0 / 6.0))
        fl_ref[F_SEA, j] = sea
        fl_ref[F_CX, j] = sixth * stretch
        fl_ref[F_CY, j] = sixth
        fl_ref[F_CUR0, j] = raw(1) * (sea * (1.0 / 6.0))
        fl_ref[F_CUR1, j] = raw(2) * (sea * (1.0 / 6.0))
        fl_ref[F_T0, j] = (TURNING_SCALE * sixth) * raw(3)
        fl_ref[F_T1, j] = (TURNING_SCALE * sixth) * raw(4)

    def load(d, carry):
        base = pl.multiple_of(8 * d, 8)
        for j in range(TILES):
            width = LANES if j < TILES - 1 else tail
            for f in range(FREQS):
                v = spec_ref[f, d, :, pl.ds(j * LANES, width)].astype(jnp.float32)
                x_ref[j, pl.ds(base + f, 4, stride=2), pl.ds(0, width)] = v
        return carry

    lax.fori_loop(0, ND, load, 0)

    def prepare(q, carry):
        base = pl.multiple_of(32 * q, 32)
        first = [None] * 4
        for j in range(TILES):
            v = [x_ref[j, pl.ds(base + 8 * i, 8), :] for i in range(4)]
            if j == TILES - 1:
                v = [jnp.where(lane < tail, w, 0.0) for w in v]
            v = [w * fl_ref[F_SEA, j] for w in v]
            if j == 0:
                first = v
            if j == TILES - 1:
                v = [
                    jnp.where(
                        lane < tail,
                        w,
                        jnp.where(lane < tail + 2, pltpu.roll(a, tail, 1), pltpu.roll(w, LANES - tail, 1)),
                    )
                    for w, a in zip(v, first)
                ]
            for i in range(4):
                x_ref[j, pl.ds(base + 8 * i, 8), :] = v[i]
            turned = [pltpu.roll(w, 4, 0) for w in v]
            low = [jnp.where(sub < 4, v[i], turned[i + 1]) for i in (0, 2)]
            high = [jnp.where(sub < 4, turned[i], v[i + 1]) for i in (0, 2)]
            rows = pl.ds(pl.multiple_of(16 * q, 16), 16)
            hs_ref[0, j, rows, :] = jnp.concatenate(low, axis=0).astype(jnp.bfloat16)
            hs_ref[1, j, rows, :] = jnp.concatenate(high, axis=0).astype(jnp.bfloat16)
        return carry

    lax.fori_loop(0, ND // 4, prepare, 0, unroll=3)

    pl.semaphore_wait(barrier, len(OFFSETS) + 2)
    halos = []

    def send_halos(c):
        for side, b in ((0, south), (1, north)):
            copy = pltpu.make_async_remote_copy(
                src_ref=hs_ref.at[side, pl.ds(PER * c, PER)],
                dst_ref=hr_ref.at[side, pl.ds(PER * c, PER)],
                send_sem=halo_send.at[side, c],
                recv_sem=halo_recv.at[side, c],
                device_id={"band": b},
                device_id_type=MESH,
            )
            copy.start()
            halos.append(copy)

    for c in range(CHUNKS // 2):
        send_halos(c)

    build_tables(counts_ref, flag_ref, tabv_ref, loc_ref)
    table_copy = pltpu.make_async_copy(tabv_ref, tab_ref, tab_sem)
    table_copy.start()

    for c in range(CHUNKS // 2, CHUNKS):
        send_halos(c)

    def along(d, carry):
        base = pl.multiple_of(8 * d, 8)
        cos_d = scalars_ref[0, d]
        x = [x_ref[j, pl.ds(base, 8), :] for j in range(TILES)]
        r1 = [pltpu.roll(v, 1, 1) for v in x]
        r2 = [pltpu.roll(v, 2, 1) for v in x]
        l1 = [pltpu.roll(v, LANES - 1, 1) for v in x]
        l2 = [pltpu.roll(v, LANES - 2, 1) for v in x]
        for j in range(TILES):
            before, after = (j - 1) % TILES, (j + 1) % TILES
            behind = jnp.where(lane < 1, r1[before], r1[j])
            far_behind = jnp.where(lane < 2, r2[before], r2[j])
            ahead = jnp.where(lane >= LANES - 1, l1[after], l1[j])
            far_ahead = jnp.where(lane >= LANES - 2, l2[after], l2[j])
            speed = fl_ref[F_CX, j] * cos_d + fl_ref[F_CUR0, j]
            out = x[j] - upwind12(far_behind, behind, x[j], ahead, far_ahead, speed)
            adv_ref[j, pl.ds(base + 16, 8), :] = out
        return carry

    lax.fori_loop(0, ND, along, 0, unroll=4)

    keep_dn = (band < bands - 1).astype(jnp.float32)
    keep_up = (band > 0).astype(jnp.float32)
    zero = jnp.zeros((8, LANES), jnp.float32)

    def reduce_start(axis, c, src, dst):
        copies = []
        for i in range(1, SIDE):
            o = (0, i) if axis == 0 else (i, 0)
            copy = pltpu.make_async_remote_copy(
                src_ref=src.at[c],
                dst_ref=dst.at[c, i - 1],
                send_sem=sum_send.at[axis, c, i - 1],
                recv_sem=sum_recv.at[axis, c, i - 1],
                device_id={"comp": peer(o)},
                device_id_type=MESH,
            )
            copy.start()
            copies.append(copy)
        return copies

    sums_y, sums_z = [], []

    def pass_on(c):
        for copy in sums_y[c]:
            copy.wait()
        total_ref[c] = (part_ref[c] + yr_ref[c, 0]) + (yr_ref[c, 1] + yr_ref[c, 2])
        sums_z.append(reduce_start(1, c, total_ref, zr_ref))

    part_ref[...] = jnp.zeros((CHUNKS, 16, LANES), jnp.float32)

    for c in range(CHUNKS):
        halos[2 * c].wait_recv()
        halos[2 * c + 1].wait_recv()

        def across(q, carry):
            rows = pl.ds(pl.multiple_of(16 * q, 16), 16)
            base = pl.multiple_of(32 * q, 32)
            for j in range(PER * c, PER * c + PER):
                dn = hr_ref[0, j, rows, :].astype(jnp.float32) * keep_dn
                up = hr_ref[1, j, rows, :].astype(jnp.float32) * keep_up
                for i in range(4):
                    a, b = dn[8 * (i // 2) : 8 * (i // 2) + 8], up[8 * (i // 2) : 8 * (i // 2) + 8]
                    if i % 2 == 0:
                        h = jnp.where(sub < 4, a, pltpu.roll(b, 4, 0))
                    else:
                        h = jnp.where(sub < 4, pltpu.roll(a, 4, 0), b)
                    here = pl.ds(base + 8 * i, 8)
                    v = x_ref[j, here, :]
                    ahead = pltpu.roll(jnp.where(row == 0, h, v), 6, 0)
                    far_ahead = pltpu.roll(jnp.where(row < 2, h, v), 4, 0)
                    far_behind = pltpu.roll(jnp.where(row < 2, v, h), 4, 0)
                    behind = pltpu.roll(jnp.where(row == 3, h, v), 2, 0)
                    speed = fl_ref[F_CY, j] * scalars_ref[1, 4 * q + i] + fl_ref[F_CUR1, j]
                    flux = upwind12(far_behind, behind, v, ahead, far_ahead, speed)
                    there = pl.ds(base + (8 * i + 16), 8)
                    adv_ref[j, there, :] = adv_ref[j, there, :] - flux
            return carry

        lax.fori_loop(0, ND // 4, across, 0)

        for j in range(PER * c, PER * c + PER):
            adv_ref[j, pl.ds(0, 16), :] = adv_ref[j, pl.ds(8 * ND, 16), :]
            adv_ref[j, pl.ds(8 * ND + 16, 16), :] = adv_ref[j, pl.ds(16, 16), :]

        def refract(q, sums):
            base = pl.multiple_of(8 * RUN * q, 8)
            sums = list(sums)
            for j in range(PER * c, PER * c + PER):
                near = [adv_ref[j, pl.ds(base + 8 * i, 8), :] for i in range(RUN + 4)]
                t0, t1 = fl_ref[F_T0, j], fl_ref[F_T1, j]
                for i in range(RUN):
                    d = RUN * q + i
                    speed = t0 * scalars_ref[1, d] - t1 * scalars_ref[0, d]
                    out = near[i + 2] - upwind12(*near[i : i + 5], speed)
                    sums[j - PER * c] = sums[j - PER * c] + out * out
                    t_ref[j, pl.ds(d, 8, stride=ND), :] = out
            return tuple(sums)

        sums = lax.fori_loop(0, ND // RUN, refract, (zero,) * PER)
        for i in range(PER):
            j = PER * c + i
            sq_ref[...] = sums[i] + pltpu.roll(sums[i], 7, 0)
            part_ref[c, pl.ds(4 * i, 4), :] = sq_ref[pl.ds(0, 4, stride=2), :]
        sums_y.append(reduce_start(0, c, part_ref, yr_ref))
        if c >= 2:
            pass_on(c - 2)

    t_rows = t_ref.reshape(GROUPS, COMPS, LANES)

    def step(k, carry):
        keep = tab_ref[AT_KEEP, k].astype(jnp.float32)
        spot = tab_ref[AT_SPOT, k]
        local = lane + tab_ref[AT_DELTA, k]
        valid = (lane < tab_ref[AT_LEN, k]) & (local >= 0) & (local < tab_ref[AT_COUNT, k])
        local = jnp.clip(local, 0, LANES - 1)
        idx = jnp.take_along_axis(loc_ref[spot], local, axis=1)
        idx_ref[k] = jnp.where(valid, idx, -1)
        parts = []
        for m in range(COMPS // 8):
            data = t_rows[spot, pl.ds(8 * m, 8), :]
            got = jnp.take_along_axis(data, idx, axis=1)
            part = jnp.where(valid, got, carry[m] * keep)
            stage_ref[k, pl.ds(8 * m, 8), :] = part
            parts.append(part)
        gust = jnp.where(valid, jnp.take_along_axis(gust_ref[spot], idx, axis=1), carry[COMPS // 8])
        gusts_ref[k] = gust
        return tuple(parts) + (gust,)

    table_copy.wait()
    carry = lax.fori_loop(0, STEPS // 2, step, (zero,) * (COMPS // 8 + 1), unroll=8)
    pass_on(CHUNKS - 2)
    pass_on(CHUNKS - 1)
    lax.fori_loop(STEPS // 2, STEPS, step, carry, unroll=8)

    def by_row(q):
        low, high = scalars_ref[q, FREQS * me], scalars_ref[q, FREQS * me + 1]
        mixed = jnp.where(sub < 4, low, high)
        return [low if m < 4 else (mixed if m == 4 else high) for m in range(COMPS // 8)]

    rise, calm = by_row(2), by_row(3)
    for i in range(2):
        for m in range(COMPS // 8):
            rows = pl.ds(8 * m, 8)
            compass_ref[i, rows, :] = compass_ref[i, rows, :] * rise[m]

    def grow(c, carry):
        for j in range(3):
            k = tab_ref[AT_LAST, 3 * c + j]
            gust = gusts_ref[k]
            east = jnp.broadcast_to(gust[0:1], (8, LANES))
            north = jnp.broadcast_to(gust[1:2], (8, LANES))
            for m in range(COMPS // 8):
                rows = pl.ds(8 * m, 8)
                push = east * compass_ref[0, rows, :] + north * compass_ref[1, rows, :]
                grown_ref[3 * c + j, rows, :] = stage_ref[k, rows, :] * jnp.exp(jnp.maximum(push - calm[m], 0.0))
        return carry

    lax.fori_loop(0, BLOCKS, grow, 0, unroll=2)
    for c in range(CHUNKS):
        for copy in sums_z[c]:
            copy.wait()
        total = (total_ref[c] + zr_ref[c, 0]) + (zr_ref[c, 1] + zr_ref[c, 2])
        total = jnp.sqrt(total * (1.0 / (BLOCKS * COMPS)) + 1e-6)
        for i in range(ROWS * PER):
            level_ref[ROWS * PER * c + i] = jnp.broadcast_to(total[i : i + 1], (8, LANES))

    def strengths(k, acc):
        keep = tab_ref[AT_KEEP, k].astype(jnp.float32)
        idx = idx_ref[k]
        got = jnp.take_along_axis(level_ref[tab_ref[AT_SPOT, k]], jnp.maximum(idx, 0), axis=1)
        acc = jnp.where(idx >= 0, got, acc * keep)
        dec_ref[k] = acc
        return acc

    lax.fori_loop(0, STEPS, strengths, zero, unroll=32)

    fade0 = scalars_ref[4, FREQS * me]
    fade1 = scalars_ref[4, FREQS * me + 1]

    def block(c, store):
        places = [tab_ref[AT_LAST, 3 * c + j] for j in range(3)]
        rows = []
        for j in range(3):
            s = dec_ref[places[j]]
            e0 = jnp.exp(-fade0 * s)
            e1 = jnp.exp(-fade1 * s)
            mixed = jnp.where(sub < 4, e0, e1)
            values = []
            for m in range(COMPS // 8):
                e = e0 if m < 4 else (mixed if m == 4 else e1)
                values.append(grown_ref[3 * c + j, pl.ds(8 * m, 8), :] * e)
            if j < 2:
                rows += values
            else:
                for m in range(5):
                    v = values[m]
                    if m < 4:
                        v = jnp.where(lane < 64, v, pltpu.roll(values[5 + m], 64, 1))
                    rows.append(v)
                rows.append(zero)
        for m in range(PACK // 16):
            store(m, jnp.concatenate(rows[2 * m : 2 * m + 2], axis=0).astype(jnp.bfloat16))

    copies = []
    for i, o in enumerate(OFFSETS):
        other = peer(o)

        def put(m, v):
            sb_ref[i, pl.ds(16 * m, 16), :] = v

        block(other, put)
        copy = pltpu.make_async_remote_copy(
            src_ref=sb_ref.at[i],
            dst_ref=rb_ref.at[me],
            send_sem=send_sem.at[i],
            recv_sem=recv_sem.at[i],
            device_id={"comp": other},
            device_id_type=MESH,
        )
        copy.start()
        copies.append(copy)

    def put_own(m, v):
        own_ref[pl.ds(16 * m, 16), :] = v

    block(me, put_own)
    own_copy = pltpu.make_async_copy(own_ref, rb_ref.at[me], own_sem)
    own_copy.start()
    own_copy.wait()
    for copy in halos:
        copy.wait_send()
    for copy in copies:
        copy.wait()


def finish_kernel(rb_ref, out_ref, in_ref, v_ref, in_sem):
    copies = [
        pltpu.make_async_copy(rb_ref.at[pl.ds(4 * i, 4)], in_ref.at[pl.ds(4 * i, 4)], in_sem.at[i]) for i in range(4)
    ]
    for copy in copies:
        copy.start()

    def spread(i, carry):
        base = pl.multiple_of(COMPS * i, 8)
        v = in_ref[i].astype(jnp.float32)
        for j in range(2):
            v_ref[j, pl.ds(base, COMPS), :] = v[COMPS * j : COMPS * (j + 1)]
        v_ref[2, pl.ds(base, 40), :] = v[2 * COMPS : 2 * COMPS + 40]
        v_ref[2, pl.ds(base + 40, 32), :] = pltpu.roll(v[2 * COMPS : 2 * COMPS + 32], 64, 1)
        return carry

    for i in range(4):
        copies[i].wait()
        lax.fori_loop(4 * i, 4 * i + 4, spread, 0, unroll=4)
    for m in range(BLOCKS * COMPS // LANES):
        for j in range(3):
            block = v_ref[j, pl.ds(LANES * m, LANES), :].T.astype(jnp.bfloat16)
            rows = min(LANES, SLOTS - LANES * j)
            out_ref[pl.ds(LANES * j, rows), pl.ds(LANES * m, LANES)] = block[:rows]


def build_tables(counts_ref, flag_ref, tabv_ref, loc_ref):
    f32, bf16, i32 = jnp.float32, jnp.bfloat16, jnp.int32
    sub = lax.broadcasted_iota(i32, (LANES, LANES), 0)
    lanes = lax.broadcasted_iota(i32, (LANES, LANES), 1)
    lane = lax.broadcasted_iota(i32, (8, LANES), 1)

    def order(i):
        return jnp.where(i < GROUPS, (i & (ROWS - 1)) * TILES + (i >> 2), i)

    def product(a, b, dims=(((1,), (0,)), ((), ()))):
        return lax.dot_general(a, b, dims, preferred_element_type=f32)

    upper = (sub <= lanes).astype(f32).astype(bf16)
    ones = jnp.ones((LANES, LANES), bf16)
    flags = flag_ref[...].astype(bf16)
    inclusive = product(flags, upper)
    count_rows = product(flags, ones)
    ends = product((order(lanes) <= order(sub)).astype(f32).astype(bf16), count_rows.astype(bf16))[:GROUPS]
    count = product(ones[:16], flags, (((1,), (1,)), ((), ())))
    first = product(count.astype(bf16), (order(sub) < order(lanes)).astype(f32).astype(bf16))
    count, first = count[:8].astype(i32), first[:8].astype(i32)

    wide = lanes[:GROUPS]
    shift = wide - (inclusive[:GROUPS].astype(i32) - 1)
    word = jnp.where(flag_ref[pl.ds(0, GROUPS), :] > 0, wide + LANES * shift + LANES * LANES, 0)
    for k in range(7):
        bit = LANES << k
        moved = pltpu.roll(word, LANES - (1 << k), 1)
        word = jnp.where((moved & bit) != 0, moved, jnp.where((word & bit) != 0, 0, word))
    word = word & (LANES - 1)
    for g in range(GROUPS):
        loc_ref[g] = jnp.broadcast_to(word[g : g + 1], (8, LANES))

    block = (lane * 171) >> 9
    part = lane - 3 * block
    size = jnp.zeros((8, LANES), i32)
    rank = jnp.zeros((8, LANES), i32)
    start = 0
    for c in range(BLOCKS):
        n = counts_ref[0, c]
        size = jnp.where(block == c, n, size)
        rank = jnp.where(block == c, start, rank)
        start = start + n
    rank = rank + LANES * part
    length = jnp.clip(size - LANES * part, 0, LANES)
    real = lane < 3 * BLOCKS

    def groups_before(r):
        hit = (ends <= r[:1].astype(f32)).astype(f32)
        return jnp.minimum(jnp.broadcast_to(jnp.sum(hit, axis=0, keepdims=True), (8, LANES)), GROUPS - 1.0)

    low = groups_before(rank)
    high = groups_before(rank + jnp.maximum(length, 1) - 1)
    width = jnp.where(real, jnp.where(length > 0, high - low + 1.0, 1.0), 0.0)
    stop = product(jnp.concatenate([width, width], axis=0).astype(bf16), upper)[:8]
    begin = stop - width
    column = jnp.sum(jnp.where(wide <= sub[:GROUPS], width[:1], 0.0), axis=1, keepdims=True)
    tile = jnp.sum((column <= wide.astype(f32)).astype(f32), axis=0, keepdims=True)
    tile = jnp.broadcast_to(jnp.minimum(tile, 3 * BLOCKS - 1.0), (8, LANES)).astype(i32)

    def at(values, index):
        return jnp.take_along_axis(values, index, axis=1)

    group = lane + at((low - begin).astype(i32), tile)
    group = jnp.clip(group, 0, GROUPS - 1)
    r = (group * 171) >> 11
    spot = ROWS * (group - TILES * r) + r
    tabv_ref[AT_SPOT : AT_SPOT + 1] = spot[:1]
    tabv_ref[AT_KEEP : AT_KEEP + 1] = (lane > at(begin.astype(i32), tile)).astype(i32)[:1]
    tabv_ref[AT_DELTA : AT_DELTA + 1] = (at(rank, tile) - at(first, spot))[:1]
    tabv_ref[AT_LEN : AT_LEN + 1] = at(length, tile)[:1]
    tabv_ref[AT_COUNT : AT_COUNT + 1] = at(count, spot)[:1]
    tabv_ref[AT_LAST : AT_LAST + 1] = jnp.clip((stop - 1.0).astype(i32), 0, STEPS - 1)[:1]
    tabv_ref[AT_LAST + 1 :] = jnp.zeros((7 - AT_LAST, LANES), i32)


def body(spectra, depth_class, group_speed, current, depth_slope, wind, land_mask, block_counts):
    cos_t, sin_t = angles()
    latitude = (-60.0 + 120.0 * (np.arange(ROWS * lax.axis_size("band")) + 0.5) / (ROWS * lax.axis_size("band"))) * (
        math.pi / 180.0
    )
    stretch = (1.0 / np.cos(latitude)).astype(np.float32)
    angular = 2.0 * math.pi * 0.0418 * np.power(1.1, np.arange(BLOCKS * FREQS, dtype=np.float64))
    ratio = angular / angular[-1]
    phase = 9.81 / angular
    coef = np.stack([GROWTH_RATE * ratio / phase, GROWTH_RATE * ratio, DAMPING * ratio]).astype(np.float32)

    scalars = np.zeros((8, LANES), np.float32)
    scalars[0, :ND], scalars[1, :ND] = cos_t, sin_t
    scalars[2:5, : BLOCKS * FREQS] = coef
    scalars[5, : stretch.size] = stretch
    compass = np.stack([np.tile(cos_t, FREQS), np.tile(sin_t, FREQS)])
    compass = np.ascontiguousarray(np.broadcast_to(compass[:, :, None], (2, COMPS, LANES)))

    vmem = pl.BlockSpec(memory_space=pltpu.VMEM)
    f32, bf16 = jnp.float32, jnp.bfloat16
    dma = pltpu.SemaphoreType.DMA
    rb = pl.pallas_call(
        step_kernel,
        out_shape=jax.ShapeDtypeStruct((BLOCKS, PACK, LANES), bf16),
        in_specs=[pl.BlockSpec(memory_space=pltpu.HBM)] * 10,
        out_specs=pl.BlockSpec(memory_space=pltpu.HBM),
        scratch_shapes=[
            pltpu.SMEM((8, LANES), f32),
            pltpu.VMEM((2, COMPS, LANES), f32),
            pltpu.SMEM(block_counts.shape, jnp.int32),
            pltpu.VMEM(spectra.shape, bf16),
            pltpu.VMEM(depth_class.shape, jnp.int32),
            pltpu.VMEM(group_speed.shape[::-1], f32),
            pltpu.VMEM(current.shape, f32),
            pltpu.VMEM(depth_slope.shape, f32),
            pltpu.VMEM(wind.shape, f32),
            pltpu.VMEM(land_mask.shape, jnp.int32),
            pltpu.VMEM((GROUPS, 8, LANES), f32),
            pltpu.VMEM((STEPS, 8, LANES), f32),
            pltpu.VMEM((8, LANES), f32),
            pltpu.VMEM((TILES, 8 * 5, LANES), f32),
            pltpu.VMEM((TILES, 8, LANES), jnp.int32),
            pltpu.VMEM((LANES, LANES), f32),
            pltpu.VMEM((8, LANES), jnp.int32),
            pltpu.SMEM((8, LANES), jnp.int32),
            pltpu.VMEM((GROUPS, 8, LANES), jnp.int32),
            pltpu.VMEM((TILES, 8 * ND, LANES), f32),
            pltpu.VMEM((TILES, 8 * (ND + 4), LANES), f32),
            pltpu.VMEM((TILES, 8 * ND, LANES), f32),
            pltpu.VMEM((STEPS, COMPS, LANES), f32),
            pltpu.VMEM((3 * BLOCKS, COMPS, LANES), f32),
            pltpu.VMEM((STEPS, 8, LANES), jnp.int32),
            pltpu.VMEM((STEPS, 8, LANES), f32),
            pltpu.VMEM((7, TILES, 8, LANES), f32),
            pltpu.VMEM((2, TILES, 4 * ND, LANES), bf16),
            pltpu.VMEM((2, TILES, 4 * ND, LANES), bf16),
            pltpu.VMEM((8, LANES), f32),
            pltpu.VMEM((CHUNKS, 16, LANES), f32),
            pltpu.VMEM((CHUNKS, 16, LANES), f32),
            pltpu.VMEM((GROUPS, 8, LANES), f32),
            pltpu.VMEM((CHUNKS, SIDE - 1, 16, LANES), f32),
            pltpu.VMEM((CHUNKS, SIDE - 1, 16, LANES), f32),
            pltpu.VMEM((BLOCKS - 1, PACK, LANES), bf16),
            pltpu.VMEM((PACK, LANES), bf16),
            dma((10,)),
            dma,
            dma,
            dma((2, CHUNKS)),
            dma((2, CHUNKS)),
            dma((2, CHUNKS, SIDE - 1)),
            dma((2, CHUNKS, SIDE - 1)),
            dma((BLOCKS - 1,)),
            dma((BLOCKS - 1,)),
        ],
        compiler_params=pltpu.CompilerParams(
            collective_id=0, has_side_effects=True, vmem_limit_bytes=58 * 1024 * 1024
        ),
        name="wave_step",
    )(
        jnp.asarray(scalars),
        jnp.asarray(compass),
        block_counts,
        spectra,
        depth_class,
        group_speed.T,
        current,
        depth_slope,
        wind,
        land_mask,
    )

    out = pl.pallas_call(
        finish_kernel,
        out_shape=jax.ShapeDtypeStruct((SLOTS, BLOCKS * COMPS), bf16),
        in_specs=[pl.BlockSpec(memory_space=pltpu.HBM)],
        out_specs=vmem,
        scratch_shapes=[
            pltpu.VMEM((BLOCKS, PACK, LANES), bf16),
            pltpu.VMEM((3, BLOCKS * COMPS, LANES), f32),
            dma((4,)),
        ],
        compiler_params=pltpu.CompilerParams(vmem_limit_bytes=58 * 1024 * 1024),
        name="finish",
    )(rb)
    return out.T


def solution(mesh):
    return jax.shard_map(
        body,
        mesh=mesh,
        in_specs=(
            P("comp", None, "band", None),
            P("band", None),
            P(),
            P(None, "band", None),
            P(None, "band", None),
            P(None, "band", None),
            P("band", None),
            P("band", None),
        ),
        out_specs=P(None, ("comp", "band")),
        check_vma=False,
    )
```

```python
import functools
import math

import jax
import jax.numpy as jnp
import numpy as np
from jax import lax
from jax.experimental import pallas as pl
from jax.experimental.pallas import tpu as pltpu
from jax.sharding import PartitionSpec as P

GROWTH_RATE = 0.05
DAMPING = 1.5
TURNING_SCALE = 0.5

FREQS = 2
LANES = 128
ND = 36
ROWS = 4
NLON = 1440
TILES = 12
GROUPS = ROWS * TILES
BLOCKS = 16
SLOTS = 315
DEPTHS = 64
STEPS = 96
COMPS = FREQS * ND
PACK = 192
CHUNKS = 3
PER = TILES // CHUNKS
RUN = 6
SIDE = 4

AT_SPOT, AT_KEEP, AT_DELTA, AT_LEN, AT_COUNT, AT_LAST = range(6)

(F_SEA, F_CX, F_CY, F_CUR0, F_CUR1, F_T0, F_T1) = range(7)

MESH = pl.DeviceIdType.MESH


def angles():
    heading = (np.arange(ND, dtype=np.float32) * np.float32(2.0 * math.pi / ND)).astype(np.float64)
    return (np.cos(heading).astype(np.float32), np.sin(heading).astype(np.float32))


def upwind12(far_behind, behind, centre, ahead, far_ahead, speed):
    forward = speed > 0
    down = jnp.where(forward, ahead, behind)
    up = jnp.where(forward, behind, ahead)
    far = jnp.where(forward, far_behind, far_ahead)
    return jnp.abs(speed) * ((2.0 * down + far) + (3.0 * centre - 6.0 * up))


OFFSETS = sorted(
    [(a, b) for a in range(SIDE) for b in range(SIDE) if a or b],
    key=lambda o: -(min(o[0], SIDE - o[0]) + min(o[1], SIDE - o[1])),
)


def step_kernel(
    scalars_hbm, compass_hbm, counts_hbm, spec_hbm, depth_hbm, speed_hbm, current_hbm, slope_hbm, wind_hbm, land_hbm,
    rb_ref,
    scalars_ref, compass_ref, counts_ref, spec_ref, depth_ref, speed_ref, current_ref, slope_ref, wind_ref, land_ref,
    gust_ref, gusts_ref,
    gs_ref, raw_ref, cls_ref, flag_ref, tabv_ref, tab_ref, loc_ref, x_ref, adv_ref, t_ref, stage_ref, grown_ref, idx_ref, dec_ref, fl_ref, hs_ref, hr_ref, sq_ref, part_ref, total_ref, level_ref, yr_ref, zr_ref, sb_ref, own_ref,
    in_sem, tab_sem, own_sem, halo_send, halo_recv, sum_send, sum_recv, send_sem, recv_sem,
):
    arrivals = [
        pltpu.make_async_copy(src, dst, in_sem.at[i])
        for i, (src, dst) in enumerate(
            [
                (land_hbm, land_ref),
                (spec_hbm, spec_ref),
                (scalars_hbm, scalars_ref),
                (speed_hbm, speed_ref),
                (depth_hbm, depth_ref),
                (current_hbm, current_ref),
                (slope_hbm, slope_ref),
                (wind_hbm, wind_ref),
                (counts_hbm, counts_ref),
                (compass_hbm, compass_ref),
            ]
        )
    ]
    for copy in arrivals:
        copy.start()
    lane = lax.broadcasted_iota(jnp.int32, (8, LANES), 1)
    sub = lax.broadcasted_iota(jnp.int32, (8, LANES), 0)
    row = sub // 2
    tail = NLON - (TILES - 1) * LANES
    me = lax.axis_index("comp")
    band = lax.axis_index("band")
    bands = lax.axis_size("band")
    z, y = me // SIDE, lax.rem(me, SIDE)
    north = lax.rem(band + 1, bands)
    south = lax.rem(band + bands - 1, bands)

    def peer(o):
        return lax.rem(z + o[0], SIDE) * SIDE + lax.rem(y + o[1], SIDE)

    barrier = pltpu.get_barrier_semaphore()
    for b in (north, south):
        pl.semaphore_signal(barrier, inc=1, device_id={"band": b}, device_id_type=MESH)
    for o in OFFSETS:
        pl.semaphore_signal(barrier, inc=1, device_id={"comp": peer(o)}, device_id_type=MESH)

    for copy in arrivals:
        copy.wait()

    even_half = lax.rem(lax.broadcasted_iota(jnp.int32, (8, DEPTHS), 0), 2) == 0
    gs_ref[:, pl.ds(0, DEPTHS)] = jnp.where(
        even_half,
        jnp.broadcast_to(speed_ref[pl.ds(FREQS * me, 1), :], (8, DEPTHS)),
        jnp.broadcast_to(speed_ref[pl.ds(FREQS * me + 1, 1), :], (8, DEPTHS)),
    )
    stretch = jnp.where(row == 0, scalars_ref[5, ROWS * band], scalars_ref[5, ROWS * band + 1])
    stretch = jnp.where(row == 2, scalars_ref[5, ROWS * band + 2], stretch)
    stretch = jnp.where(row == 3, scalars_ref[5, ROWS * band + 3], stretch)
    flag_ref[...] = jnp.zeros((LANES, LANES), jnp.float32)
    for j in range(TILES):
        width = LANES if j < TILES - 1 else tail
        cols = pl.ds(j * LANES, width)
        sea = (land_ref[:, cols] == 0).astype(jnp.float32)
        flag_ref[pl.ds(ROWS * j, ROWS), pl.ds(0, width)] = sea
        for i in range(2):
            gust = wind_ref[i, :, cols]
            for r in range(ROWS):
                gust_ref[ROWS * j + r, i : i + 1, pl.ds(0, width)] = gust[r : r + 1]
        parts = [sea] + [ref[i, :, cols] for ref in (current_ref, slope_ref) for i in range(2)]
        for n, v in enumerate(parts):
            for f in range(FREQS):
                raw_ref[j, pl.ds(8 * n + f, 4, stride=2), pl.ds(0, width)] = v
        v = depth_ref[:, cols]
        for f in range(FREQS):
            cls_ref[j, pl.ds(f, 4, stride=2), pl.ds(0, width)] = v
    for j in range(TILES):
        def raw(n):
            v = raw_ref[j, pl.ds(8 * n, 8), :]
            return v if j < TILES - 1 else jnp.where(lane < tail, v, 0.0)

        cls = cls_ref[j]
        if j == TILES - 1:
            cls = jnp.where(lane < tail, cls, 0)
        cel = jnp.take_along_axis(gs_ref[...], cls, axis=1)
        sea = raw(0)
        sixth = cel * (sea * (1.0 / 6.0))
        fl_ref[F_SEA, j] = sea
        fl_ref[F_CX, j] = sixth * stretch
        fl_ref[F_CY, j] = sixth
        fl_ref[F_CUR0, j] = raw(1) * (sea * (1.0 / 6.0))
        fl_ref[F_CUR1, j] = raw(2) * (sea * (1.0 / 6.0))
        fl_ref[F_T0, j] = (TURNING_SCALE * sixth) * raw(3)
        fl_ref[F_T1, j] = (TURNING_SCALE * sixth) * raw(4)

    def load(d, carry):
        base = pl.multiple_of(8 * d, 8)
        for j in range(TILES):
            width = LANES if j < TILES - 1 else tail
            for f in range(FREQS):
                v = spec_ref[f, d, :, pl.ds(j * LANES, width)].astype(jnp.float32)
                x_ref[j, pl.ds(base + f, 4, stride=2), pl.ds(0, width)] = v
        return carry

    lax.fori_loop(0, ND, load, 0)

    def prepare(c, q, carry):
        base = pl.multiple_of(32 * q, 32)
        for j in range(PER * c, PER * c + PER):
            v = [x_ref[j, pl.ds(base + 8 * i, 8), :] for i in range(4)]
            if j == TILES - 1:
                v = [jnp.where(lane < tail, w, 0.0) for w in v]
            v = [w * fl_ref[F_SEA, j] for w in v]
            if j == TILES - 1:
                first = [x_ref[0, pl.ds(base + 8 * i, 8), :] for i in range(4)]
                v = [
                    jnp.where(
                        lane < tail,
                        w,
                        jnp.where(lane < tail + 2, pltpu.roll(a, tail, 1), pltpu.roll(w, LANES - tail, 1)),
                    )
                    for w, a in zip(v, first)
                ]
            for i in range(4):
                x_ref[j, pl.ds(base + 8 * i, 8), :] = v[i]
            turned = [pltpu.roll(w, 4, 0) for w in v]
            low = [jnp.where(sub < 4, v[i], turned[i + 1]) for i in (0, 2)]
            high = [jnp.where(sub < 4, turned[i], v[i + 1]) for i in (0, 2)]
            rows = pl.ds(pl.multiple_of(16 * q, 16), 16)
            hs_ref[0, j, rows, :] = jnp.concatenate(low, axis=0).astype(jnp.bfloat16)
            hs_ref[1, j, rows, :] = jnp.concatenate(high, axis=0).astype(jnp.bfloat16)
        return carry

    halos = []

    def send_halos(c):
        for side, b in ((0, south), (1, north)):
            copy = pltpu.make_async_remote_copy(
                src_ref=hs_ref.at[side, pl.ds(PER * c, PER)],
                dst_ref=hr_ref.at[side, pl.ds(PER * c, PER)],
                send_sem=halo_send.at[side, c],
                recv_sem=halo_recv.at[side, c],
                device_id={"band": b},
                device_id_type=MESH,
            )
            copy.start()
            halos.append(copy)

    for c in range(CHUNKS):
        lax.fori_loop(0, ND // 4, functools.partial(prepare, c), 0, unroll=3)
        if c == 0:
            pl.semaphore_wait(barrier, len(OFFSETS) + 2)
        send_halos(c)

    build_tables(counts_ref, flag_ref, tabv_ref, loc_ref)
    table_copy = pltpu.make_async_copy(tabv_ref, tab_ref, tab_sem)
    table_copy.start()

    def along(d, carry):
        base = pl.multiple_of(8 * d, 8)
        cos_d = scalars_ref[0, d]
        x = [x_ref[j, pl.ds(base, 8), :] for j in range(TILES)]
        r1 = [pltpu.roll(v, 1, 1) for v in x]
        r2 = [pltpu.roll(v, 2, 1) for v in x]
        l1 = [pltpu.roll(v, LANES - 1, 1) for v in x]
        l2 = [pltpu.roll(v, LANES - 2, 1) for v in x]
        for j in range(TILES):
            before, after = (j - 1) % TILES, (j + 1) % TILES
            behind = jnp.where(lane < 1, r1[before], r1[j])
            far_behind = jnp.where(lane < 2, r2[before], r2[j])
            ahead = jnp.where(lane >= LANES - 1, l1[after], l1[j])
            far_ahead = jnp.where(lane >= LANES - 2, l2[after], l2[j])
            speed = fl_ref[F_CX, j] * cos_d + fl_ref[F_CUR0, j]
            out = x[j] - upwind12(far_behind, behind, x[j], ahead, far_ahead, speed)
            adv_ref[j, pl.ds(base + 16, 8), :] = out
        return carry

    lax.fori_loop(0, ND, along, 0, unroll=4)

    keep_dn = (band < bands - 1).astype(jnp.float32)
    keep_up = (band > 0).astype(jnp.float32)
    zero = jnp.zeros((8, LANES), jnp.float32)

    def reduce_start(axis, c, src, dst):
        copies = []
        for i in range(1, SIDE):
            o = (0, i) if axis == 0 else (i, 0)
            copy = pltpu.make_async_remote_copy(
                src_ref=src.at[c],
                dst_ref=dst.at[c, i - 1],
                send_sem=sum_send.at[axis, c, i - 1],
                recv_sem=sum_recv.at[axis, c, i - 1],
                device_id={"comp": peer(o)},
                device_id_type=MESH,
            )
            copy.start()
            copies.append(copy)
        return copies

    sums_y, sums_z = [], []

    def pass_on(c):
        for copy in sums_y[c]:
            copy.wait()
        total_ref[c] = (part_ref[c] + yr_ref[c, 0]) + (yr_ref[c, 1] + yr_ref[c, 2])
        sums_z.append(reduce_start(1, c, total_ref, zr_ref))

    part_ref[...] = jnp.zeros((CHUNKS, 16, LANES), jnp.float32)

    for c in range(CHUNKS):
        halos[2 * c].wait_recv()
        halos[2 * c + 1].wait_recv()

        def across(q, carry):
            rows = pl.ds(pl.multiple_of(16 * q, 16), 16)
            base = pl.multiple_of(32 * q, 32)
            for j in range(PER * c, PER * c + PER):
                dn = hr_ref[0, j, rows, :].astype(jnp.float32) * keep_dn
                up = hr_ref[1, j, rows, :].astype(jnp.float32) * keep_up
                for i in range(4):
                    a, b = dn[8 * (i // 2) : 8 * (i // 2) + 8], up[8 * (i // 2) : 8 * (i // 2) + 8]
                    if i % 2 == 0:
                        h = jnp.where(sub < 4, a, pltpu.roll(b, 4, 0))
                    else:
                        h = jnp.where(sub < 4, pltpu.roll(a, 4, 0), b)
                    here = pl.ds(base + 8 * i, 8)
                    v = x_ref[j, here, :]
                    ahead = pltpu.roll(jnp.where(row == 0, h, v), 6, 0)
                    far_ahead = pltpu.roll(jnp.where(row < 2, h, v), 4, 0)
                    far_behind = pltpu.roll(jnp.where(row < 2, v, h), 4, 0)
                    behind = pltpu.roll(jnp.where(row == 3, h, v), 2, 0)
                    speed = fl_ref[F_CY, j] * scalars_ref[1, 4 * q + i] + fl_ref[F_CUR1, j]
                    flux = upwind12(far_behind, behind, v, ahead, far_ahead, speed)
                    there = pl.ds(base + (8 * i + 16), 8)
                    adv_ref[j, there, :] = adv_ref[j, there, :] - flux
            return carry

        lax.fori_loop(0, ND // 4, across, 0)

        for j in range(PER * c, PER * c + PER):
            adv_ref[j, pl.ds(0, 16), :] = adv_ref[j, pl.ds(8 * ND, 16), :]
            adv_ref[j, pl.ds(8 * ND + 16, 16), :] = adv_ref[j, pl.ds(16, 16), :]

        def refract(q, sums):
            base = pl.multiple_of(8 * RUN * q, 8)
            sums = list(sums)
            for j in range(PER * c, PER * c + PER):
                near = [adv_ref[j, pl.ds(base + 8 * i, 8), :] for i in range(RUN + 4)]
                t0, t1 = fl_ref[F_T0, j], fl_ref[F_T1, j]
                for i in range(RUN):
                    d = RUN * q + i
                    speed = t0 * scalars_ref[1, d] - t1 * scalars_ref[0, d]
                    out = near[i + 2] - upwind12(*near[i : i + 5], speed)
                    sums[j - PER * c] = sums[j - PER * c] + out * out
                    t_ref[j, pl.ds(d, 8, stride=ND), :] = out
            return tuple(sums)

        sums = lax.fori_loop(0, ND // RUN, refract, (zero,) * PER)
        for i in range(PER):
            j = PER * c + i
            sq_ref[...] = sums[i] + pltpu.roll(sums[i], 7, 0)
            part_ref[c, pl.ds(4 * i, 4), :] = sq_ref[pl.ds(0, 4, stride=2), :]
        sums_y.append(reduce_start(0, c, part_ref, yr_ref))
        if c >= 2:
            pass_on(c - 2)

    t_rows = t_ref.reshape(GROUPS, COMPS, LANES)

    def step(k, carry):
        keep = tab_ref[AT_KEEP, k].astype(jnp.float32)
        spot = tab_ref[AT_SPOT, k]
        local = lane + tab_ref[AT_DELTA, k]
        valid = (lane < tab_ref[AT_LEN, k]) & (local >= 0) & (local < tab_ref[AT_COUNT, k])
        local = jnp.clip(local, 0, LANES - 1)
        idx = jnp.take_along_axis(loc_ref[spot], local, axis=1)
        idx_ref[k] = jnp.where(valid, idx, -1)
        parts = []
        for m in range(COMPS // 8):
            data = t_rows[spot, pl.ds(8 * m, 8), :]
            got = jnp.take_along_axis(data, idx, axis=1)
            part = jnp.where(valid, got, carry[m] * keep)
            stage_ref[k, pl.ds(8 * m, 8), :] = part
            parts.append(part)
        gust = jnp.where(valid, jnp.take_along_axis(gust_ref[spot], idx, axis=1), carry[COMPS // 8])
        gusts_ref[k] = gust
        return tuple(parts) + (gust,)

    table_copy.wait()
    carry = lax.fori_loop(0, STEPS // 2, step, (zero,) * (COMPS // 8 + 1), unroll=8)
    pass_on(CHUNKS - 2)
    pass_on(CHUNKS - 1)
    lax.fori_loop(STEPS // 2, STEPS, step, carry, unroll=8)

    def by_row(q):
        low, high = scalars_ref[q, FREQS * me], scalars_ref[q, FREQS * me + 1]
        mixed = jnp.where(sub < 4, low, high)
        return [low if m < 4 else (mixed if m == 4 else high) for m in range(COMPS // 8)]

    rise, calm = by_row(2), by_row(3)
    for i in range(2):
        for m in range(COMPS // 8):
            rows = pl.ds(8 * m, 8)
            compass_ref[i, rows, :] = compass_ref[i, rows, :] * rise[m]

    def grow(c, carry):
        for j in range(3):
            k = tab_ref[AT_LAST, 3 * c + j]
            gust = gusts_ref[k]
            east = jnp.broadcast_to(gust[0:1], (8, LANES))
            north = jnp.broadcast_to(gust[1:2], (8, LANES))
            for m in range(COMPS // 8):
                rows = pl.ds(8 * m, 8)
                push = east * compass_ref[0, rows, :] + north * compass_ref[1, rows, :]
                grown_ref[3 * c + j, rows, :] = stage_ref[k, rows, :] * jnp.exp(jnp.maximum(push - calm[m], 0.0))
        return carry

    lax.fori_loop(0, BLOCKS, grow, 0, unroll=2)
    for c in range(CHUNKS):
        for copy in sums_z[c]:
            copy.wait()
        total = (total_ref[c] + zr_ref[c, 0]) + (zr_ref[c, 1] + zr_ref[c, 2])
        total = jnp.sqrt(total * (1.0 / (BLOCKS * COMPS)) + 1e-6)
        for i in range(ROWS * PER):
            level_ref[ROWS * PER * c + i] = jnp.broadcast_to(total[i : i + 1], (8, LANES))

    def strengths(k, acc):
        keep = tab_ref[AT_KEEP, k].astype(jnp.float32)
        idx = idx_ref[k]
        got = jnp.take_along_axis(level_ref[tab_ref[AT_SPOT, k]], jnp.maximum(idx, 0), axis=1)
        acc = jnp.where(idx >= 0, got, acc * keep)
        dec_ref[k] = acc
        return acc

    lax.fori_loop(0, STEPS, strengths, zero, unroll=32)

    fade0 = scalars_ref[4, FREQS * me]
    fade1 = scalars_ref[4, FREQS * me + 1]

    def block(c, store):
        places = [tab_ref[AT_LAST, 3 * c + j] for j in range(3)]
        rows = []
        for j in range(3):
            s = dec_ref[places[j]]
            e0 = jnp.exp(-fade0 * s)
            e1 = jnp.exp(-fade1 * s)
            mixed = jnp.where(sub < 4, e0, e1)
            values = []
            for m in range(COMPS // 8):
                e = e0 if m < 4 else (mixed if m == 4 else e1)
                values.append(grown_ref[3 * c + j, pl.ds(8 * m, 8), :] * e)
            if j < 2:
                rows += values
            else:
                for m in range(5):
                    v = values[m]
                    if m < 4:
                        v = jnp.where(lane < 64, v, pltpu.roll(values[5 + m], 64, 1))
                    rows.append(v)
                rows.append(zero)
        for m in range(PACK // 16):
            store(m, jnp.concatenate(rows[2 * m : 2 * m + 2], axis=0).astype(jnp.bfloat16))

    copies = []
    for i, o in enumerate(OFFSETS):
        other = peer(o)

        def put(m, v):
            sb_ref[i, pl.ds(16 * m, 16), :] = v

        block(other, put)
        copy = pltpu.make_async_remote_copy(
            src_ref=sb_ref.at[i],
            dst_ref=rb_ref.at[me],
            send_sem=send_sem.at[i],
            recv_sem=recv_sem.at[i],
            device_id={"comp": other},
            device_id_type=MESH,
        )
        copy.start()
        copies.append(copy)

    def put_own(m, v):
        own_ref[pl.ds(16 * m, 16), :] = v

    block(me, put_own)
    own_copy = pltpu.make_async_copy(own_ref, rb_ref.at[me], own_sem)
    own_copy.start()
    own_copy.wait()
    for copy in halos:
        copy.wait_send()
    for copy in copies:
        copy.wait()


def finish_kernel(rb_ref, out_ref, in_ref, v_ref, in_sem):
    copies = [
        pltpu.make_async_copy(rb_ref.at[pl.ds(4 * i, 4)], in_ref.at[pl.ds(4 * i, 4)], in_sem.at[i]) for i in range(4)
    ]
    for copy in copies:
        copy.start()

    def spread(i, carry):
        base = pl.multiple_of(COMPS * i, 8)
        v = in_ref[i].astype(jnp.float32)
        for j in range(2):
            v_ref[j, pl.ds(base, COMPS), :] = v[COMPS * j : COMPS * (j + 1)]
        v_ref[2, pl.ds(base, 40), :] = v[2 * COMPS : 2 * COMPS + 40]
        v_ref[2, pl.ds(base + 40, 32), :] = pltpu.roll(v[2 * COMPS : 2 * COMPS + 32], 64, 1)
        return carry

    for i in range(4):
        copies[i].wait()
        lax.fori_loop(4 * i, 4 * i + 4, spread, 0, unroll=4)
    for m in range(BLOCKS * COMPS // LANES):
        for j in range(3):
            block = v_ref[j, pl.ds(LANES * m, LANES), :].T.astype(jnp.bfloat16)
            rows = min(LANES, SLOTS - LANES * j)
            out_ref[pl.ds(LANES * j, rows), pl.ds(LANES * m, LANES)] = block[:rows]


def build_tables(counts_ref, flag_ref, tabv_ref, loc_ref):
    f32, bf16, i32 = jnp.float32, jnp.bfloat16, jnp.int32
    sub = lax.broadcasted_iota(i32, (LANES, LANES), 0)
    lanes = lax.broadcasted_iota(i32, (LANES, LANES), 1)
    lane = lax.broadcasted_iota(i32, (8, LANES), 1)

    def order(i):
        return jnp.where(i < GROUPS, (i & (ROWS - 1)) * TILES + (i >> 2), i)

    def product(a, b, dims=(((1,), (0,)), ((), ()))):
        return lax.dot_general(a, b, dims, preferred_element_type=f32)

    upper = (sub <= lanes).astype(f32).astype(bf16)
    ones = jnp.ones((LANES, LANES), bf16)
    flags = flag_ref[...].astype(bf16)
    inclusive = product(flags, upper)
    count_rows = product(flags, ones)
    ends = product((order(lanes) <= order(sub)).astype(f32).astype(bf16), count_rows.astype(bf16))[:GROUPS]
    count = product(ones[:16], flags, (((1,), (1,)), ((), ())))
    first = product(count.astype(bf16), (order(sub) < order(lanes)).astype(f32).astype(bf16))
    count, first = count[:8].astype(i32), first[:8].astype(i32)

    wide = lanes[:GROUPS]
    shift = wide - (inclusive[:GROUPS].astype(i32) - 1)
    word = jnp.where(flag_ref[pl.ds(0, GROUPS), :] > 0, wide + LANES * shift + LANES * LANES, 0)
    for k in range(7):
        bit = LANES << k
        moved = pltpu.roll(word, LANES - (1 << k), 1)
        word = jnp.where((moved & bit) != 0, moved, jnp.where((word & bit) != 0, 0, word))
    word = word & (LANES - 1)
    for g in range(GROUPS):
        loc_ref[g] = jnp.broadcast_to(word[g : g + 1], (8, LANES))

    block = (lane * 171) >> 9
    part = lane - 3 * block
    size = jnp.zeros((8, LANES), i32)
    rank = jnp.zeros((8, LANES), i32)
    start = 0
    for c in range(BLOCKS):
        n = counts_ref[0, c]
        size = jnp.where(block == c, n, size)
        rank = jnp.where(block == c, start, rank)
        start = start + n
    rank = rank + LANES * part
    length = jnp.clip(size - LANES * part, 0, LANES)
    real = lane < 3 * BLOCKS

    def groups_before(r):
        hit = (ends <= r[:1].astype(f32)).astype(f32)
        return jnp.minimum(jnp.broadcast_to(jnp.sum(hit, axis=0, keepdims=True), (8, LANES)), GROUPS - 1.0)

    low = groups_before(rank)
    high = groups_before(rank + jnp.maximum(length, 1) - 1)
    width = jnp.where(real, jnp.where(length > 0, high - low + 1.0, 1.0), 0.0)
    stop = product(jnp.concatenate([width, width], axis=0).astype(bf16), upper)[:8]
    begin = stop - width
    column = jnp.sum(jnp.where(wide <= sub[:GROUPS], width[:1], 0.0), axis=1, keepdims=True)
    tile = jnp.sum((column <= wide.astype(f32)).astype(f32), axis=0, keepdims=True)
    tile = jnp.broadcast_to(jnp.minimum(tile, 3 * BLOCKS - 1.0), (8, LANES)).astype(i32)

    def at(values, index):
        return jnp.take_along_axis(values, index, axis=1)

    group = lane + at((low - begin).astype(i32), tile)
    group = jnp.clip(group, 0, GROUPS - 1)
    r = (group * 171) >> 11
    spot = ROWS * (group - TILES * r) + r
    tabv_ref[AT_SPOT : AT_SPOT + 1] = spot[:1]
    tabv_ref[AT_KEEP : AT_KEEP + 1] = (lane > at(begin.astype(i32), tile)).astype(i32)[:1]
    tabv_ref[AT_DELTA : AT_DELTA + 1] = (at(rank, tile) - at(first, spot))[:1]
    tabv_ref[AT_LEN : AT_LEN + 1] = at(length, tile)[:1]
    tabv_ref[AT_COUNT : AT_COUNT + 1] = at(count, spot)[:1]
    tabv_ref[AT_LAST : AT_LAST + 1] = jnp.clip((stop - 1.0).astype(i32), 0, STEPS - 1)[:1]
    tabv_ref[AT_LAST + 1 :] = jnp.zeros((7 - AT_LAST, LANES), i32)


def body(spectra, depth_class, group_speed, current, depth_slope, wind, land_mask, block_counts):
    cos_t, sin_t = angles()
    latitude = (-60.0 + 120.0 * (np.arange(ROWS * lax.axis_size("band")) + 0.5) / (ROWS * lax.axis_size("band"))) * (
        math.pi / 180.0
    )
    stretch = (1.0 / np.cos(latitude)).astype(np.float32)
    angular = 2.0 * math.pi * 0.0418 * np.power(1.1, np.arange(BLOCKS * FREQS, dtype=np.float64))
    ratio = angular / angular[-1]
    phase = 9.81 / angular
    coef = np.stack([GROWTH_RATE * ratio / phase, GROWTH_RATE * ratio, DAMPING * ratio]).astype(np.float32)

    scalars = np.zeros((8, LANES), np.float32)
    scalars[0, :ND], scalars[1, :ND] = cos_t, sin_t
    scalars[2:5, : BLOCKS * FREQS] = coef
    scalars[5, : stretch.size] = stretch
    compass = np.stack([np.tile(cos_t, FREQS), np.tile(sin_t, FREQS)])
    compass = np.ascontiguousarray(np.broadcast_to(compass[:, :, None], (2, COMPS, LANES)))

    vmem = pl.BlockSpec(memory_space=pltpu.VMEM)
    f32, bf16 = jnp.float32, jnp.bfloat16
    dma = pltpu.SemaphoreType.DMA
    rb = pl.pallas_call(
        step_kernel,
        out_shape=jax.ShapeDtypeStruct((BLOCKS, PACK, LANES), bf16),
        in_specs=[pl.BlockSpec(memory_space=pltpu.HBM)] * 10,
        out_specs=pl.BlockSpec(memory_space=pltpu.HBM),
        scratch_shapes=[
            pltpu.SMEM((8, LANES), f32),
            pltpu.VMEM((2, COMPS, LANES), f32),
            pltpu.SMEM(block_counts.shape, jnp.int32),
            pltpu.VMEM(spectra.shape, bf16),
            pltpu.VMEM(depth_class.shape, jnp.int32),
            pltpu.VMEM(group_speed.shape[::-1], f32),
            pltpu.VMEM(current.shape, f32),
            pltpu.VMEM(depth_slope.shape, f32),
            pltpu.VMEM(wind.shape, f32),
            pltpu.VMEM(land_mask.shape, jnp.int32),
            pltpu.VMEM((GROUPS, 8, LANES), f32),
            pltpu.VMEM((STEPS, 8, LANES), f32),
            pltpu.VMEM((8, LANES), f32),
            pltpu.VMEM((TILES, 8 * 5, LANES), f32),
            pltpu.VMEM((TILES, 8, LANES), jnp.int32),
            pltpu.VMEM((LANES, LANES), f32),
            pltpu.VMEM((8, LANES), jnp.int32),
            pltpu.SMEM((8, LANES), jnp.int32),
            pltpu.VMEM((GROUPS, 8, LANES), jnp.int32),
            pltpu.VMEM((TILES, 8 * ND, LANES), f32),
            pltpu.VMEM((TILES, 8 * (ND + 4), LANES), f32),
            pltpu.VMEM((TILES, 8 * ND, LANES), f32),
            pltpu.VMEM((STEPS, COMPS, LANES), f32),
            pltpu.VMEM((3 * BLOCKS, COMPS, LANES), f32),
            pltpu.VMEM((STEPS, 8, LANES), jnp.int32),
            pltpu.VMEM((STEPS, 8, LANES), f32),
            pltpu.VMEM((7, TILES, 8, LANES), f32),
            pltpu.VMEM((2, TILES, 4 * ND, LANES), bf16),
            pltpu.VMEM((2, TILES, 4 * ND, LANES), bf16),
            pltpu.VMEM((8, LANES), f32),
            pltpu.VMEM((CHUNKS, 16, LANES), f32),
            pltpu.VMEM((CHUNKS, 16, LANES), f32),
            pltpu.VMEM((GROUPS, 8, LANES), f32),
            pltpu.VMEM((CHUNKS, SIDE - 1, 16, LANES), f32),
            pltpu.VMEM((CHUNKS, SIDE - 1, 16, LANES), f32),
            pltpu.VMEM((BLOCKS - 1, PACK, LANES), bf16),
            pltpu.VMEM((PACK, LANES), bf16),
            dma((10,)),
            dma,
            dma,
            dma((2, CHUNKS)),
            dma((2, CHUNKS)),
            dma((2, CHUNKS, SIDE - 1)),
            dma((2, CHUNKS, SIDE - 1)),
            dma((BLOCKS - 1,)),
            dma((BLOCKS - 1,)),
        ],
        compiler_params=pltpu.CompilerParams(
            collective_id=0, has_side_effects=True, vmem_limit_bytes=58 * 1024 * 1024
        ),
        name="wave_step",
    )(
        jnp.asarray(scalars),
        jnp.asarray(compass),
        block_counts,
        spectra,
        depth_class,
        group_speed.T,
        current,
        depth_slope,
        wind,
        land_mask,
    )

    out = pl.pallas_call(
        finish_kernel,
        out_shape=jax.ShapeDtypeStruct((SLOTS, BLOCKS * COMPS), bf16),
        in_specs=[pl.BlockSpec(memory_space=pltpu.HBM)],
        out_specs=vmem,
        scratch_shapes=[
            pltpu.VMEM((BLOCKS, PACK, LANES), bf16),
            pltpu.VMEM((3, BLOCKS * COMPS, LANES), f32),
            dma((4,)),
        ],
        compiler_params=pltpu.CompilerParams(vmem_limit_bytes=58 * 1024 * 1024),
        name="finish",
    )(rb)
    return out.T


def solution(mesh):
    return jax.shard_map(
        body,
        mesh=mesh,
        in_specs=(
            P("comp", None, "band", None),
            P("band", None),
            P(),
            P(None, "band", None),
            P(None, "band", None),
            P(None, "band", None),
            P("band", None),
            P("band", None),
        ),
        out_specs=P(None, ("comp", "band")),
        check_vma=False,
    )
```

```python
import math

import jax
import jax.numpy as jnp
import numpy as np
from jax import lax
from jax.experimental import pallas as pl
from jax.experimental.pallas import tpu as pltpu
from jax.sharding import PartitionSpec as P

GROWTH_RATE = 0.05
DAMPING = 1.5
TURNING_SCALE = 0.5

FREQS = 2
LANES = 128
ND = 36
ROWS = 4
NLON = 1440
TILES = 12
GROUPS = ROWS * TILES
BLOCKS = 16
SLOTS = 315
DEPTHS = 64
STEPS = 96
COMPS = FREQS * ND
PACK = 192
CHUNKS = 3
PER = TILES // CHUNKS
RUN = 6
SIDE = 4

AT_SPOT, AT_KEEP, AT_DELTA, AT_LEN, AT_COUNT, AT_LAST = range(6)

(F_SEA, F_CX, F_CY, F_CUR0, F_CUR1, F_T0, F_T1) = range(7)

MESH = pl.DeviceIdType.MESH


def angles():
    heading = (np.arange(ND, dtype=np.float32) * np.float32(2.0 * math.pi / ND)).astype(np.float64)
    return (np.cos(heading).astype(np.float32), np.sin(heading).astype(np.float32))


def upwind12(far_behind, behind, centre, ahead, far_ahead, speed):
    forward = speed > 0
    down = jnp.where(forward, ahead, behind)
    up = jnp.where(forward, behind, ahead)
    far = jnp.where(forward, far_behind, far_ahead)
    return jnp.abs(speed) * ((2.0 * down + far) + (3.0 * centre - 6.0 * up))


OFFSETS = sorted(
    [(a, b) for a in range(SIDE) for b in range(SIDE) if a or b],
    key=lambda o: -(min(o[0], SIDE - o[0]) + min(o[1], SIDE - o[1])),
)


def step_kernel(
    scalars_hbm, compass_hbm, counts_hbm, spec_hbm, depth_hbm, speed_hbm, current_hbm, slope_hbm, wind_hbm, land_hbm,
    rb_ref,
    scalars_ref, compass_ref, counts_ref, spec_ref, depth_ref, speed_ref, current_ref, slope_ref, wind_ref, land_ref,
    gust_ref, gusts_ref,
    gs_ref, raw_ref, cls_ref, flag_ref, tabv_ref, tab_ref, loc_ref, x_ref, adv_ref, t_ref, stage_ref, grown_ref, idx_ref, dec_ref, fl_ref, hs_ref, hr_ref, sq_ref, part_ref, total_ref, level_ref, yr_ref, zr_ref, sb_ref, own_ref,
    in_sem, tab_sem, own_sem, halo_send, halo_recv, sum_send, sum_recv, send_sem, recv_sem,
):
    arrivals = [
        pltpu.make_async_copy(src, dst, in_sem.at[i])
        for i, (src, dst) in enumerate(
            [
                (land_hbm, land_ref),
                (spec_hbm, spec_ref),
                (scalars_hbm, scalars_ref),
                (speed_hbm, speed_ref),
                (depth_hbm, depth_ref),
                (current_hbm, current_ref),
                (slope_hbm, slope_ref),
                (wind_hbm, wind_ref),
                (counts_hbm, counts_ref),
                (compass_hbm, compass_ref),
            ]
        )
    ]
    for copy in arrivals:
        copy.start()
    lane = lax.broadcasted_iota(jnp.int32, (8, LANES), 1)
    sub = lax.broadcasted_iota(jnp.int32, (8, LANES), 0)
    row = sub // 2
    tail = NLON - (TILES - 1) * LANES
    me = lax.axis_index("comp")
    band = lax.axis_index("band")
    bands = lax.axis_size("band")
    z, y = me // SIDE, lax.rem(me, SIDE)
    north = lax.rem(band + 1, bands)
    south = lax.rem(band + bands - 1, bands)

    def peer(o):
        return lax.rem(z + o[0], SIDE) * SIDE + lax.rem(y + o[1], SIDE)

    barrier = pltpu.get_barrier_semaphore()
    for b in (north, south):
        pl.semaphore_signal(barrier, inc=1, device_id={"band": b}, device_id_type=MESH)
    for o in OFFSETS:
        pl.semaphore_signal(barrier, inc=1, device_id={"comp": peer(o)}, device_id_type=MESH)

    for copy in arrivals:
        copy.wait()

    even_half = lax.rem(lax.broadcasted_iota(jnp.int32, (8, DEPTHS), 0), 2) == 0
    gs_ref[:, pl.ds(0, DEPTHS)] = jnp.where(
        even_half,
        jnp.broadcast_to(speed_ref[pl.ds(FREQS * me, 1), :], (8, DEPTHS)),
        jnp.broadcast_to(speed_ref[pl.ds(FREQS * me + 1, 1), :], (8, DEPTHS)),
    )
    stretch = jnp.where(row == 0, scalars_ref[5, ROWS * band], scalars_ref[5, ROWS * band + 1])
    stretch = jnp.where(row == 2, scalars_ref[5, ROWS * band + 2], stretch)
    stretch = jnp.where(row == 3, scalars_ref[5, ROWS * band + 3], stretch)
    flag_ref[...] = jnp.zeros((LANES, LANES), jnp.float32)
    for j in range(TILES):
        width = LANES if j < TILES - 1 else tail
        cols = pl.ds(j * LANES, width)
        sea = (land_ref[:, cols] == 0).astype(jnp.float32)
        flag_ref[pl.ds(ROWS * j, ROWS), pl.ds(0, width)] = sea
        for i in range(2):
            gust = wind_ref[i, :, cols]
            for r in range(ROWS):
                gust_ref[ROWS * j + r, i : i + 1, pl.ds(0, width)] = gust[r : r + 1]
        parts = [sea] + [ref[i, :, cols] for ref in (current_ref, slope_ref) for i in range(2)]
        for n, v in enumerate(parts):
            for f in range(FREQS):
                raw_ref[j, pl.ds(8 * n + f, 4, stride=2), pl.ds(0, width)] = v
        v = depth_ref[:, cols]
        for f in range(FREQS):
            cls_ref[j, pl.ds(f, 4, stride=2), pl.ds(0, width)] = v
    for j in range(TILES):
        def raw(n):
            v = raw_ref[j, pl.ds(8 * n, 8), :]
            return v if j < TILES - 1 else jnp.where(lane < tail, v, 0.0)

        cls = cls_ref[j]
        if j == TILES - 1:
            cls = jnp.where(lane < tail, cls, 0)
        cel = jnp.take_along_axis(gs_ref[...], cls, axis=1)
        sea = raw(0)
        sixth = cel * (sea * (1.0 / 6.0))
        fl_ref[F_SEA, j] = sea
        fl_ref[F_CX, j] = sixth * stretch
        fl_ref[F_CY, j] = sixth
        fl_ref[F_CUR0, j] = raw(1) * (sea * (1.0 / 6.0))
        fl_ref[F_CUR1, j] = raw(2) * (sea * (1.0 / 6.0))
        fl_ref[F_T0, j] = (TURNING_SCALE * sixth) * raw(3)
        fl_ref[F_T1, j] = (TURNING_SCALE * sixth) * raw(4)

    def load(d, carry):
        base = pl.multiple_of(8 * d, 8)
        for j in range(TILES):
            width = LANES if j < TILES - 1 else tail
            for f in range(FREQS):
                v = spec_ref[f, d, :, pl.ds(j * LANES, width)].astype(jnp.float32)
                x_ref[j, pl.ds(base + f, 4, stride=2), pl.ds(0, width)] = v
        return carry

    lax.fori_loop(0, ND, load, 0)

    def prepare(q, carry):
        base = pl.multiple_of(32 * q, 32)
        first = [None] * 4
        for j in range(TILES):
            v = [x_ref[j, pl.ds(base + 8 * i, 8), :] for i in range(4)]
            if j == TILES - 1:
                v = [jnp.where(lane < tail, w, 0.0) for w in v]
            v = [w * fl_ref[F_SEA, j] for w in v]
            if j == 0:
                first = v
            if j == TILES - 1:
                v = [
                    jnp.where(
                        lane < tail,
                        w,
                        jnp.where(lane < tail + 2, pltpu.roll(a, tail, 1), pltpu.roll(w, LANES - tail, 1)),
                    )
                    for w, a in zip(v, first)
                ]
            for i in range(4):
                x_ref[j, pl.ds(base + 8 * i, 8), :] = v[i]
            turned = [pltpu.roll(w, 4, 0) for w in v]
            low = [jnp.where(sub < 4, v[i], turned[i + 1]) for i in (0, 2)]
            high = [jnp.where(sub < 4, turned[i], v[i + 1]) for i in (0, 2)]
            rows = pl.ds(pl.multiple_of(16 * q, 16), 16)
            hs_ref[0, j, rows, :] = jnp.concatenate(low, axis=0).astype(jnp.bfloat16)
            hs_ref[1, j, rows, :] = jnp.concatenate(high, axis=0).astype(jnp.bfloat16)
        return carry

    lax.fori_loop(0, ND // 4, prepare, 0, unroll=3)

    pl.semaphore_wait(barrier, len(OFFSETS) + 2)
    halos = []

    def send_halos(c):
        for side, b in ((0, south), (1, north)):
            copy = pltpu.make_async_remote_copy(
                src_ref=hs_ref.at[side, pl.ds(PER * c, PER)],
                dst_ref=hr_ref.at[side, pl.ds(PER * c, PER)],
                send_sem=halo_send.at[side, c],
                recv_sem=halo_recv.at[side, c],
                device_id={"band": b},
                device_id_type=MESH,
            )
            copy.start()
            halos.append(copy)

    for c in range(CHUNKS // 2):
        send_halos(c)

    build_tables(counts_ref, flag_ref, tabv_ref, loc_ref)
    table_copy = pltpu.make_async_copy(tabv_ref, tab_ref, tab_sem)
    table_copy.start()

    for c in range(CHUNKS // 2, CHUNKS):
        send_halos(c)

    def along(d, carry):
        base = pl.multiple_of(8 * d, 8)
        cos_d = scalars_ref[0, d]
        x = [x_ref[j, pl.ds(base, 8), :] for j in range(TILES)]
        r1 = [pltpu.roll(v, 1, 1) for v in x]
        r2 = [pltpu.roll(v, 2, 1) for v in x]
        l1 = [pltpu.roll(v, LANES - 1, 1) for v in x]
        l2 = [pltpu.roll(v, LANES - 2, 1) for v in x]
        for j in range(TILES):
            before, after = (j - 1) % TILES, (j + 1) % TILES
            behind = jnp.where(lane < 1, r1[before], r1[j])
            far_behind = jnp.where(lane < 2, r2[before], r2[j])
            ahead = jnp.where(lane >= LANES - 1, l1[after], l1[j])
            far_ahead = jnp.where(lane >= LANES - 2, l2[after], l2[j])
            speed = fl_ref[F_CX, j] * cos_d + fl_ref[F_CUR0, j]
            out = x[j] - upwind12(far_behind, behind, x[j], ahead, far_ahead, speed)
            adv_ref[j, pl.ds(base + 16, 8), :] = out
        return carry

    lax.fori_loop(0, ND, along, 0, unroll=4)

    keep_dn = (band < bands - 1).astype(jnp.float32)
    keep_up = (band > 0).astype(jnp.float32)
    zero = jnp.zeros((8, LANES), jnp.float32)

    def reduce_start(axis, c, src, dst):
        copies = []
        for i in range(1, SIDE):
            o = (0, i) if axis == 0 else (i, 0)
            copy = pltpu.make_async_remote_copy(
                src_ref=src.at[c],
                dst_ref=dst.at[c, i - 1],
                send_sem=sum_send.at[axis, c, i - 1],
                recv_sem=sum_recv.at[axis, c, i - 1],
                device_id={"comp": peer(o)},
                device_id_type=MESH,
            )
            copy.start()
            copies.append(copy)
        return copies

    sums_y, sums_z = [], []

    def pass_on(c):
        for copy in sums_y[c]:
            copy.wait()
        total_ref[c] = (part_ref[c] + yr_ref[c, 0]) + (yr_ref[c, 1] + yr_ref[c, 2])
        sums_z.append(reduce_start(1, c, total_ref, zr_ref))

    part_ref[...] = jnp.zeros((CHUNKS, 16, LANES), jnp.float32)

    for c in range(CHUNKS):
        halos[2 * c].wait_recv()
        halos[2 * c + 1].wait_recv()

        def across(q, carry):
            rows = pl.ds(pl.multiple_of(16 * q, 16), 16)
            base = pl.multiple_of(32 * q, 32)
            for j in range(PER * c, PER * c + PER):
                dn = hr_ref[0, j, rows, :].astype(jnp.float32) * keep_dn
                up = hr_ref[1, j, rows, :].astype(jnp.float32) * keep_up
                for i in range(4):
                    a, b = dn[8 * (i // 2) : 8 * (i // 2) + 8], up[8 * (i // 2) : 8 * (i // 2) + 8]
                    if i % 2 == 0:
                        h = jnp.where(sub < 4, a, pltpu.roll(b, 4, 0))
                    else:
                        h = jnp.where(sub < 4, pltpu.roll(a, 4, 0), b)
                    here = pl.ds(base + 8 * i, 8)
                    v = x_ref[j, here, :]
                    ahead = pltpu.roll(jnp.where(row == 0, h, v), 6, 0)
                    far_ahead = pltpu.roll(jnp.where(row < 2, h, v), 4, 0)
                    far_behind = pltpu.roll(jnp.where(row < 2, v, h), 4, 0)
                    behind = pltpu.roll(jnp.where(row == 3, h, v), 2, 0)
                    speed = fl_ref[F_CY, j] * scalars_ref[1, 4 * q + i] + fl_ref[F_CUR1, j]
                    flux = upwind12(far_behind, behind, v, ahead, far_ahead, speed)
                    there = pl.ds(base + (8 * i + 16), 8)
                    adv_ref[j, there, :] = adv_ref[j, there, :] - flux
            return carry

        lax.fori_loop(0, ND // 4, across, 0)

        for j in range(PER * c, PER * c + PER):
            adv_ref[j, pl.ds(0, 16), :] = adv_ref[j, pl.ds(8 * ND, 16), :]
            adv_ref[j, pl.ds(8 * ND + 16, 16), :] = adv_ref[j, pl.ds(16, 16), :]

        def refract(q, sums):
            base = pl.multiple_of(8 * RUN * q, 8)
            sums = list(sums)
            for j in range(PER * c, PER * c + PER):
                near = [adv_ref[j, pl.ds(base + 8 * i, 8), :] for i in range(RUN + 4)]
                t0, t1 = fl_ref[F_T0, j], fl_ref[F_T1, j]
                for i in range(RUN):
                    d = RUN * q + i
                    speed = t0 * scalars_ref[1, d] - t1 * scalars_ref[0, d]
                    out = near[i + 2] - upwind12(*near[i : i + 5], speed)
                    sums[j - PER * c] = sums[j - PER * c] + out * out
                    t_ref[j, pl.ds(d, 8, stride=ND), :] = out
            return tuple(sums)

        sums = lax.fori_loop(0, ND // RUN, refract, (zero,) * PER)
        for i in range(PER):
            j = PER * c + i
            sq_ref[...] = sums[i] + pltpu.roll(sums[i], 7, 0)
            part_ref[c, pl.ds(4 * i, 4), :] = sq_ref[pl.ds(0, 4, stride=2), :]
        sums_y.append(reduce_start(0, c, part_ref, yr_ref))
        if c >= 2:
            pass_on(c - 2)

    t_rows = t_ref.reshape(GROUPS, COMPS, LANES)

    def step(k, carry):
        keep = tab_ref[AT_KEEP, k].astype(jnp.float32)
        spot = tab_ref[AT_SPOT, k]
        local = lane + tab_ref[AT_DELTA, k]
        valid = (lane < tab_ref[AT_LEN, k]) & (local >= 0) & (local < tab_ref[AT_COUNT, k])
        local = jnp.clip(local, 0, LANES - 1)
        idx = jnp.take_along_axis(loc_ref[spot], local, axis=1)
        idx_ref[k] = jnp.where(valid, idx, -1)
        parts = []
        for m in range(COMPS // 8):
            data = t_rows[spot, pl.ds(8 * m, 8), :]
            got = jnp.take_along_axis(data, idx, axis=1)
            part = jnp.where(valid, got, carry[m] * keep)
            stage_ref[k, pl.ds(8 * m, 8), :] = part
            parts.append(part)
        gust = jnp.where(valid, jnp.take_along_axis(gust_ref[spot], idx, axis=1), carry[COMPS // 8])
        gusts_ref[k] = gust
        return tuple(parts) + (gust,)

    table_copy.wait()
    carry = lax.fori_loop(0, STEPS // 2, step, (zero,) * (COMPS // 8 + 1), unroll=8)
    pass_on(CHUNKS - 2)
    pass_on(CHUNKS - 1)
    lax.fori_loop(STEPS // 2, STEPS, step, carry, unroll=8)

    def by_row(q):
        low, high = scalars_ref[q, FREQS * me], scalars_ref[q, FREQS * me + 1]
        mixed = jnp.where(sub < 4, low, high)
        return [low if m < 4 else (mixed if m == 4 else high) for m in range(COMPS // 8)]

    rise, calm = by_row(2), by_row(3)
    for i in range(2):
        for m in range(COMPS // 8):
            rows = pl.ds(8 * m, 8)
            compass_ref[i, rows, :] = compass_ref[i, rows, :] * rise[m]

    def grow(c, carry):
        for j in range(3):
            k = tab_ref[AT_LAST, 3 * c + j]
            gust = gusts_ref[k]
            east = jnp.broadcast_to(gust[0:1], (8, LANES))
            north = jnp.broadcast_to(gust[1:2], (8, LANES))
            for m in range(COMPS // 8):
                rows = pl.ds(8 * m, 8)
                push = east * compass_ref[0, rows, :] + north * compass_ref[1, rows, :]
                grown_ref[3 * c + j, rows, :] = stage_ref[k, rows, :] * jnp.exp(jnp.maximum(push - calm[m], 0.0))
        return carry

    lax.fori_loop(0, BLOCKS, grow, 0, unroll=2)
    for c in range(CHUNKS):
        for copy in sums_z[c]:
            copy.wait()
        total = (total_ref[c] + zr_ref[c, 0]) + (zr_ref[c, 1] + zr_ref[c, 2])
        total = jnp.sqrt(total * (1.0 / (BLOCKS * COMPS)) + 1e-6)
        for i in range(ROWS * PER):
            level_ref[ROWS * PER * c + i] = jnp.broadcast_to(total[i : i + 1], (8, LANES))

    def strengths(k, acc):
        idx = idx_ref[k]
        got = jnp.take_along_axis(level_ref[tab_ref[AT_SPOT, k]], jnp.maximum(idx, 0), axis=1)
        acc = jnp.where(idx >= 0, got, acc)
        dec_ref[k] = acc
        return acc

    lax.fori_loop(0, STEPS, strengths, zero, unroll=32)

    fade0 = scalars_ref[4, FREQS * me]
    fade1 = scalars_ref[4, FREQS * me + 1]

    def block(c, store):
        places = [tab_ref[AT_LAST, 3 * c + j] for j in range(3)]
        rows = []
        for j in range(3):
            s = dec_ref[places[j]]
            e0 = jnp.exp(-fade0 * s)
            e1 = jnp.exp(-fade1 * s)
            mixed = jnp.where(sub < 4, e0, e1)
            values = []
            for m in range(COMPS // 8):
                e = e0 if m < 4 else (mixed if m == 4 else e1)
                values.append(grown_ref[3 * c + j, pl.ds(8 * m, 8), :] * e)
            if j < 2:
                rows += values
            else:
                for m in range(5):
                    v = values[m]
                    if m < 4:
                        v = jnp.where(lane < 64, v, pltpu.roll(values[5 + m], 64, 1))
                    rows.append(v)
                rows.append(zero)
        for m in range(PACK // 16):
            store(m, jnp.concatenate(rows[2 * m : 2 * m + 2], axis=0).astype(jnp.bfloat16))

    copies = []
    for i, o in enumerate(OFFSETS):
        other = peer(o)

        def put(m, v):
            sb_ref[i, pl.ds(16 * m, 16), :] = v

        block(other, put)
        copy = pltpu.make_async_remote_copy(
            src_ref=sb_ref.at[i],
            dst_ref=rb_ref.at[me],
            send_sem=send_sem.at[i],
            recv_sem=recv_sem.at[i],
            device_id={"comp": other},
            device_id_type=MESH,
        )
        copy.start()
        copies.append(copy)

    def put_own(m, v):
        own_ref[pl.ds(16 * m, 16), :] = v

    block(me, put_own)
    own_copy = pltpu.make_async_copy(own_ref, rb_ref.at[me], own_sem)
    own_copy.start()
    own_copy.wait()
    for copy in halos:
        copy.wait_send()
    for copy in copies:
        copy.wait()


def finish_kernel(rb_ref, out_ref, in_ref, v_ref, in_sem):
    copies = [
        pltpu.make_async_copy(rb_ref.at[pl.ds(4 * i, 4)], in_ref.at[pl.ds(4 * i, 4)], in_sem.at[i]) for i in range(4)
    ]
    for copy in copies:
        copy.start()

    def spread(i, carry):
        base = pl.multiple_of(COMPS * i, 8)
        v = in_ref[i].astype(jnp.float32)
        for j in range(2):
            v_ref[j, pl.ds(base, COMPS), :] = v[COMPS * j : COMPS * (j + 1)]
        v_ref[2, pl.ds(base, 40), :] = v[2 * COMPS : 2 * COMPS + 40]
        v_ref[2, pl.ds(base + 40, 32), :] = pltpu.roll(v[2 * COMPS : 2 * COMPS + 32], 64, 1)
        return carry

    for i in range(4):
        copies[i].wait()
        lax.fori_loop(4 * i, 4 * i + 4, spread, 0, unroll=4)
    def turn(m, carry):
        at = pl.multiple_of(LANES * m, LANES)
        for j in range(3):
            block = v_ref[j, pl.ds(at, LANES), :].T.astype(jnp.bfloat16)
            rows = min(LANES, SLOTS - LANES * j)
            out_ref[pl.ds(LANES * j, rows), pl.ds(at, LANES)] = block[:rows]
        return carry

    lax.fori_loop(0, BLOCKS * COMPS // LANES, turn, 0)


def build_tables(counts_ref, flag_ref, tabv_ref, loc_ref):
    f32, bf16, i32 = jnp.float32, jnp.bfloat16, jnp.int32
    sub = lax.broadcasted_iota(i32, (LANES, LANES), 0)
    lanes = lax.broadcasted_iota(i32, (LANES, LANES), 1)
    lane = lax.broadcasted_iota(i32, (8, LANES), 1)

    def order(i):
        return jnp.where(i < GROUPS, (i & (ROWS - 1)) * TILES + (i >> 2), i)

    def product(a, b, dims=(((1,), (0,)), ((), ()))):
        return lax.dot_general(a, b, dims, preferred_element_type=f32)

    upper = (sub <= lanes).astype(f32).astype(bf16)
    ones = jnp.ones((LANES, LANES), bf16)
    flags = flag_ref[...].astype(bf16)
    inclusive = product(flags, upper)
    count_rows = product(flags, ones)
    ends = product((order(lanes) <= order(sub)).astype(f32).astype(bf16), count_rows.astype(bf16))[:GROUPS]
    count = product(ones[:16], flags, (((1,), (1,)), ((), ())))
    first = product(count.astype(bf16), (order(sub) < order(lanes)).astype(f32).astype(bf16))
    count, first = count[:8].astype(i32), first[:8].astype(i32)

    wide = lanes[:GROUPS]
    shift = wide - (inclusive[:GROUPS].astype(i32) - 1)
    word = jnp.where(flag_ref[pl.ds(0, GROUPS), :] > 0, wide + LANES * shift + LANES * LANES, 0)
    for k in range(7):
        bit = LANES << k
        moved = pltpu.roll(word, LANES - (1 << k), 1)
        word = jnp.where((moved & bit) != 0, moved, jnp.where((word & bit) != 0, 0, word))
    word = word & (LANES - 1)
    for g in range(GROUPS):
        loc_ref[g] = jnp.broadcast_to(word[g : g + 1], (8, LANES))

    block = (lane * 171) >> 9
    part = lane - 3 * block
    size = jnp.zeros((8, LANES), i32)
    rank = jnp.zeros((8, LANES), i32)
    start = 0
    for c in range(BLOCKS):
        n = counts_ref[0, c]
        size = jnp.where(block == c, n, size)
        rank = jnp.where(block == c, start, rank)
        start = start + n
    rank = rank + LANES * part
    length = jnp.clip(size - LANES * part, 0, LANES)
    real = lane < 3 * BLOCKS

    def groups_before(r):
        hit = (ends <= r[:1].astype(f32)).astype(f32)
        return jnp.minimum(jnp.broadcast_to(jnp.sum(hit, axis=0, keepdims=True), (8, LANES)), GROUPS - 1.0)

    low = groups_before(rank)
    high = groups_before(rank + jnp.maximum(length, 1) - 1)
    width = jnp.where(real, jnp.where(length > 0, high - low + 1.0, 1.0), 0.0)
    stop = product(jnp.concatenate([width, width], axis=0).astype(bf16), upper)[:8]
    begin = stop - width
    column = jnp.sum(jnp.where(wide <= sub[:GROUPS], width[:1], 0.0), axis=1, keepdims=True)
    tile = jnp.sum((column <= wide.astype(f32)).astype(f32), axis=0, keepdims=True)
    tile = jnp.broadcast_to(jnp.minimum(tile, 3 * BLOCKS - 1.0), (8, LANES)).astype(i32)

    def at(values, index):
        return jnp.take_along_axis(values, index, axis=1)

    group = lane + at((low - begin).astype(i32), tile)
    group = jnp.clip(group, 0, GROUPS - 1)
    r = (group * 171) >> 11
    spot = ROWS * (group - TILES * r) + r
    tabv_ref[AT_SPOT : AT_SPOT + 1] = spot[:1]
    tabv_ref[AT_KEEP : AT_KEEP + 1] = (lane > at(begin.astype(i32), tile)).astype(i32)[:1]
    tabv_ref[AT_DELTA : AT_DELTA + 1] = (at(rank, tile) - at(first, spot))[:1]
    tabv_ref[AT_LEN : AT_LEN + 1] = at(length, tile)[:1]
    tabv_ref[AT_COUNT : AT_COUNT + 1] = at(count, spot)[:1]
    tabv_ref[AT_LAST : AT_LAST + 1] = jnp.clip((stop - 1.0).astype(i32), 0, STEPS - 1)[:1]
    tabv_ref[AT_LAST + 1 :] = jnp.zeros((7 - AT_LAST, LANES), i32)


def body(spectra, depth_class, group_speed, current, depth_slope, wind, land_mask, block_counts):
    cos_t, sin_t = angles()
    latitude = (-60.0 + 120.0 * (np.arange(ROWS * lax.axis_size("band")) + 0.5) / (ROWS * lax.axis_size("band"))) * (
        math.pi / 180.0
    )
    stretch = (1.0 / np.cos(latitude)).astype(np.float32)
    angular = 2.0 * math.pi * 0.0418 * np.power(1.1, np.arange(BLOCKS * FREQS, dtype=np.float64))
    ratio = angular / angular[-1]
    phase = 9.81 / angular
    coef = np.stack([GROWTH_RATE * ratio / phase, GROWTH_RATE * ratio, DAMPING * ratio]).astype(np.float32)

    scalars = np.zeros((8, LANES), np.float32)
    scalars[0, :ND], scalars[1, :ND] = cos_t, sin_t
    scalars[2:5, : BLOCKS * FREQS] = coef
    scalars[5, : stretch.size] = stretch
    compass = np.stack([np.tile(cos_t, FREQS), np.tile(sin_t, FREQS)])
    compass = np.ascontiguousarray(np.broadcast_to(compass[:, :, None], (2, COMPS, LANES)))

    vmem = pl.BlockSpec(memory_space=pltpu.VMEM)
    f32, bf16 = jnp.float32, jnp.bfloat16
    dma = pltpu.SemaphoreType.DMA
    rb = pl.pallas_call(
        step_kernel,
        out_shape=jax.ShapeDtypeStruct((BLOCKS, PACK, LANES), bf16),
        in_specs=[pl.BlockSpec(memory_space=pltpu.HBM)] * 10,
        out_specs=pl.BlockSpec(memory_space=pltpu.HBM),
        scratch_shapes=[
            pltpu.SMEM((8, LANES), f32),
            pltpu.VMEM((2, COMPS, LANES), f32),
            pltpu.SMEM(block_counts.shape, jnp.int32),
            pltpu.VMEM(spectra.shape, bf16),
            pltpu.VMEM(depth_class.shape, jnp.int32),
            pltpu.VMEM(group_speed.shape[::-1], f32),
            pltpu.VMEM(current.shape, f32),
            pltpu.VMEM(depth_slope.shape, f32),
            pltpu.VMEM(wind.shape, f32),
            pltpu.VMEM(land_mask.shape, jnp.int32),
            pltpu.VMEM((GROUPS, 8, LANES), f32),
            pltpu.VMEM((STEPS, 8, LANES), f32),
            pltpu.VMEM((8, LANES), f32),
            pltpu.VMEM((TILES, 8 * 5, LANES), f32),
            pltpu.VMEM((TILES, 8, LANES), jnp.int32),
            pltpu.VMEM((LANES, LANES), f32),
            pltpu.VMEM((8, LANES), jnp.int32),
            pltpu.SMEM((8, LANES), jnp.int32),
            pltpu.VMEM((GROUPS, 8, LANES), jnp.int32),
            pltpu.VMEM((TILES, 8 * ND, LANES), f32),
            pltpu.VMEM((TILES, 8 * (ND + 4), LANES), f32),
            pltpu.VMEM((TILES, 8 * ND, LANES), f32),
            pltpu.VMEM((STEPS, COMPS, LANES), f32),
            pltpu.VMEM((3 * BLOCKS, COMPS, LANES), f32),
            pltpu.VMEM((STEPS, 8, LANES), jnp.int32),
            pltpu.VMEM((STEPS, 8, LANES), f32),
            pltpu.VMEM((7, TILES, 8, LANES), f32),
            pltpu.VMEM((2, TILES, 4 * ND, LANES), bf16),
            pltpu.VMEM((2, TILES, 4 * ND, LANES), bf16),
            pltpu.VMEM((8, LANES), f32),
            pltpu.VMEM((CHUNKS, 16, LANES), f32),
            pltpu.VMEM((CHUNKS, 16, LANES), f32),
            pltpu.VMEM((GROUPS, 8, LANES), f32),
            pltpu.VMEM((CHUNKS, SIDE - 1, 16, LANES), f32),
            pltpu.VMEM((CHUNKS, SIDE - 1, 16, LANES), f32),
            pltpu.VMEM((BLOCKS - 1, PACK, LANES), bf16),
            pltpu.VMEM((PACK, LANES), bf16),
            dma((10,)),
            dma,
            dma,
            dma((2, CHUNKS)),
            dma((2, CHUNKS)),
            dma((2, CHUNKS, SIDE - 1)),
            dma((2, CHUNKS, SIDE - 1)),
            dma((BLOCKS - 1,)),
            dma((BLOCKS - 1,)),
        ],
        compiler_params=pltpu.CompilerParams(
            collective_id=0, has_side_effects=True, vmem_limit_bytes=58 * 1024 * 1024
        ),
        name="wave_step",
    )(
        jnp.asarray(scalars),
        jnp.asarray(compass),
        block_counts,
        spectra,
        depth_class,
        group_speed.T,
        current,
        depth_slope,
        wind,
        land_mask,
    )

    out = pl.pallas_call(
        finish_kernel,
        out_shape=jax.ShapeDtypeStruct((SLOTS, BLOCKS * COMPS), bf16),
        in_specs=[pl.BlockSpec(memory_space=pltpu.HBM)],
        out_specs=vmem,
        scratch_shapes=[
            pltpu.VMEM((BLOCKS, PACK, LANES), bf16),
            pltpu.VMEM((3, BLOCKS * COMPS, LANES), f32),
            dma((4,)),
        ],
        compiler_params=pltpu.CompilerParams(vmem_limit_bytes=58 * 1024 * 1024),
        name="finish",
    )(rb)
    return out.T


def solution(mesh):
    return jax.shard_map(
        body,
        mesh=mesh,
        in_specs=(
            P("comp", None, "band", None),
            P("band", None),
            P(),
            P(None, "band", None),
            P(None, "band", None),
            P(None, "band", None),
            P("band", None),
            P("band", None),
        ),
        out_specs=P(None, ("comp", "band")),
        check_vma=False,
    )
```

```python
import math

import jax
import jax.numpy as jnp
import numpy as np
from jax import lax
from jax.experimental import pallas as pl
from jax.experimental.pallas import tpu as pltpu
from jax.sharding import PartitionSpec as P

GROWTH_RATE = 0.05
DAMPING = 1.5
TURNING_SCALE = 0.5

FREQS = 2
LANES = 128
ND = 36
ROWS = 4
NLON = 1440
TILES = 12
GROUPS = ROWS * TILES
BLOCKS = 16
SLOTS = 315
DEPTHS = 64
STEPS = 96
COMPS = FREQS * ND
PACK = 192
CHUNKS = 3
PER = TILES // CHUNKS
RUN = 6
SIDE = 4

AT_SPOT, AT_KEEP, AT_DELTA, AT_LEN, AT_COUNT, AT_LAST = range(6)

(F_SEA, F_CX, F_CY, F_CUR0, F_CUR1, F_T0, F_T1) = range(7)

MESH = pl.DeviceIdType.MESH


def angles():
    heading = (np.arange(ND, dtype=np.float32) * np.float32(2.0 * math.pi / ND)).astype(np.float64)
    return (np.cos(heading).astype(np.float32), np.sin(heading).astype(np.float32))


def upwind12(far_behind, behind, centre, ahead, far_ahead, speed):
    forward = speed > 0
    down = jnp.where(forward, ahead, behind)
    up = jnp.where(forward, behind, ahead)
    far = jnp.where(forward, far_behind, far_ahead)
    return jnp.abs(speed) * ((2.0 * down + far) + (3.0 * centre - 6.0 * up))


OFFSETS = sorted(
    [(a, b) for a in range(SIDE) for b in range(SIDE) if a or b],
    key=lambda o: -(min(o[0], SIDE - o[0]) + min(o[1], SIDE - o[1])),
)


def step_kernel(
    scalars_hbm, compass_hbm, counts_hbm, spec_hbm, depth_hbm, speed_hbm, current_hbm, slope_hbm, wind_hbm, land_hbm,
    rb_ref,
    scalars_ref, compass_ref, counts_ref, spec_ref, depth_ref, speed_ref, current_ref, slope_ref, wind_ref, land_ref,
    gust_ref, gusts_ref,
    gs_ref, raw_ref, cls_ref, flag_ref, tabv_ref, tab_ref, loc_ref, x_ref, adv_ref, t_ref, stage_ref, grown_ref, idx_ref, dec_ref, fl_ref, hs_ref, hr_ref, sq_ref, part_ref, total_ref, level_ref, yr_ref, zr_ref, sb_ref, own_ref,
    in_sem, tab_sem, own_sem, halo_send, halo_recv, sum_send, sum_recv, send_sem, recv_sem,
):
    arrivals = [
        pltpu.make_async_copy(src, dst, in_sem.at[i])
        for i, (src, dst) in enumerate(
            [
                (land_hbm, land_ref),
                (spec_hbm, spec_ref),
                (scalars_hbm, scalars_ref),
                (speed_hbm, speed_ref),
                (depth_hbm, depth_ref),
                (current_hbm, current_ref),
                (slope_hbm, slope_ref),
                (wind_hbm, wind_ref),
                (counts_hbm, counts_ref),
                (compass_hbm, compass_ref),
            ]
        )
    ]
    for copy in arrivals:
        copy.start()
    lane = lax.broadcasted_iota(jnp.int32, (8, LANES), 1)
    sub = lax.broadcasted_iota(jnp.int32, (8, LANES), 0)
    row = sub // 2
    tail = NLON - (TILES - 1) * LANES
    me = lax.axis_index("comp")
    band = lax.axis_index("band")
    bands = lax.axis_size("band")
    z, y = me // SIDE, lax.rem(me, SIDE)
    north = lax.rem(band + 1, bands)
    south = lax.rem(band + bands - 1, bands)

    def peer(o):
        return lax.rem(z + o[0], SIDE) * SIDE + lax.rem(y + o[1], SIDE)

    barrier = pltpu.get_barrier_semaphore()
    for b in (north, south):
        pl.semaphore_signal(barrier, inc=1, device_id={"band": b}, device_id_type=MESH)
    for o in OFFSETS:
        pl.semaphore_signal(barrier, inc=1, device_id={"comp": peer(o)}, device_id_type=MESH)

    for copy in arrivals:
        copy.wait()

    even_half = lax.rem(lax.broadcasted_iota(jnp.int32, (8, DEPTHS), 0), 2) == 0
    gs_ref[:, pl.ds(0, DEPTHS)] = jnp.where(
        even_half,
        jnp.broadcast_to(speed_ref[pl.ds(FREQS * me, 1), :], (8, DEPTHS)),
        jnp.broadcast_to(speed_ref[pl.ds(FREQS * me + 1, 1), :], (8, DEPTHS)),
    )
    stretch = jnp.where(row == 0, scalars_ref[5, ROWS * band], scalars_ref[5, ROWS * band + 1])
    stretch = jnp.where(row == 2, scalars_ref[5, ROWS * band + 2], stretch)
    stretch = jnp.where(row == 3, scalars_ref[5, ROWS * band + 3], stretch)
    flag_ref[...] = jnp.zeros((LANES, LANES), jnp.float32)
    for j in range(TILES):
        width = LANES if j < TILES - 1 else tail
        cols = pl.ds(j * LANES, width)
        sea = (land_ref[:, cols] == 0).astype(jnp.float32)
        flag_ref[pl.ds(ROWS * j, ROWS), pl.ds(0, width)] = sea
        for i in range(2):
            gust = wind_ref[i, :, cols]
            for r in range(ROWS):
                gust_ref[ROWS * j + r, i : i + 1, pl.ds(0, width)] = gust[r : r + 1]
        parts = [sea] + [ref[i, :, cols] for ref in (current_ref, slope_ref) for i in range(2)]
        for n, v in enumerate(parts):
            for f in range(FREQS):
                raw_ref[j, pl.ds(8 * n + f, 4, stride=2), pl.ds(0, width)] = v
        v = depth_ref[:, cols]
        for f in range(FREQS):
            cls_ref[j, pl.ds(f, 4, stride=2), pl.ds(0, width)] = v
    for j in range(TILES):
        def raw(n):
            v = raw_ref[j, pl.ds(8 * n, 8), :]
            return v if j < TILES - 1 else jnp.where(lane < tail, v, 0.0)

        cls = cls_ref[j]
        if j == TILES - 1:
            cls = jnp.where(lane < tail, cls, 0)
        cel = jnp.take_along_axis(gs_ref[...], cls, axis=1)
        sea = raw(0)
        sixth = cel * (sea * (1.0 / 6.0))
        fl_ref[F_SEA, j] = sea
        fl_ref[F_CX, j] = sixth * stretch
        fl_ref[F_CY, j] = sixth
        fl_ref[F_CUR0, j] = raw(1) * (sea * (1.0 / 6.0))
        fl_ref[F_CUR1, j] = raw(2) * (sea * (1.0 / 6.0))
        fl_ref[F_T0, j] = (TURNING_SCALE * sixth) * raw(3)
        fl_ref[F_T1, j] = (TURNING_SCALE * sixth) * raw(4)

    def load(d, carry):
        base = pl.multiple_of(8 * d, 8)
        for j in range(TILES):
            width = LANES if j < TILES - 1 else tail
            for f in range(FREQS):
                v = spec_ref[f, d, :, pl.ds(j * LANES, width)].astype(jnp.float32)
                x_ref[j, pl.ds(base + f, 4, stride=2), pl.ds(0, width)] = v
        return carry

    lax.fori_loop(0, ND, load, 0)

    def prepare(q, carry):
        base = pl.multiple_of(32 * q, 32)
        first = [None] * 4
        for j in range(TILES):
            v = [x_ref[j, pl.ds(base + 8 * i, 8), :] for i in range(4)]
            if j == TILES - 1:
                v = [jnp.where(lane < tail, w, 0.0) for w in v]
            v = [w * fl_ref[F_SEA, j] for w in v]
            if j == 0:
                first = v
            if j == TILES - 1:
                v = [
                    jnp.where(
                        lane < tail,
                        w,
                        jnp.where(lane < tail + 2, pltpu.roll(a, tail, 1), pltpu.roll(w, LANES - tail, 1)),
                    )
                    for w, a in zip(v, first)
                ]
            for i in range(4):
                x_ref[j, pl.ds(base + 8 * i, 8), :] = v[i]
            turned = [pltpu.roll(w, 4, 0) for w in v]
            low = [jnp.where(sub < 4, v[i], turned[i + 1]) for i in (0, 2)]
            high = [jnp.where(sub < 4, turned[i], v[i + 1]) for i in (0, 2)]
            rows = pl.ds(pl.multiple_of(16 * q, 16), 16)
            hs_ref[0, j, rows, :] = jnp.concatenate(low, axis=0).astype(jnp.bfloat16)
            hs_ref[1, j, rows, :] = jnp.concatenate(high, axis=0).astype(jnp.bfloat16)
        return carry

    lax.fori_loop(0, ND // 4, prepare, 0, unroll=3)

    pl.semaphore_wait(barrier, len(OFFSETS) + 2)
    halos = []

    def send_halos(c):
        for side, b in ((0, south), (1, north)):
            copy = pltpu.make_async_remote_copy(
                src_ref=hs_ref.at[side, pl.ds(PER * c, PER)],
                dst_ref=hr_ref.at[side, pl.ds(PER * c, PER)],
                send_sem=halo_send.at[side, c],
                recv_sem=halo_recv.at[side, c],
                device_id={"band": b},
                device_id_type=MESH,
            )
            copy.start()
            halos.append(copy)

    for c in range(CHUNKS // 2):
        send_halos(c)

    build_tables(counts_ref, flag_ref, tabv_ref, loc_ref)
    table_copy = pltpu.make_async_copy(tabv_ref, tab_ref, tab_sem)
    table_copy.start()

    for c in range(CHUNKS // 2, CHUNKS):
        send_halos(c)

    def along(d, carry):
        base = pl.multiple_of(8 * d, 8)
        cos_d = scalars_ref[0, d]
        x = [x_ref[j, pl.ds(base, 8), :] for j in range(TILES)]
        r1 = [pltpu.roll(v, 1, 1) for v in x]
        r2 = [pltpu.roll(v, 2, 1) for v in x]
        l1 = [pltpu.roll(v, LANES - 1, 1) for v in x]
        l2 = [pltpu.roll(v, LANES - 2, 1) for v in x]
        for j in range(TILES):
            before, after = (j - 1) % TILES, (j + 1) % TILES
            behind = jnp.where(lane < 1, r1[before], r1[j])
            far_behind = jnp.where(lane < 2, r2[before], r2[j])
            ahead = jnp.where(lane >= LANES - 1, l1[after], l1[j])
            far_ahead = jnp.where(lane >= LANES - 2, l2[after], l2[j])
            speed = fl_ref[F_CX, j] * cos_d + fl_ref[F_CUR0, j]
            out = x[j] - upwind12(far_behind, behind, x[j], ahead, far_ahead, speed)
            adv_ref[j, pl.ds(base + 16, 8), :] = out
        return carry

    lax.fori_loop(0, ND, along, 0, unroll=4)

    keep_dn = (band < bands - 1).astype(jnp.float32)
    keep_up = (band > 0).astype(jnp.float32)
    zero = jnp.zeros((8, LANES), jnp.float32)

    def reduce_start(axis, c, src, dst):
        copies = []
        for i in range(1, SIDE):
            o = (0, i) if axis == 0 else (i, 0)
            copy = pltpu.make_async_remote_copy(
                src_ref=src.at[c],
                dst_ref=dst.at[c, i - 1],
                send_sem=sum_send.at[axis, c, i - 1],
                recv_sem=sum_recv.at[axis, c, i - 1],
                device_id={"comp": peer(o)},
                device_id_type=MESH,
            )
            copy.start()
            copies.append(copy)
        return copies

    sums_y, sums_z = [], []

    def pass_on(c):
        for copy in sums_y[c]:
            copy.wait()
        total_ref[c] = (part_ref[c] + yr_ref[c, 0]) + (yr_ref[c, 1] + yr_ref[c, 2])
        sums_z.append(reduce_start(1, c, total_ref, zr_ref))

    part_ref[...] = jnp.zeros((CHUNKS, 16, LANES), jnp.float32)

    for c in range(CHUNKS):
        halos[2 * c].wait_recv()
        halos[2 * c + 1].wait_recv()

        def across(q, carry):
            rows = pl.ds(pl.multiple_of(16 * q, 16), 16)
            base = pl.multiple_of(32 * q, 32)
            for j in range(PER * c, PER * c + PER):
                dn = hr_ref[0, j, rows, :].astype(jnp.float32) * keep_dn
                up = hr_ref[1, j, rows, :].astype(jnp.float32) * keep_up
                for i in range(4):
                    a, b = dn[8 * (i // 2) : 8 * (i // 2) + 8], up[8 * (i // 2) : 8 * (i // 2) + 8]
                    if i % 2 == 0:
                        h = jnp.where(sub < 4, a, pltpu.roll(b, 4, 0))
                    else:
                        h = jnp.where(sub < 4, pltpu.roll(a, 4, 0), b)
                    here = pl.ds(base + 8 * i, 8)
                    v = x_ref[j, here, :]
                    ahead = pltpu.roll(jnp.where(row == 0, h, v), 6, 0)
                    far_ahead = pltpu.roll(jnp.where(row < 2, h, v), 4, 0)
                    far_behind = pltpu.roll(jnp.where(row < 2, v, h), 4, 0)
                    behind = pltpu.roll(jnp.where(row == 3, h, v), 2, 0)
                    speed = fl_ref[F_CY, j] * scalars_ref[1, 4 * q + i] + fl_ref[F_CUR1, j]
                    flux = upwind12(far_behind, behind, v, ahead, far_ahead, speed)
                    there = pl.ds(base + (8 * i + 16), 8)
                    adv_ref[j, there, :] = adv_ref[j, there, :] - flux
            return carry

        lax.fori_loop(0, ND // 4, across, 0)

        for j in range(PER * c, PER * c + PER):
            adv_ref[j, pl.ds(0, 16), :] = adv_ref[j, pl.ds(8 * ND, 16), :]
            adv_ref[j, pl.ds(8 * ND + 16, 16), :] = adv_ref[j, pl.ds(16, 16), :]

        def refract(q, sums):
            base = pl.multiple_of(8 * RUN * q, 8)
            sums = list(sums)
            for j in range(PER * c, PER * c + PER):
                near = [adv_ref[j, pl.ds(base + 8 * i, 8), :] for i in range(RUN + 4)]
                t0, t1 = fl_ref[F_T0, j], fl_ref[F_T1, j]
                for i in range(RUN):
                    d = RUN * q + i
                    speed = t0 * scalars_ref[1, d] - t1 * scalars_ref[0, d]
                    out = near[i + 2] - upwind12(*near[i : i + 5], speed)
                    sums[j - PER * c] = sums[j - PER * c] + out * out
                    t_ref[j, pl.ds(d, 8, stride=ND), :] = out
            return tuple(sums)

        sums = lax.fori_loop(0, ND // RUN, refract, (zero,) * PER)
        for i in range(PER):
            j = PER * c + i
            sq_ref[...] = sums[i] + pltpu.roll(sums[i], 7, 0)
            part_ref[c, pl.ds(4 * i, 4), :] = sq_ref[pl.ds(0, 4, stride=2), :]
        sums_y.append(reduce_start(0, c, part_ref, yr_ref))
        if c >= 2:
            pass_on(c - 2)

    t_rows = t_ref.reshape(GROUPS, COMPS, LANES)

    def step(k, carry):
        keep = tab_ref[AT_KEEP, k].astype(jnp.float32)
        spot = tab_ref[AT_SPOT, k]
        local = lane + tab_ref[AT_DELTA, k]
        valid = (lane < tab_ref[AT_LEN, k]) & (local >= 0) & (local < tab_ref[AT_COUNT, k])
        local = jnp.clip(local, 0, LANES - 1)
        idx = jnp.take_along_axis(loc_ref[spot], local, axis=1)
        idx_ref[k] = jnp.where(valid, idx, -1)
        parts = []
        for m in range(COMPS // 8):
            data = t_rows[spot, pl.ds(8 * m, 8), :]
            got = jnp.take_along_axis(data, idx, axis=1)
            part = jnp.where(valid, got, carry[m] * keep)
            stage_ref[k, pl.ds(8 * m, 8), :] = part
            parts.append(part)
        gust = jnp.where(valid, jnp.take_along_axis(gust_ref[spot], idx, axis=1), carry[COMPS // 8])
        gusts_ref[k] = gust
        return tuple(parts) + (gust,)

    table_copy.wait()
    carry = lax.fori_loop(0, STEPS // 2, step, (zero,) * (COMPS // 8 + 1), unroll=8)
    pass_on(CHUNKS - 2)
    pass_on(CHUNKS - 1)
    lax.fori_loop(STEPS // 2, STEPS, step, carry, unroll=8)

    def by_row(q):
        low, high = scalars_ref[q, FREQS * me], scalars_ref[q, FREQS * me + 1]
        mixed = jnp.where(sub < 4, low, high)
        return [low if m < 4 else (mixed if m == 4 else high) for m in range(COMPS // 8)]

    rise, calm = by_row(2), by_row(3)
    for i in range(2):
        for m in range(COMPS // 8):
            rows = pl.ds(8 * m, 8)
            compass_ref[i, rows, :] = compass_ref[i, rows, :] * rise[m]

    def grow(c, carry):
        for j in range(3):
            k = tab_ref[AT_LAST, 3 * c + j]
            gust = gusts_ref[k]
            east = jnp.broadcast_to(gust[0:1], (8, LANES))
            north = jnp.broadcast_to(gust[1:2], (8, LANES))
            for m in range(COMPS // 8):
                rows = pl.ds(8 * m, 8)
                push = east * compass_ref[0, rows, :] + north * compass_ref[1, rows, :]
                grown_ref[3 * c + j, rows, :] = stage_ref[k, rows, :] * jnp.exp(jnp.maximum(push - calm[m], 0.0))
        return carry

    lax.fori_loop(0, BLOCKS, grow, 0, unroll=2)
    for c in range(CHUNKS):
        for copy in sums_z[c]:
            copy.wait()
        total = (total_ref[c] + zr_ref[c, 0]) + (zr_ref[c, 1] + zr_ref[c, 2])
        total = jnp.sqrt(total * (1.0 / (BLOCKS * COMPS)) + 1e-6)
        for i in range(ROWS * PER):
            level_ref[ROWS * PER * c + i] = jnp.broadcast_to(total[i : i + 1], (8, LANES))

    def strengths(k, acc):
        idx = idx_ref[k]
        got = jnp.take_along_axis(level_ref[tab_ref[AT_SPOT, k]], jnp.maximum(idx, 0), axis=1)
        acc = jnp.where(idx >= 0, got, acc)
        dec_ref[k] = acc
        return acc

    lax.fori_loop(0, STEPS, strengths, zero, unroll=32)

    fade0 = scalars_ref[4, FREQS * me]
    fade1 = scalars_ref[4, FREQS * me + 1]

    def block(c, store):
        places = [tab_ref[AT_LAST, 3 * c + j] for j in range(3)]
        rows = []
        for j in range(3):
            s = dec_ref[places[j]]
            e0 = jnp.exp(-fade0 * s)
            e1 = jnp.exp(-fade1 * s)
            mixed = jnp.where(sub < 4, e0, e1)
            values = []
            for m in range(COMPS // 8):
                e = e0 if m < 4 else (mixed if m == 4 else e1)
                values.append(grown_ref[3 * c + j, pl.ds(8 * m, 8), :] * e)
            if j < 2:
                rows += values
            else:
                for m in range(5):
                    v = values[m]
                    if m < 4:
                        v = jnp.where(lane < 64, v, pltpu.roll(values[5 + m], 64, 1))
                    rows.append(v)
                rows.append(zero)
        for m in range(PACK // 16):
            store(m, jnp.concatenate(rows[2 * m : 2 * m + 2], axis=0).astype(jnp.bfloat16))

    copies = []
    for i, o in enumerate(OFFSETS):
        other = peer(o)

        def put(m, v):
            sb_ref[i, pl.ds(16 * m, 16), :] = v

        block(other, put)
        copy = pltpu.make_async_remote_copy(
            src_ref=sb_ref.at[i],
            dst_ref=rb_ref.at[me],
            send_sem=send_sem.at[i],
            recv_sem=recv_sem.at[i],
            device_id={"comp": other},
            device_id_type=MESH,
        )
        copy.start()
        copies.append(copy)

    def put_own(m, v):
        own_ref[pl.ds(16 * m, 16), :] = v

    block(me, put_own)
    own_copy = pltpu.make_async_copy(own_ref, rb_ref.at[me], own_sem)
    own_copy.start()
    own_copy.wait()
    for copy in halos:
        copy.wait_send()
    for copy in copies:
        copy.wait()


def finish_kernel(rb_ref, out_ref, in_ref, v_ref, in_sem):
    copies = [
        pltpu.make_async_copy(rb_ref.at[pl.ds(4 * i, 4)], in_ref.at[pl.ds(4 * i, 4)], in_sem.at[i]) for i in range(4)
    ]
    for copy in copies:
        copy.start()

    def spread(i, carry):
        base = pl.multiple_of(COMPS * i, 8)
        v = in_ref[i].astype(jnp.float32)
        for j in range(2):
            v_ref[j, pl.ds(base, COMPS), :] = v[COMPS * j : COMPS * (j + 1)]
        v_ref[2, pl.ds(base, 40), :] = v[2 * COMPS : 2 * COMPS + 40]
        v_ref[2, pl.ds(base + 40, 32), :] = pltpu.roll(v[2 * COMPS : 2 * COMPS + 32], 64, 1)
        return carry

    for i in range(4):
        copies[i].wait()
        lax.fori_loop(4 * i, 4 * i + 4, spread, 0, unroll=4)
    for m in range(BLOCKS * COMPS // LANES):
        for j in range(3):
            block = v_ref[j, pl.ds(LANES * m, LANES), :].T.astype(jnp.bfloat16)
            rows = min(LANES, SLOTS - LANES * j)
            out_ref[pl.ds(LANES * j, rows), pl.ds(LANES * m, LANES)] = block[:rows]


def build_tables(counts_ref, flag_ref, tabv_ref, loc_ref):
    f32, bf16, i32 = jnp.float32, jnp.bfloat16, jnp.int32
    sub = lax.broadcasted_iota(i32, (LANES, LANES), 0)
    lanes = lax.broadcasted_iota(i32, (LANES, LANES), 1)
    lane = lax.broadcasted_iota(i32, (8, LANES), 1)

    def order(i):
        return jnp.where(i < GROUPS, (i & (ROWS - 1)) * TILES + (i >> 2), i)

    def product(a, b, dims=(((1,), (0,)), ((), ()))):
        return lax.dot_general(a, b, dims, preferred_element_type=f32)

    upper = (sub <= lanes).astype(f32).astype(bf16)
    ones = jnp.ones((LANES, LANES), bf16)
    flags = flag_ref[...].astype(bf16)
    inclusive = product(flags, upper)
    count_rows = product(flags, ones)
    ends = product((order(lanes) <= order(sub)).astype(f32).astype(bf16), count_rows.astype(bf16))[:GROUPS]
    count = product(ones[:16], flags, (((1,), (1,)), ((), ())))
    first = product(count.astype(bf16), (order(sub) < order(lanes)).astype(f32).astype(bf16))
    count, first = count[:8].astype(i32), first[:8].astype(i32)

    wide = lanes[:GROUPS]
    shift = wide - (inclusive[:GROUPS].astype(i32) - 1)
    word = jnp.where(flag_ref[pl.ds(0, GROUPS), :] > 0, wide + LANES * shift + LANES * LANES, 0)
    for k in range(7):
        bit = LANES << k
        moved = pltpu.roll(word, LANES - (1 << k), 1)
        word = jnp.where((moved & bit) != 0, moved, jnp.where((word & bit) != 0, 0, word))
    word = word & (LANES - 1)
    for g in range(GROUPS):
        loc_ref[g] = jnp.broadcast_to(word[g : g + 1], (8, LANES))

    block = (lane * 171) >> 9
    part = lane - 3 * block
    size = jnp.zeros((8, LANES), i32)
    rank = jnp.zeros((8, LANES), i32)
    start = 0
    for c in range(BLOCKS):
        n = counts_ref[0, c]
        size = jnp.where(block == c, n, size)
        rank = jnp.where(block == c, start, rank)
        start = start + n
    rank = rank + LANES * part
    length = jnp.clip(size - LANES * part, 0, LANES)
    real = lane < 3 * BLOCKS

    def groups_before(r):
        hit = (ends <= r[:1].astype(f32)).astype(f32)
        return jnp.minimum(jnp.broadcast_to(jnp.sum(hit, axis=0, keepdims=True), (8, LANES)), GROUPS - 1.0)

    low = groups_before(rank)
    high = groups_before(rank + jnp.maximum(length, 1) - 1)
    width = jnp.where(real, jnp.where(length > 0, high - low + 1.0, 1.0), 0.0)
    stop = product(jnp.concatenate([width, width], axis=0).astype(bf16), upper)[:8]
    begin = stop - width
    column = jnp.sum(jnp.where(wide <= sub[:GROUPS], width[:1], 0.0), axis=1, keepdims=True)
    tile = jnp.sum((column <= wide.astype(f32)).astype(f32), axis=0, keepdims=True)
    tile = jnp.broadcast_to(jnp.minimum(tile, 3 * BLOCKS - 1.0), (8, LANES)).astype(i32)

    def at(values, index):
        return jnp.take_along_axis(values, index, axis=1)

    group = lane + at((low - begin).astype(i32), tile)
    group = jnp.clip(group, 0, GROUPS - 1)
    r = (group * 171) >> 11
    spot = ROWS * (group - TILES * r) + r
    tabv_ref[AT_SPOT : AT_SPOT + 1] = spot[:1]
    tabv_ref[AT_KEEP : AT_KEEP + 1] = (lane > at(begin.astype(i32), tile)).astype(i32)[:1]
    tabv_ref[AT_DELTA : AT_DELTA + 1] = (at(rank, tile) - at(first, spot))[:1]
    tabv_ref[AT_LEN : AT_LEN + 1] = at(length, tile)[:1]
    tabv_ref[AT_COUNT : AT_COUNT + 1] = at(count, spot)[:1]
    tabv_ref[AT_LAST : AT_LAST + 1] = jnp.clip((stop - 1.0).astype(i32), 0, STEPS - 1)[:1]
    tabv_ref[AT_LAST + 1 :] = jnp.zeros((7 - AT_LAST, LANES), i32)


def body(spectra, depth_class, group_speed, current, depth_slope, wind, land_mask, block_counts):
    cos_t, sin_t = angles()
    latitude = (-60.0 + 120.0 * (np.arange(ROWS * lax.axis_size("band")) + 0.5) / (ROWS * lax.axis_size("band"))) * (
        math.pi / 180.0
    )
    stretch = (1.0 / np.cos(latitude)).astype(np.float32)
    angular = 2.0 * math.pi * 0.0418 * np.power(1.1, np.arange(BLOCKS * FREQS, dtype=np.float64))
    ratio = angular / angular[-1]
    phase = 9.81 / angular
    coef = np.stack([GROWTH_RATE * ratio / phase, GROWTH_RATE * ratio, DAMPING * ratio]).astype(np.float32)

    scalars = np.zeros((8, LANES), np.float32)
    scalars[0, :ND], scalars[1, :ND] = cos_t, sin_t
    scalars[2:5, : BLOCKS * FREQS] = coef
    scalars[5, : stretch.size] = stretch
    compass = np.stack([np.tile(cos_t, FREQS), np.tile(sin_t, FREQS)])
    compass = np.ascontiguousarray(np.broadcast_to(compass[:, :, None], (2, COMPS, LANES)))

    vmem = pl.BlockSpec(memory_space=pltpu.VMEM)
    f32, bf16 = jnp.float32, jnp.bfloat16
    dma = pltpu.SemaphoreType.DMA
    rb = pl.pallas_call(
        step_kernel,
        out_shape=jax.ShapeDtypeStruct((BLOCKS, PACK, LANES), bf16),
        in_specs=[pl.BlockSpec(memory_space=pltpu.HBM)] * 10,
        out_specs=pl.BlockSpec(memory_space=pltpu.HBM),
        scratch_shapes=[
            pltpu.SMEM((8, LANES), f32),
            pltpu.VMEM((2, COMPS, LANES), f32),
            pltpu.SMEM(block_counts.shape, jnp.int32),
            pltpu.VMEM(spectra.shape, bf16),
            pltpu.VMEM(depth_class.shape, jnp.int32),
            pltpu.VMEM(group_speed.shape[::-1], f32),
            pltpu.VMEM(current.shape, f32),
            pltpu.VMEM(depth_slope.shape, f32),
            pltpu.VMEM(wind.shape, f32),
            pltpu.VMEM(land_mask.shape, jnp.int32),
            pltpu.VMEM((GROUPS, 8, LANES), f32),
            pltpu.VMEM((STEPS, 8, LANES), f32),
            pltpu.VMEM((8, LANES), f32),
            pltpu.VMEM((TILES, 8 * 5, LANES), f32),
            pltpu.VMEM((TILES, 8, LANES), jnp.int32),
            pltpu.VMEM((LANES, LANES), f32),
            pltpu.VMEM((8, LANES), jnp.int32),
            pltpu.SMEM((8, LANES), jnp.int32),
            pltpu.VMEM((GROUPS, 8, LANES), jnp.int32),
            pltpu.VMEM((TILES, 8 * ND, LANES), f32),
            pltpu.VMEM((TILES, 8 * (ND + 4), LANES), f32),
            pltpu.VMEM((TILES, 8 * ND, LANES), f32),
            pltpu.VMEM((STEPS, COMPS, LANES), f32),
            pltpu.VMEM((3 * BLOCKS, COMPS, LANES), f32),
            pltpu.VMEM((STEPS, 8, LANES), jnp.int32),
            pltpu.VMEM((STEPS, 8, LANES), f32),
            pltpu.VMEM((7, TILES, 8, LANES), f32),
            pltpu.VMEM((2, TILES, 4 * ND, LANES), bf16),
            pltpu.VMEM((2, TILES, 4 * ND, LANES), bf16),
            pltpu.VMEM((8, LANES), f32),
            pltpu.VMEM((CHUNKS, 16, LANES), f32),
            pltpu.VMEM((CHUNKS, 16, LANES), f32),
            pltpu.VMEM((GROUPS, 8, LANES), f32),
            pltpu.VMEM((CHUNKS, SIDE - 1, 16, LANES), f32),
            pltpu.VMEM((CHUNKS, SIDE - 1, 16, LANES), f32),
            pltpu.VMEM((BLOCKS - 1, PACK, LANES), bf16),
            pltpu.VMEM((PACK, LANES), bf16),
            dma((10,)),
            dma,
            dma,
            dma((2, CHUNKS)),
            dma((2, CHUNKS)),
            dma((2, CHUNKS, SIDE - 1)),
            dma((2, CHUNKS, SIDE - 1)),
            dma((BLOCKS - 1,)),
            dma((BLOCKS - 1,)),
        ],
        compiler_params=pltpu.CompilerParams(
            collective_id=0, has_side_effects=True, vmem_limit_bytes=58 * 1024 * 1024
        ),
        name="wave_step",
    )(
        jnp.asarray(scalars),
        jnp.asarray(compass),
        block_counts,
        spectra,
        depth_class,
        group_speed.T,
        current,
        depth_slope,
        wind,
        land_mask,
    )

    out = pl.pallas_call(
        finish_kernel,
        out_shape=jax.ShapeDtypeStruct((SLOTS, BLOCKS * COMPS), bf16),
        in_specs=[pl.BlockSpec(memory_space=pltpu.HBM)],
        out_specs=vmem,
        scratch_shapes=[
            pltpu.VMEM((BLOCKS, PACK, LANES), bf16),
            pltpu.VMEM((3, BLOCKS * COMPS, LANES), f32),
            dma((4,)),
        ],
        compiler_params=pltpu.CompilerParams(vmem_limit_bytes=58 * 1024 * 1024),
        name="finish",
    )(rb)
    return out.T


def solution(mesh):
    return jax.shard_map(
        body,
        mesh=mesh,
        in_specs=(
            P("comp", None, "band", None),
            P("band", None),
            P(),
            P(None, "band", None),
            P(None, "band", None),
            P(None, "band", None),
            P("band", None),
            P("band", None),
        ),
        out_specs=P(None, ("comp", "band")),
        check_vma=False,
    )
```
